512 devices in a mesh: ctx: 16 (over z), ch: 32 (over x, y, core).
Axes of the slice: x: 4, y: 4, z: 16, core: 2. Of those that a mesh axis runs over, the one named last changes fastest.
Arguments:
- projected: bfloat16 [3, 8192, 4096], P(None, 'ctx', 'ch'), may hold values from -6 to 6
- conv_weight: float32 [3, 7, 4096], P(None, None, 'ch'), may hold values from -2 to 2
- residues: float32 [256, 16], P('ch'), may hold values from -0.26 to 0.26
- decay_rates: float32 [256, 16], P('ch'), may hold values from 5.6152344e-05 to 0.0333333333
- grad_out: bfloat16 [8192, 4096], P('ctx', 'ch'), may hold values from -0.9722718 to 0.9722718
Outputs:
- grad_projected: bfloat16 [3, 8192, 4096], P(None, 'ctx', 'ch')
- grad_conv: float32 [3, 7, 4096], P(None, None, 'ch')
- grad_residues: float32 [256, 16], P('ch')
- grad_log_rates: float32 [256, 16], P('ch')
The draws below stay inside these ranges and needn't reach their ends.
All inputs are finite; a program needn't handle non-finite values.
Results may differ from the reference program's by a relative error of at most 0.0017.
Values may be sent and summed in bfloat16 or wider, within the bound.
No kernel may reach another device: no remote copies, remote signals or barrier semaphores. Data moves between devices by JAX's collectives and lax.ppermute only.
A program may use at most 64 MiB of HBM per device.

```python
import math
import jax
import jax.numpy as jnp
from jax import lax

D = 4096
G = 256
MODES = 16
KW = 7
TOKENS = 8192


def rate_table(key):
    base_key = jax.random.fold_in(key, 11)
    pick_key, slow_key, fast_key = jax.random.split(base_key, 3)
    slow_share = 0.5
    keep_rate = math.log(10.0) / TOKENS
    slow_rate = keep_rate * jnp.exp(math.log(0.2) * jax.random.uniform(slow_key, (G, MODES)))
    fast_rate = keep_rate * jnp.exp(math.log(1.0 / (30.0 * keep_rate)) * jax.random.uniform(fast_key, (G, MODES)))
    chooser = jax.random.uniform(pick_key, (G, MODES))
    return jnp.where(chooser < slow_share, slow_rate, fast_rate).astype(jnp.float32)


def draw_decay_rates(key, part):
    return rate_table(key)


def draw_residues(key, part):
    key = jax.random.fold_in(key, 12)
    amplitude = 0.13 * jax.random.truncated_normal(key, -2.0, 2.0, (G, MODES))
    return amplitude.astype(jnp.float32)


def draw_grad_out(key, part):
    column_key = jax.random.fold_in(key, 21)
    value_key = jax.random.fold_in(key, 22)
    column_pos = jnp.arange(D, dtype=jnp.float32) / max(D - 1, 1)
    spread = jnp.exp(math.log(10.0) * (jax.random.uniform(column_key, (D,)) - 0.5))
    overall = 4.0 / math.sqrt(TOKENS)
    column_ramp = jnp.exp(0.5 * math.log(3.0) * column_pos)
    values = jax.random.truncated_normal(value_key, -4.0, 4.0, (TOKENS, D))
    return (values * spread * column_ramp * overall).astype(jnp.bfloat16)


def steps_of(key, shape, cuts, least, top_value):
    loudness, own = 1.0, jax.random.fold_in(key, 6)
    for dim, parts in cuts:
        steps = jnp.exp(jax.random.uniform(jax.random.fold_in(own, dim), (parts,), jnp.float32, least / len(cuts), top_value / len(cuts)))
        loudness = loudness * jnp.repeat(steps, shape[dim] // parts).reshape([-1 if axis == dim else 1 for axis in range(len(shape))])
    return loudness


def scatter_about(own_key, extent, width, reach, cuts=(), kind=jnp.bfloat16):
    entries = jax.random.normal(own_key, extent, jnp.float32) * width
    if len(cuts) > 0:
        entries = steps_of(own_key, extent, cuts, -0.22, 0.18) * entries
    return jnp.clip(entries, min=-reach, max=reach).astype(kind)


def setup_inputs(seed: int = 0) -> dict:
    splits = jax.random.split(jax.random.key(seed), 6)
    return {
        "projected": scatter_about(splits[0], (3, TOKENS, D), 1.0, 6.0, ((1, 16), (2, 32))),
        "conv_weight": scatter_about(splits[1], (3, KW, D), KW ** -0.5, 2.0, ((2, 32),), jnp.float32),
        "residues": draw_residues(jax.random.fold_in(splits[5], 71), 0),
        "decay_rates": draw_decay_rates(jax.random.fold_in(splits[5], 71), 0),
        "grad_out": draw_grad_out(jax.random.fold_in(splits[5], 71), 0),
    }


TOP_PRECISION = lax.Precision.HIGHEST

def group_backward(pieces):
    inputs_group, weights_group, residue_group, rate_group, upstream = pieces
    length = upstream.shape[0]
    tap_count = weights_group.shape[1]
    margin = tap_count - 1
    widened = jnp.pad(inputs_group.astype(jnp.float32), ((0, 0), (margin, 0), (0, 0)))
    feature = jnp.zeros(inputs_group.shape, jnp.float32)
    for offset in range(tap_count):
        feature = feature + weights_group[:, offset, None, :] * widened[:, margin - offset:margin - offset + length, :]
    queries, keyed, valued = (feature[0], feature[1], feature[2])
    gated_input = keyed * valued
    lag_index = jnp.arange(length, dtype=jnp.float32)
    powers = jnp.exp(-rate_group[:, None] * lag_index[None, :])
    filter_kernel = jnp.dot(residue_group, powers, precision=TOP_PRECISION)
    fft_size = 2 * length
    kernel_hat = jnp.fft.rfft(filter_kernel, n=fft_size)
    gated_hat = jnp.fft.rfft(gated_input, n=fft_size, axis=0)
    long_out = jnp.fft.irfft(gated_hat * kernel_hat[:, None], n=fft_size, axis=0)[:length]
    signal = upstream.astype(jnp.float32)
    grad_query = signal * long_out
    grad_long = signal * queries
    long_hat = jnp.fft.rfft(grad_long, n=fft_size, axis=0)
    grad_gated = jnp.fft.irfft(long_hat * jnp.conj(kernel_hat)[:, None], n=fft_size, axis=0)[:length]
    lag_grad = jnp.fft.irfft(lax.optimization_barrier(jnp.sum(long_hat * jnp.conj(gated_hat), axis=1)), n=fft_size)[:length]
    raw_residue = jnp.dot(powers, lag_grad, precision=TOP_PRECISION)
    raw_rate = -rate_group * residue_group * jnp.dot(powers, lag_index * lag_grad, precision=TOP_PRECISION)
    grad_feature = jnp.stack([grad_query, grad_gated * valued, grad_gated * keyed])
    trailing = jnp.pad(grad_feature, ((0, 0), (0, margin), (0, 0)))
    grad_inputs = jnp.zeros(grad_feature.shape, jnp.float32)
    for offset in range(tap_count):
        grad_inputs = grad_inputs + weights_group[:, offset, None, :] * trailing[:, offset:offset + length, :]
    raw_conv = jnp.stack([lax.optimization_barrier(jnp.sum(grad_feature * widened[:, margin - offset:margin - offset + length, :], axis=1)) for offset in range(tap_count)], axis=1)
    return (grad_inputs.astype(jnp.bfloat16), raw_conv, raw_residue, raw_rate)

def reference(projected, conv_weight, residues, decay_rates, grad_out):
    groups = residues.shape[0]
    channels = projected.shape[2]
    group_width = channels // groups
    length = projected.shape[1]
    inputs_split = projected.reshape(3, length, groups, group_width).transpose(2, 0, 1, 3)
    weight_split = conv_weight.reshape(3, KW, groups, group_width).transpose(2, 0, 1, 3)
    upstream_split = grad_out.reshape(length, groups, group_width).transpose(1, 0, 2)
    grad_inputs, raw_conv, raw_residue, raw_rate = lax.map(group_backward, (inputs_split, weight_split, residues, decay_rates, upstream_split))
    grad_projected = grad_inputs.transpose(1, 2, 0, 3).reshape(3, length, channels)
    raw_conv = raw_conv.transpose(1, 2, 0, 3).reshape(3, KW, channels)
    entry_count = 3 * KW * D + 2 * G * MODES
    squares = jnp.sum(raw_conv * raw_conv) + jnp.sum(raw_residue * raw_residue) + jnp.sum(raw_rate * raw_rate)
    factor = jnp.minimum(1.0, lax.rsqrt(squares / entry_count + 1e-06))
    return (grad_projected, raw_conv * factor, raw_residue * factor, raw_rate * factor)
```

```python
import jax
import jax.numpy as jnp
from jax import lax
from jax.experimental import pallas as pl
from jax.experimental.pallas import tpu as pltpu
from jax.sharding import PartitionSpec as P

D = 4096
G = 256
MODES = 16
KW = 7

ROWS = 512
CHANNELS = 128
GROUPS = 8
WIDTH = 16
CHUNK = 128
CHUNKS = ROWS // CHUNK
LEAD = 16
MARGIN = KW - 1
STATS = 24

F32 = jnp.float32
BF16 = jnp.bfloat16
EXACT = lax.Precision.HIGHEST
MM = (((1,), (0,)), ((), ()))
NT = (((1,), (1,)), ((), ()))


def split(value):
    high = value.astype(BF16)
    low = (value - high.astype(F32)).astype(BF16)
    return high, low


def dot3(left, right, dims=MM):
    lh, ll = left
    rh, rl = right

    def product(a, b):
        return lax.dot_general(a, b, dims, preferred_element_type=F32)

    return product(lh, rh) + (product(lh, rl) + product(ll, rh))


def iota(shape, axis):
    return lax.broadcasted_iota(jnp.int32, shape, axis)


def lane_group(rows):
    return (iota((rows, CHANNELS), 1) // WIDTH == iota((rows, CHANNELS), 0)).astype(F32)


def mode_row(table):
    pick = (iota((MODES, CHANNELS), 1) % MODES == iota((MODES, CHANNELS), 0)).astype(F32)
    spread = lax.dot_general(table, pick, MM, precision=EXACT, preferred_element_type=F32)
    return jnp.sum(spread * lane_group(GROUPS), axis=0, keepdims=True)


def mode_column(row):
    eye = iota((CHANNELS, CHANNELS), 0) == iota((CHANNELS, CHANNELS), 1)
    return jnp.sum(jnp.where(eye, row, 0.0), axis=1, keepdims=True)


def mode_compact(table):
    return lax.dot_general(
        table, lane_group(GROUPS), (((0,), (0,)), ((), ())), precision=EXACT, preferred_element_type=F32
    )


def compact(full):
    lanes = full.shape[1]
    total = None
    for g in range(GROUPS):
        own = (iota((MODES, lanes), 1) % CHANNELS) // WIDTH == g
        part = jnp.where(own, full[g * MODES : (g + 1) * MODES, :], 0.0)
        total = part if total is None else total + part
    return total


def expand(small):
    lanes = small.shape[1]
    own = (iota((CHANNELS, lanes), 0) // MODES == (iota((CHANNELS, lanes), 1) % CHANNELS) // WIDTH).astype(F32)
    return split(jnp.concatenate([small] * GROUPS, axis=0) * own)


def side_by_side(value):
    return jnp.concatenate([value[q * CHUNK : (q + 1) * CHUNK, :] for q in range(CHUNKS)], axis=1)


def chunk_lanes(value, q):
    return value[:, q * CHANNELS : (q + 1) * CHANNELS]


def first_kernel(me_ref, proj_ref, before_ref, weight_ref, rate_ref, out_grad_ref,
                 ext_ref, kv_ref, gi_ref, gl_ref, states_ref, send_ref):
    me = me_ref[0]
    for i in range(3):
        ext_ref[i, 0:LEAD, :] = before_ref[i].astype(F32)
        ext_ref[i, LEAD:, :] = proj_ref[i].astype(F32)
    for q in range(CHUNKS):
        feature = []
        for i in range(3):
            total = None
            for j in range(KW):
                term = weight_ref[i, j : j + 1, :] * ext_ref[i, pl.ds(LEAD - j + q * CHUNK, CHUNK), :]
                total = term if total is None else total + term
            feature.append(total)
        rows = pl.ds(q * CHUNK, CHUNK)
        kv_ref[0, rows, :] = feature[1]
        kv_ref[1, rows, :] = feature[2]
        gi_ref[:, q * CHANNELS : (q + 1) * CHANNELS] = feature[1] * feature[2]
        gl_ref[:, q * CHANNELS : (q + 1) * CHANNELS] = out_grad_ref[rows, :].astype(F32) * feature[0]
    rates = rate_ref[...]
    column = mode_column(mode_row(rates))
    lag = iota((CHANNELS, CHUNK), 1).astype(F32)
    ascending = jnp.exp(-column * lag)
    descending = jnp.exp(-column * (CHUNK - 1 - lag))
    small_rates = mode_compact(rates)
    one_step = jnp.exp(-small_rates)
    chunk_decay = jnp.exp(-small_rates * CHUNK)
    ends = compact(dot3(split(descending), split(gi_ref[...])))
    leads = compact(dot3(split(ascending), split(gl_ref[...])))
    state = jnp.zeros((MODES, CHANNELS), F32)
    for q in range(CHUNKS):
        part = chunk_lanes(ends, q)
        states_ref[0, :, q * CHANNELS : (q + 1) * CHANNELS] = part
        state = chunk_decay * state + part
    back = jnp.zeros((MODES, CHANNELS), F32)
    for q in reversed(range(CHUNKS)):
        part = one_step * chunk_lanes(leads, q)
        states_ref[1, :, q * CHANNELS : (q + 1) * CHANNELS] = part
        back = chunk_decay * back + part
    for d in range(send_ref.shape[0]):
        send_ref[d] = jnp.where(d > me, state, back)


def middle_kernel(rate_ref, residue_ref, gi_ref, gl_ref, states_ref,
                  long_ref, gated_ref, local_ref, small_ref, lag_ref):
    rates = rate_ref[...]
    row = mode_row(rates)
    column = mode_column(row)
    lag = iota((CHANNELS, CHUNK), 1)
    back_lag = lax.rem(CHUNK - lag, CHUNK)
    ascending = jnp.exp(-column * lag.astype(F32))
    descending = jnp.exp(-column * (CHUNK - 1 - lag).astype(F32))
    turned = jnp.exp(-column * back_lag.astype(F32))
    residue_row = mode_row(residue_ref[...]) * lane_group(GROUPS)
    filters = lax.dot_general(residue_row, ascending, MM, precision=EXACT, preferred_element_type=F32)
    turned_filters = lax.dot_general(residue_row, turned, MM, precision=EXACT, preferred_element_type=F32)
    gi = split(gi_ref[...])
    gl = split(gl_ref[...])
    down = iota((CHUNK, CHUNK), 0)
    across = iota((CHUNK, CHUNK), 1)
    mirror = (down + across == CHUNK - 1).astype(F32).astype(BF16)
    mirrored = [
        lax.dot_general(mirror, part, MM, preferred_element_type=F32).astype(BF16) for part in gl
    ]
    wide_group = (iota((1, ROWS), 1) % CHANNELS) // WIDTH
    lane_of = iota((CHUNK, CHANNELS), 1) // WIDTH
    for g in range(GROUPS):
        straight = jnp.broadcast_to(turned_filters[g : g + 1, :], (CHUNK, CHUNK))
        straight = pltpu.roll(straight, 0, 1, stride=1, stride_axis=0)
        straight = split(jnp.where(across <= down, straight, 0.0))
        flipped = jnp.broadcast_to(filters[g : g + 1, :], (CHUNK, CHUNK))
        flipped = pltpu.roll(flipped, 0, 1, stride=1, stride_axis=0)
        flipped = split(jnp.where(across >= down, flipped, 0.0))
        forward = dot3(straight, gi)
        backward = dot3(flipped, gl)
        for q in range(CHUNKS):
            rows = pl.ds(q * CHUNK, CHUNK)
            if g == 0:
                long_ref[rows, :] = chunk_lanes(forward, q)
                gated_ref[rows, :] = chunk_lanes(backward, q)
            else:
                long_ref[rows, :] = jnp.where(lane_of == g, chunk_lanes(forward, q), long_ref[rows, :])
                gated_ref[rows, :] = jnp.where(lane_of == g, chunk_lanes(backward, q), gated_ref[rows, :])
        own = (wide_group == g).astype(F32).astype(BF16)
        products = dot3((mirrored[0] * own, mirrored[1] * own), gi, NT)
        products = jnp.where(across + down <= CHUNK - 1, products, 0.0)
        sheared = pltpu.roll(products, 1, 1, stride=1, stride_axis=0)
        lag_ref[g : g + 1, :] = jnp.sum(sheared, axis=0, keepdims=True)
    lag_grad = lag_ref[...]
    down_lag = lax.rem(CHUNK - down, CHUNK).astype(F32)
    powers = jnp.exp(-row * down_lag)
    residue_sums = lax.dot_general(lag_grad, powers, MM, precision=EXACT, preferred_element_type=F32)
    moment_sums = lax.dot_general(lag_grad, powers * down_lag, MM, precision=EXACT, preferred_element_type=F32)
    own_group = lane_group(GROUPS)
    local_ref[...] = jnp.zeros(local_ref.shape, F32)
    local_ref[0:1, :] = jnp.sum(residue_sums * own_group, axis=0, keepdims=True)
    local_ref[1:2, :] = jnp.sum(moment_sums * own_group, axis=0, keepdims=True)
    small_rates = mode_compact(rates)
    chunk_decay = jnp.exp(-small_rates * CHUNK)
    lag_value = lag.astype(F32)
    end_moments = compact(dot3(split(descending * (CHUNK - 1 - lag_value)), gi))
    lead_moments = compact(dot3(split(ascending * (jnp.exp(-column) * (lag_value + 1.0))), gl))
    zero = jnp.zeros((MODES, CHANNELS), F32)
    state, moment = zero, zero
    residue_part, moment_part, lead_moment = zero, zero, zero
    offset_decay = jnp.ones((MODES, CHANNELS), F32)
    for q in range(CHUNKS):
        lead = chunk_lanes(states_ref[1], q)
        end = chunk_lanes(states_ref[0], q)
        lead_here = chunk_lanes(lead_moments, q)
        small_ref[0, :, q * CHANNELS : (q + 1) * CHANNELS] = state
        residue_part = residue_part + lead * state
        moment_part = moment_part + lead_here * state + lead * moment
        lead_moment = lead_moment + offset_decay * (lead_here + float(q * CHUNK) * lead)
        offset_decay = offset_decay * chunk_decay
        moment = chunk_decay * (moment + float(CHUNK) * state) + chunk_lanes(end_moments, q)
        state = chunk_decay * state + end
    back = zero
    for q in reversed(range(CHUNKS)):
        small_ref[1, :, q * CHANNELS : (q + 1) * CHANNELS] = back
        back = chunk_decay * back + chunk_lanes(states_ref[1], q)
    for at, value in enumerate((residue_part, moment_part, lead_moment, moment)):
        small_ref[2, :, at * CHANNELS : (at + 1) * CHANNELS] = value
    small_ref[3, :, 0:CHANNELS] = back


def finish_kernel(me_ref, arrived_ref, rate_ref, residue_ref, small_ref, local_ref, long_ref, gated_ref,
                  kv_ref, out_grad_ref, ext_ref, feature_ref, stats_ref):
    me = me_ref[0]
    rates = rate_ref[...]
    residues = residue_ref[...]
    row = mode_row(rates)
    small_rates = mode_compact(rates)
    small_residues = mode_compact(residues)
    chunk_decay = jnp.exp(-small_rates * CHUNK)
    zero = jnp.zeros((MODES, CHANNELS), F32)
    state_in, late_in, back_in = zero, zero, zero
    for d in range(arrived_ref.shape[0]):
        away = (jnp.abs(me - d) - 1).astype(F32) * float(ROWS)
        term = jnp.exp(-small_rates * away) * arrived_ref[d]
        state_in = state_in + jnp.where(d < me, term, 0.0)
        late_in = late_in + jnp.where(d < me, term * away, 0.0)
        back_in = back_in + jnp.where(d > me, term, 0.0)
    states, backs = [], []
    carried = state_in
    for q in range(CHUNKS):
        states.append(small_residues * (chunk_lanes(small_ref[0], q) + carried))
        carried = carried * chunk_decay
    carried = back_in
    for q in reversed(range(CHUNKS)):
        backs.insert(0, small_residues * (chunk_lanes(small_ref[1], q) + carried))
        carried = carried * chunk_decay
    down = iota((CHUNK, CHANNELS), 0).astype(F32)
    long_far = dot3(split(jnp.exp(-row * (down + 1.0))), expand(jnp.concatenate(states, axis=1)))
    gated_far = dot3(split(jnp.exp(-row * (CHUNK - 1 - down))), expand(jnp.concatenate(backs, axis=1)))
    sums = [jnp.zeros((8, CHANNELS), F32) for _ in range(3 * KW)]
    for q in range(CHUNKS):
        rows = pl.ds(q * CHUNK, CHUNK)
        signal = out_grad_ref[rows, :].astype(F32)
        grad_gated = gated_ref[rows, :] + chunk_lanes(gated_far, q)
        parts = (
            signal * (long_ref[rows, :] + chunk_lanes(long_far, q)),
            grad_gated * kv_ref[1, rows, :],
            grad_gated * kv_ref[0, rows, :],
        )
        for i in range(3):
            feature_ref[i, rows, :] = parts[i]
            for j in range(KW):
                product = parts[i] * ext_ref[i, pl.ds(LEAD - j + q * CHUNK, CHUNK), :]
                sums[i * KW + j] = sums[i * KW + j] + jnp.sum(
                    product.reshape(CHUNK // 8, 8, CHANNELS), axis=0
                )
    residue_part, moment_part, lead_moment, end_moment = (
        chunk_lanes(small_ref[2], at) for at in range(4)
    )
    lead = small_ref[3, :, 0:CHANNELS]
    residue_part = residue_part + lead * state_in
    moment_part = moment_part + lead_moment * state_in + lead * late_in + end_moment * back_in
    same = (iota((CHANNELS, CHANNELS), 0) // WIDTH == iota((CHANNELS, CHANNELS), 1) // MODES).astype(F32)
    pick = (iota((MODES, CHANNELS), 1) % MODES == iota((MODES, CHANNELS), 0)).astype(F32)

    def by_mode(part):
        spread = lax.dot_general(part, same, MM, precision=EXACT, preferred_element_type=F32)
        return jnp.sum(spread * pick, axis=0, keepdims=True)

    residue_row = local_ref[0:1, :] + by_mode(residue_part)
    moment_row = local_ref[1:2, :] + by_mode(moment_part)
    rate_row = -row * mode_row(residues) * moment_row
    lines = [jnp.sum(part, axis=0, keepdims=True) for part in sums]
    stats = jnp.concatenate(lines + [residue_row, rate_row, jnp.zeros((1, CHANNELS), F32)], axis=0)
    for d in range(stats_ref.shape[0]):
        stats_ref[d] = stats


def inputs_kernel(feature_ref, after_ref, weight_ref, out_ref, ext_ref):
    for i in range(3):
        ext_ref[0:ROWS, :] = feature_ref[i]
        ext_ref[ROWS:, :] = after_ref[i]
        for q in range(CHUNKS):
            total = None
            for j in range(KW):
                term = weight_ref[i, j : j + 1, :] * ext_ref[pl.ds(j + q * CHUNK, CHUNK), :]
                total = term if total is None else total + term
            out_ref[i, pl.ds(q * CHUNK, CHUNK), :] = total.astype(BF16)


def total_kernel(stats_ref, total_ref, square_ref):
    total = jnp.sum(stats_ref[...], axis=0)
    total_ref[...] = total
    square = jnp.sum(total * total, axis=0, keepdims=True)
    for d in range(square_ref.shape[0]):
        square_ref[d] = jnp.broadcast_to(square, square_ref.shape[1:])


def scale_kernel(square_ref, total_ref, conv_ref, residue_ref, rate_ref):
    squares = jnp.sum(jnp.sum(square_ref[:, 0, :], axis=0, keepdims=True), axis=1, keepdims=True)
    factor = jnp.minimum(1.0, lax.rsqrt(squares / (3 * KW * D + 2 * G * MODES) + 1e-6))
    total = total_ref[...] * factor
    for i in range(3):
        conv_ref[i] = total[i * KW : (i + 1) * KW, :]
    pick = (iota((MODES, CHANNELS), 1) % MODES == iota((MODES, CHANNELS), 0)).astype(F32)
    own = lane_group(GROUPS)
    at = 3 * KW
    residue_ref[...] = lax.dot_general(
        total[at : at + 1, :] * own, pick, NT, precision=EXACT, preferred_element_type=F32
    )
    rate_ref[...] = lax.dot_general(
        total[at + 1 : at + 2, :] * own, pick, NT, precision=EXACT, preferred_element_type=F32
    )


def shape(*dims, dtype=F32):
    return jax.ShapeDtypeStruct(dims, dtype)


VMEM = pl.BlockSpec(memory_space=pltpu.VMEM)
SMEM = pl.BlockSpec(memory_space=pltpu.SMEM)


def call(kernel, name, out_shape, scalars, inputs, cost_us, scratch=()):
    return pl.pallas_call(
        kernel,
        out_shape=out_shape,
        in_specs=[SMEM] * scalars + [VMEM] * (inputs - scalars),
        out_specs=jax.tree.map(lambda _: VMEM, out_shape),
        scratch_shapes=list(scratch),
        compiler_params=pltpu.CompilerParams(vmem_limit_bytes=24 * 2**20),
        cost_estimate=pl.CostEstimate(
            flops=int(cost_us * 1e9), bytes_accessed=int(cost_us * 3e6), transcendentals=0
        ),
        name=name,
    )


def shards(projected, conv_weight, residues, decay_rates, grad_out):
    ctx = lax.axis_size("ctx")
    planes = lax.axis_size("ch")
    me = lax.axis_index("ctx").astype(jnp.int32).reshape(1)
    before = lax.ppermute(
        projected[:, ROWS - LEAD :, :], "ctx", [(source, source + 1) for source in range(ctx - 1)]
    )
    rows = shape(ROWS, CHANNELS)
    wide = shape(CHUNK, CHUNKS * CHANNELS)
    ext, kv, gi, gl, states, send = call(
        first_kernel, "features",
        (shape(3, LEAD + ROWS, CHANNELS), shape(2, ROWS, CHANNELS), wide, wide,
         shape(2, MODES, CHUNKS * CHANNELS), shape(ctx, MODES, CHANNELS)),
        1, 6, 3,
    )(me, projected, before, conv_weight, decay_rates, grad_out)
    arrived = lax.all_to_all(send, "ctx", 0, 0)
    long_near, gated_near, local, small = call(
        middle_kernel, "within",
        (rows, rows, shape(8, CHANNELS), shape(4, MODES, CHUNKS * CHANNELS)),
        0, 5, 8,
        scratch=[pltpu.VMEM((GROUPS, CHANNELS), F32)],
    )(decay_rates, residues, gi, gl, states)
    grad_feature, stats = call(
        finish_kernel, "across",
        (shape(3, ROWS, CHANNELS), shape(ctx, STATS, CHANNELS)),
        1, 11, 4,
    )(me, arrived, decay_rates, residues, small, local, long_near, gated_near, kv, grad_out, ext)
    after = lax.ppermute(
        grad_feature[:, :8, :], "ctx", [(source + 1, source) for source in range(ctx - 1)]
    )
    gathered = lax.all_to_all(stats, "ctx", 0, 0)
    grad_projected = call(
        inputs_kernel, "inputs", shape(3, ROWS, CHANNELS, dtype=BF16), 0, 3, 2,
        scratch=[pltpu.VMEM((ROWS + 8, CHANNELS), F32)],
    )(grad_feature, after, conv_weight)
    total, square = call(
        total_kernel, "total", (shape(STATS, CHANNELS), shape(planes, 8, CHANNELS)), 0, 1, 1,
    )(gathered)
    squares = lax.all_to_all(square, "ch", 0, 0)
    grad_conv, grad_residues, grad_log_rates = call(
        scale_kernel, "scale",
        (shape(3, KW, CHANNELS), shape(GROUPS, MODES), shape(GROUPS, MODES)), 0, 2, 1,
    )(squares, total)
    return grad_projected, grad_conv, grad_residues, grad_log_rates


def solution(mesh):
    in_specs = (
        P(None, "ctx", "ch"),
        P(None, None, "ch"),
        P("ch", None),
        P("ch", None),
        P("ctx", "ch"),
    )
    out_specs = (P(None, "ctx", "ch"), P(None, None, "ch"), P("ch", None), P("ch", None))
    return jax.shard_map(shards, mesh=mesh, in_specs=in_specs, out_specs=out_specs, check_vma=False)
```

```python
import jax
import jax.numpy as jnp
from jax import lax
from jax.experimental import pallas as pl
from jax.experimental.pallas import tpu as pltpu
from jax.sharding import PartitionSpec as P

D = 4096
G = 256
MODES = 16
KW = 7

ROWS = 512
CHANNELS = 128
GROUPS = 8
WIDTH = 16
CHUNK = 128
CHUNKS = ROWS // CHUNK
LEAD = 16
HEAD = 8
STATS = 24
LOCAL = (2 * CHUNKS + 5) * MODES

F32 = jnp.float32
BF16 = jnp.bfloat16
EXACT = lax.Precision.HIGHEST
MM = (((1,), (0,)), ((), ()))
NT = (((1,), (1,)), ((), ()))


def split(value):
    high = value.astype(BF16)
    low = (value - high.astype(F32)).astype(BF16)
    return high, low


def dot3(left, right, dims=MM):
    lh, ll = left
    rh, rl = right

    def product(a, b):
        return lax.dot_general(a, b, dims, preferred_element_type=F32)

    return product(lh, rh) + (product(lh, rl) + product(ll, rh))


def iota(shape, axis):
    return lax.broadcasted_iota(jnp.int32, shape, axis)


def lane_group(rows):
    return (iota((rows, CHANNELS), 1) // WIDTH == iota((rows, CHANNELS), 0)).astype(F32)


def mode_row(table):
    pick = (iota((MODES, CHANNELS), 1) % MODES == iota((MODES, CHANNELS), 0)).astype(F32)
    spread = lax.dot_general(table, pick, MM, precision=EXACT, preferred_element_type=F32)
    return jnp.sum(spread * lane_group(GROUPS), axis=0, keepdims=True)


def mode_column(row):
    eye = iota((CHANNELS, CHANNELS), 0) == iota((CHANNELS, CHANNELS), 1)
    return jnp.sum(jnp.where(eye, row, 0.0), axis=1, keepdims=True)


def mode_compact(table):
    return lax.dot_general(
        table, lane_group(GROUPS), (((0,), (0,)), ((), ())), precision=EXACT, preferred_element_type=F32
    )


def compact(full):
    lanes = full.shape[1]
    total = None
    for g in range(GROUPS):
        own = (iota((MODES, lanes), 1) % CHANNELS) // WIDTH == g
        part = jnp.where(own, full[g * MODES : (g + 1) * MODES, :], 0.0)
        total = part if total is None else total + part
    return total


def expand(small):
    lanes = small.shape[1]
    own = (iota((CHANNELS, lanes), 0) // MODES == (iota((CHANNELS, lanes), 1) % CHANNELS) // WIDTH).astype(F32)
    return split(jnp.concatenate([small] * GROUPS, axis=0) * own)


def near_parts(near_ref):
    return near_ref.at[0:ROWS, :], near_ref.at[ROWS : 2 * ROWS, :], near_ref.at[2 * ROWS :, :]


def piece(at):
    return slice(at * MODES, (at + 1) * MODES)


def chunk_lanes(value, q):
    return value[:, q * CHANNELS : (q + 1) * CHANNELS]


def prepare_kernel(weight_ref, rate_ref, residue_ref, proj_ref, out_grad_ref,
                   kv_ref, pair_ref, states_ref, ends_ref, head_ref, power_ref, table_ref,
                   raw_ref, signal_ref, ext_ref, sem_ref):
    gi_ref, gl_ref = pair_ref.at[0], pair_ref.at[1]
    copies = [
        pltpu.make_async_copy(proj_ref, raw_ref, sem_ref.at[0]),
        pltpu.make_async_copy(out_grad_ref, signal_ref, sem_ref.at[1]),
    ]
    for copy in copies:
        copy.start()
    rates = rate_ref[...]
    table_ref[0] = rates
    table_ref[1] = residue_ref[...]
    column = mode_column(mode_row(rates))
    lag = iota((CHANNELS, CHUNK), 1).astype(F32)
    ascending = split(jnp.exp(-column * lag))
    descending = split(jnp.exp(-column * (CHUNK - 1 - lag)))
    small_rates = mode_compact(rates)
    one_step = jnp.exp(-small_rates)
    chunk_decay = jnp.exp(-small_rates * CHUNK)
    for r in range(HEAD):
        power_ref[0, r] = jnp.exp(-small_rates * float(CHUNK - 1 - r))
        power_ref[1, r] = jnp.exp(-small_rates * float(r + 1))
    power_ref[2, 0] = jnp.exp(-small_rates * float(ROWS - CHUNK))
    for r in range(1, HEAD):
        power_ref[2, r] = jnp.zeros((MODES, CHANNELS), F32)
    for copy in copies:
        copy.wait()
    for i in range(3):
        ext_ref[i, 0:LEAD, :] = jnp.zeros((LEAD, CHANNELS), F32)
        ext_ref[i, LEAD:, :] = raw_ref[i].astype(F32)
    blank = jnp.zeros((HEAD, CHANNELS), F32)
    for q in range(CHUNKS):
        feature = []
        for i in range(3):
            total = None
            for j in range(KW):
                term = weight_ref[i, j : j + 1, :] * ext_ref[i, pl.ds(LEAD - j + q * CHUNK, CHUNK), :]
                total = term if total is None else total + term
            feature.append(total)
        rows = pl.ds(q * CHUNK, CHUNK)
        lanes = slice(q * CHANNELS, (q + 1) * CHANNELS)
        signal = signal_ref[rows, :].astype(F32)
        kv_ref[0, rows, :] = feature[1]
        kv_ref[1, rows, :] = feature[2]
        gi_ref[:, lanes] = feature[1] * feature[2]
        gl_ref[:, lanes] = signal * feature[0]
        if q == 0:
            for i in range(3):
                head_ref[i] = feature[i][0:HEAD, :]
            head_ref[3] = signal[0:HEAD, :]
            gi_ref[0:HEAD, lanes] = blank
            gl_ref[0:HEAD, lanes] = blank
    ends = compact(dot3(descending, split(gi_ref[...])))
    leads = compact(dot3(ascending, split(gl_ref[...])))
    state = jnp.zeros((MODES, CHANNELS), F32)
    for q in range(CHUNKS):
        part = chunk_lanes(ends, q)
        states_ref[0, :, q * CHANNELS : (q + 1) * CHANNELS] = part
        state = chunk_decay * state + part
    back = jnp.zeros((MODES, CHANNELS), F32)
    for q in reversed(range(CHUNKS)):
        part = one_step * chunk_lanes(leads, q)
        states_ref[1, :, q * CHANNELS : (q + 1) * CHANNELS] = part
        back = chunk_decay * back + part
    ends_ref[0] = state
    ends_ref[1] = back


def patch_kernel(me_ref, before_ref, weight_ref, head_ref, power_ref, ends_ref,
                 patch_ref, delta_ref, send_ref, ext_ref):
    me = me_ref[0]
    feature = []
    for i in range(3):
        ext_ref[0:LEAD, :] = before_ref[i].astype(F32)
        ext_ref[LEAD:, :] = jnp.zeros((HEAD, CHANNELS), F32)
        total = head_ref[i]
        for j in range(1, KW):
            total = total + weight_ref[i, j : j + 1, :] * ext_ref[pl.ds(LEAD - j, HEAD), :]
        feature.append(total)
    gi = feature[1] * feature[2]
    gl = head_ref[3] * feature[0]
    for at, value in enumerate((feature[1], feature[2], gi, gl)):
        patch_ref[at] = value
    state_part, back_part = None, None
    for r in range(HEAD):
        ahead = power_ref[0, r] * gi[r : r + 1, :]
        behind = power_ref[1, r] * gl[r : r + 1, :]
        state_part = ahead if r == 0 else state_part + ahead
        back_part = behind if r == 0 else back_part + behind
    delta_ref[0] = state_part
    delta_ref[1] = back_part
    state = ends_ref[0] + power_ref[2, 0] * state_part
    back = ends_ref[1] + back_part
    for d in range(send_ref.shape[0]):
        send_ref[d] = jnp.where(d > me, state, back).astype(send_ref.dtype)


def spliced(wide_ref, patch):
    top = jnp.concatenate([patch, wide_ref[0:HEAD, CHANNELS:]], axis=1)
    return jnp.concatenate([top, wide_ref[HEAD:, :]], axis=0)


def middle_kernel(table_ref, pair_ref, states_ref, patch_ref, delta_ref,
                  near_ref, lag_ref):
    long_ref, gated_ref, small_ref = near_parts(near_ref)
    gi_ref, gl_ref = pair_ref.at[0], pair_ref.at[1]
    rates = table_ref[0]
    row = mode_row(rates)
    column = mode_column(row)
    lag = iota((CHANNELS, CHUNK), 1)
    back_lag = lax.rem(CHUNK - lag, CHUNK)
    ascending = jnp.exp(-column * lag.astype(F32))
    descending = jnp.exp(-column * (CHUNK - 1 - lag).astype(F32))
    turned = jnp.exp(-column * back_lag.astype(F32))
    residue_row = mode_row(table_ref[1]) * lane_group(GROUPS)
    filters = lax.dot_general(residue_row, ascending, MM, precision=EXACT, preferred_element_type=F32)
    turned_filters = lax.dot_general(residue_row, turned, MM, precision=EXACT, preferred_element_type=F32)
    gi = split(spliced(gi_ref, patch_ref[2]))
    gl = split(spliced(gl_ref, patch_ref[3]))
    down = iota((CHUNK, CHUNK), 0)
    across = iota((CHUNK, CHUNK), 1)
    mirror = (down + across == CHUNK - 1).astype(F32).astype(BF16)
    mirrored = [
        lax.dot_general(mirror, part, MM, preferred_element_type=F32).astype(BF16) for part in gl
    ]
    wide_group = (iota((1, ROWS), 1) % CHANNELS) // WIDTH
    lane_of = iota((CHUNK, CHANNELS), 1) // WIDTH
    for g in range(GROUPS):
        straight = jnp.broadcast_to(turned_filters[g : g + 1, :], (CHUNK, CHUNK))
        straight = pltpu.roll(straight, 0, 1, stride=1, stride_axis=0)
        straight = split(jnp.where(across <= down, straight, 0.0))
        flipped = jnp.broadcast_to(filters[g : g + 1, :], (CHUNK, CHUNK))
        flipped = pltpu.roll(flipped, 0, 1, stride=1, stride_axis=0)
        flipped = split(jnp.where(across >= down, flipped, 0.0))
        forward = dot3(straight, gi)
        backward = dot3(flipped, gl)
        for q in range(CHUNKS):
            rows = pl.ds(q * CHUNK, CHUNK)
            if g == 0:
                long_ref[rows, :] = chunk_lanes(forward, q)
                gated_ref[rows, :] = chunk_lanes(backward, q)
            else:
                long_ref[rows, :] = jnp.where(lane_of == g, chunk_lanes(forward, q), long_ref[rows, :])
                gated_ref[rows, :] = jnp.where(lane_of == g, chunk_lanes(backward, q), gated_ref[rows, :])
        own = (wide_group == g).astype(F32).astype(BF16)
        products = dot3((mirrored[0] * own, mirrored[1] * own), gi, NT)
        products = jnp.where(across + down <= CHUNK - 1, products, 0.0)
        sheared = pltpu.roll(products, 1, 1, stride=1, stride_axis=0)
        lag_ref[g : g + 1, :] = jnp.sum(sheared, axis=0, keepdims=True)
    lag_grad = lag_ref[...]
    down_lag = lax.rem(CHUNK - down, CHUNK).astype(F32)
    powers = jnp.exp(-row * down_lag)
    residue_sums = lax.dot_general(lag_grad, powers, MM, precision=EXACT, preferred_element_type=F32)
    moment_sums = lax.dot_general(lag_grad, powers * down_lag, MM, precision=EXACT, preferred_element_type=F32)
    own_group = lane_group(GROUPS)
    small_ref[LOCAL : LOCAL + 1, :] = jnp.sum(residue_sums * own_group, axis=0, keepdims=True)
    small_ref[LOCAL + 1 : LOCAL + 2, :] = jnp.sum(moment_sums * own_group, axis=0, keepdims=True)
    small_rates = mode_compact(rates)
    chunk_decay = jnp.exp(-small_rates * CHUNK)
    lag_value = lag.astype(F32)
    end_moments = compact(dot3(split(descending * (CHUNK - 1 - lag_value)), gi))
    lead_moments = compact(dot3(split(ascending * (jnp.exp(-column) * (lag_value + 1.0))), gl))
    zero = jnp.zeros((MODES, CHANNELS), F32)
    leads = []
    state, moment = zero, zero
    residue_part, moment_part, lead_moment = zero, zero, zero
    offset_decay = jnp.ones((MODES, CHANNELS), F32)
    for q in range(CHUNKS):
        lead = chunk_lanes(states_ref[1], q)
        end = chunk_lanes(states_ref[0], q)
        if q == 0:
            end, lead = end + delta_ref[0], lead + delta_ref[1]
        leads.append(lead)
        lead_here = chunk_lanes(lead_moments, q)
        small_ref[piece(q), :] = state
        residue_part = residue_part + lead * state
        moment_part = moment_part + lead_here * state + lead * moment
        lead_moment = lead_moment + offset_decay * (lead_here + float(q * CHUNK) * lead)
        offset_decay = offset_decay * chunk_decay
        moment = chunk_decay * (moment + float(CHUNK) * state) + chunk_lanes(end_moments, q)
        state = chunk_decay * state + end
    back = zero
    for q in reversed(range(CHUNKS)):
        small_ref[piece(CHUNKS + q), :] = back
        back = chunk_decay * back + leads[q]
    for at, value in enumerate((residue_part, moment_part, lead_moment, moment, back)):
        small_ref[piece(2 * CHUNKS + at), :] = value


def finish_kernel(me_ref, arrived_ref, table_ref, near_ref,
                  kv_ref, patch_ref, out_grad_ref, proj_ref, before_ref, feature_ref, stats_ref, ext_ref):
    for i in range(3):
        ext_ref[i, 0:LEAD, :] = before_ref[i].astype(F32)
        ext_ref[i, LEAD:, :] = proj_ref[i].astype(F32)
    long_ref, gated_ref, small_ref = near_parts(near_ref)
    me = me_ref[0]
    rates, residues = table_ref[0], table_ref[1]
    row = mode_row(rates)
    small_rates = mode_compact(rates)
    small_residues = mode_compact(residues)
    chunk_decay = jnp.exp(-small_rates * CHUNK)
    zero = jnp.zeros((MODES, CHANNELS), F32)
    state_in, late_in, back_in = zero, zero, zero
    for d in range(arrived_ref.shape[0]):
        away = (jnp.abs(me - d) - 1).astype(F32) * float(ROWS)
        term = jnp.exp(-small_rates * away) * arrived_ref[d].astype(F32)
        state_in = state_in + jnp.where(d < me, term, 0.0)
        late_in = late_in + jnp.where(d < me, term * away, 0.0)
        back_in = back_in + jnp.where(d > me, term, 0.0)
    states, backs = [], []
    carried = state_in
    for q in range(CHUNKS):
        states.append(small_residues * (small_ref[piece(q), :] + carried))
        carried = carried * chunk_decay
    carried = back_in
    for q in reversed(range(CHUNKS)):
        backs.insert(0, small_residues * (small_ref[piece(CHUNKS + q), :] + carried))
        carried = carried * chunk_decay
    down = iota((CHUNK, CHANNELS), 0).astype(F32)
    long_far = dot3(split(jnp.exp(-row * (down + 1.0))), expand(jnp.concatenate(states, axis=1)))
    gated_far = dot3(split(jnp.exp(-row * (CHUNK - 1 - down))), expand(jnp.concatenate(backs, axis=1)))
    sums = [jnp.zeros((8, CHANNELS), F32) for _ in range(3 * KW)]
    for q in range(CHUNKS):
        rows = pl.ds(q * CHUNK, CHUNK)
        signal = out_grad_ref[rows, :].astype(F32)
        grad_gated = gated_ref[rows, :] + chunk_lanes(gated_far, q)
        keyed, valued = kv_ref[0, rows, :], kv_ref[1, rows, :]
        if q == 0:
            keyed = jnp.concatenate([patch_ref[0], keyed[HEAD:, :]], axis=0)
            valued = jnp.concatenate([patch_ref[1], valued[HEAD:, :]], axis=0)
        parts = (
            signal * (long_ref[rows, :] + chunk_lanes(long_far, q)),
            grad_gated * valued,
            grad_gated * keyed,
        )
        for i in range(3):
            feature_ref[i, rows, :] = parts[i]
            for j in range(KW):
                product = parts[i] * ext_ref[i, pl.ds(LEAD - j + q * CHUNK, CHUNK), :]
                sums[i * KW + j] = sums[i * KW + j] + jnp.sum(
                    product.reshape(CHUNK // 8, 8, CHANNELS), axis=0
                )
    residue_part, moment_part, lead_moment, end_moment, lead = (
        small_ref[piece(2 * CHUNKS + at), :] for at in range(5)
    )
    residue_part = residue_part + lead * state_in
    moment_part = moment_part + lead_moment * state_in + lead * late_in + end_moment * back_in
    same = (iota((CHANNELS, CHANNELS), 0) // WIDTH == iota((CHANNELS, CHANNELS), 1) // MODES).astype(F32)
    pick = (iota((MODES, CHANNELS), 1) % MODES == iota((MODES, CHANNELS), 0)).astype(F32)

    def by_mode(part):
        spread = lax.dot_general(part, same, MM, precision=EXACT, preferred_element_type=F32)
        return jnp.sum(spread * pick, axis=0, keepdims=True)

    residue_row = small_ref[LOCAL : LOCAL + 1, :] + by_mode(residue_part)
    moment_row = small_ref[LOCAL + 1 : LOCAL + 2, :] + by_mode(moment_part)
    rate_row = -row * mode_row(residues) * moment_row
    lines = [jnp.sum(part, axis=0, keepdims=True) for part in sums]
    stats = jnp.concatenate(lines + [residue_row, rate_row, jnp.zeros((1, CHANNELS), F32)], axis=0)
    for d in range(stats_ref.shape[0]):
        stats_ref[d] = stats


def inputs_kernel(feature_ref, after_ref, weight_ref, out_ref, ext_ref):
    for i in range(3):
        ext_ref[0:ROWS, :] = feature_ref[i]
        ext_ref[ROWS:, :] = after_ref[i]
        for q in range(CHUNKS):
            total = None
            for j in range(KW):
                term = weight_ref[i, j : j + 1, :] * ext_ref[pl.ds(j + q * CHUNK, CHUNK), :]
                total = term if total is None else total + term
            out_ref[i, pl.ds(q * CHUNK, CHUNK), :] = total.astype(BF16)


def total_kernel(stats_ref, total_ref, square_ref):
    total = jnp.sum(stats_ref[...], axis=0)
    total_ref[...] = total
    square = jnp.sum(total * total, axis=0, keepdims=True)
    for d in range(square_ref.shape[0]):
        square_ref[d] = jnp.broadcast_to(square, square_ref.shape[1:])


def scale_kernel(square_ref, total_ref, conv_ref, residue_ref, rate_ref):
    squares = jnp.sum(jnp.sum(square_ref[:, 0, :], axis=0, keepdims=True), axis=1, keepdims=True)
    factor = jnp.minimum(1.0, lax.rsqrt(squares / (3 * KW * D + 2 * G * MODES) + 1e-6))
    total = total_ref[...] * factor
    for i in range(3):
        conv_ref[i] = total[i * KW : (i + 1) * KW, :]
    pick = (iota((MODES, CHANNELS), 1) % MODES == iota((MODES, CHANNELS), 0)).astype(F32)
    own = lane_group(GROUPS)
    at = 3 * KW
    residue_ref[...] = lax.dot_general(
        total[at : at + 1, :] * own, pick, NT, precision=EXACT, preferred_element_type=F32
    )
    rate_ref[...] = lax.dot_general(
        total[at + 1 : at + 2, :] * own, pick, NT, precision=EXACT, preferred_element_type=F32
    )


def shape(*dims, dtype=F32):
    return jax.ShapeDtypeStruct(dims, dtype)


VMEM = pl.BlockSpec(memory_space=pltpu.VMEM)
SMEM = pl.BlockSpec(memory_space=pltpu.SMEM)


HBM = pl.BlockSpec(memory_space=pltpu.HBM)


def call(kernel, name, out_shape, specs, cost_us, scratch=()):
    return pl.pallas_call(
        kernel,
        out_shape=out_shape,
        in_specs=specs,
        out_specs=jax.tree.map(lambda _: VMEM, out_shape),
        scratch_shapes=list(scratch),
        compiler_params=pltpu.CompilerParams(vmem_limit_bytes=12 * 2**20),
        cost_estimate=pl.CostEstimate(
            flops=int(cost_us * 1e9), bytes_accessed=int(cost_us * 3e6), transcendentals=0
        ),
        name=name,
    )


def shards(projected, conv_weight, residues, decay_rates, grad_out):
    ctx = lax.axis_size("ctx")
    planes = lax.axis_size("ch")
    me = lax.axis_index("ctx").astype(jnp.int32).reshape(1)
    before = lax.ppermute(
        projected[:, ROWS - LEAD :, :], "ctx", [(source, source + 1) for source in range(ctx - 1)]
    )
    kv, pair, states, ends, head, powers, table = call(
        prepare_kernel, "prepare",
        (shape(2, ROWS, CHANNELS), shape(2, CHUNK, CHUNKS * CHANNELS), shape(2, MODES, CHUNKS * CHANNELS),
         shape(2, MODES, CHANNELS), shape(4, HEAD, CHANNELS), shape(3, HEAD, MODES, CHANNELS),
         shape(2, GROUPS, MODES)),
        [VMEM] * 3 + [HBM] * 2, 3,
        scratch=[pltpu.VMEM((3, ROWS, CHANNELS), BF16), pltpu.VMEM((ROWS, CHANNELS), BF16),
                 pltpu.VMEM((3, LEAD + ROWS, CHANNELS), F32), pltpu.SemaphoreType.DMA((2,))],
    )(conv_weight, decay_rates, residues,
      *(pltpu.with_memory_space_constraint(part, pltpu.HBM) for part in (projected, grad_out)))
    patch, delta, send = call(
        patch_kernel, "patch",
        (shape(4, HEAD, CHANNELS), shape(2, MODES, CHANNELS), shape(ctx, MODES, CHANNELS)),
        [SMEM] + [VMEM] * 5, 1,
        scratch=[pltpu.VMEM((LEAD + HEAD, CHANNELS), F32)],
    )(me, before, conv_weight, head, powers, ends)
    arrived = lax.all_to_all(send, "ctx", 0, 0)
    near = call(
        middle_kernel, "within",
        shape(2 * ROWS + LOCAL + 8, CHANNELS),
        [VMEM] * 5, 8,
        scratch=[pltpu.VMEM((GROUPS, CHANNELS), F32)],
    )(table, pair, states, patch, delta)
    grad_feature, stats = call(
        finish_kernel, "across",
        (shape(3, ROWS, CHANNELS), shape(ctx, STATS, CHANNELS)),
        [SMEM] + [VMEM] * 8, 4,
        scratch=[pltpu.VMEM((3, LEAD + ROWS, CHANNELS), F32)],
    )(me, arrived, table, near, kv, patch, grad_out, projected, before)
    after = lax.ppermute(
        grad_feature[:, :8, :], "ctx", [(source + 1, source) for source in range(ctx - 1)]
    )
    gathered = lax.all_to_all(stats, "ctx", 0, 0)
    grad_projected = call(
        inputs_kernel, "inputs", shape(3, ROWS, CHANNELS, dtype=BF16), [VMEM] * 3, 2,
        scratch=[pltpu.VMEM((ROWS + 8, CHANNELS), F32)],
    )(grad_feature, after, conv_weight)
    total, square = call(
        total_kernel, "total", (shape(STATS, CHANNELS), shape(planes, 1, CHANNELS)), [VMEM], 1,
    )(gathered)
    squares = lax.all_to_all(square, "ch", 0, 0)
    grad_conv, grad_residues, grad_log_rates = call(
        scale_kernel, "scale",
        (shape(3, KW, CHANNELS), shape(GROUPS, MODES), shape(GROUPS, MODES)), [VMEM] * 2, 1,
    )(squares, total)
    return grad_projected, grad_conv, grad_residues, grad_log_rates


def solution(mesh):
    in_specs = (
        P(None, "ctx", "ch"),
        P(None, None, "ch"),
        P("ch", None),
        P("ch", None),
        P("ctx", "ch"),
    )
    out_specs = (P(None, "ctx", "ch"), P(None, None, "ch"), P("ch", None), P("ch", None))
    return jax.shard_map(shards, mesh=mesh, in_specs=in_specs, out_specs=out_specs, check_vma=False)
```

```python
import jax
import jax.numpy as jnp
from jax import lax
from jax.experimental import pallas as pl
from jax.experimental.pallas import tpu as pltpu
from jax.sharding import PartitionSpec as P

D = 4096
G = 256
MODES = 16
KW = 7

ROWS = 512
CHANNELS = 128
GROUPS = 8
WIDTH = 16
CHUNK = 128
CHUNKS = ROWS // CHUNK
LEAD = 16
HEAD = 8
STATS = 24
LOCAL = (2 * CHUNKS + 5) * MODES

F32 = jnp.float32
BF16 = jnp.bfloat16
F16 = jnp.float16
EXACT = lax.Precision.HIGHEST
MM = (((1,), (0,)), ((), ()))
NT = (((1,), (1,)), ((), ()))


def split(value):
    high = value.astype(BF16)
    low = (value - high.astype(F32)).astype(BF16)
    return high, low


def dot3(left, right, dims=MM):
    lh, ll = left
    rh, rl = right

    def product(a, b):
        return lax.dot_general(a, b, dims, preferred_element_type=F32)

    return product(lh, rh) + (product(lh, rl) + product(ll, rh))


def iota(shape, axis):
    return lax.broadcasted_iota(jnp.int32, shape, axis)


def lane_group(rows):
    return (iota((rows, CHANNELS), 1) // WIDTH == iota((rows, CHANNELS), 0)).astype(F32)


def mode_row(table):
    pick = (iota((MODES, CHANNELS), 1) % MODES == iota((MODES, CHANNELS), 0)).astype(F32)
    spread = lax.dot_general(table, pick, MM, precision=EXACT, preferred_element_type=F32)
    return jnp.sum(spread * lane_group(GROUPS), axis=0, keepdims=True)


def mode_column(row):
    eye = iota((CHANNELS, CHANNELS), 0) == iota((CHANNELS, CHANNELS), 1)
    return jnp.sum(jnp.where(eye, row, 0.0), axis=1, keepdims=True)


def mode_compact(table):
    return lax.dot_general(
        table, lane_group(GROUPS), (((0,), (0,)), ((), ())), precision=EXACT, preferred_element_type=F32
    )


def compact(full):
    lanes = full.shape[1]
    total = None
    for g in range(GROUPS):
        own = (iota((MODES, lanes), 1) % CHANNELS) // WIDTH == g
        part = jnp.where(own, full[g * MODES : (g + 1) * MODES, :], 0.0)
        total = part if total is None else total + part
    return total


def expand(small):
    lanes = small.shape[1]
    own = (iota((CHANNELS, lanes), 0) // MODES == (iota((CHANNELS, lanes), 1) % CHANNELS) // WIDTH).astype(F32)
    return split(jnp.concatenate([small] * GROUPS, axis=0) * own)


def near_parts(near_ref):
    return near_ref.at[0:ROWS, :], near_ref.at[ROWS : 2 * ROWS, :], near_ref.at[2 * ROWS :, :]


def piece(at):
    return slice(at * MODES, (at + 1) * MODES)


def chunk_lanes(value, q):
    return value[:, q * CHANNELS : (q + 1) * CHANNELS]


def prepare_kernel(weight_ref, rate_ref, residue_ref, proj_ref, out_grad_ref,
                   kv_ref, pair_ref, states_ref, ends_ref, head_ref, power_ref, table_ref,
                   raw_ref, signal_ref, ext_ref, sem_ref):
    gi_ref, gl_ref = pair_ref.at[0], pair_ref.at[1]
    copies = [
        pltpu.make_async_copy(proj_ref, raw_ref, sem_ref.at[0]),
        pltpu.make_async_copy(out_grad_ref, signal_ref, sem_ref.at[1]),
    ]
    for copy in copies:
        copy.start()
    rates = rate_ref[...]
    table_ref[0] = rates
    table_ref[1] = residue_ref[...]
    column = mode_column(mode_row(rates))
    lag = iota((CHANNELS, CHUNK), 1).astype(F32)
    ascending = split(jnp.exp(-column * lag))
    descending = split(jnp.exp(-column * (CHUNK - 1 - lag)))
    small_rates = mode_compact(rates)
    one_step = jnp.exp(-small_rates)
    chunk_decay = jnp.exp(-small_rates * CHUNK)
    for r in range(HEAD):
        power_ref[0, r] = jnp.exp(-small_rates * float(CHUNK - 1 - r))
        power_ref[1, r] = jnp.exp(-small_rates * float(r + 1))
    power_ref[2, 0] = jnp.exp(-small_rates * float(ROWS - CHUNK))
    for r in range(1, HEAD):
        power_ref[2, r] = jnp.zeros((MODES, CHANNELS), F32)
    for copy in copies:
        copy.wait()
    for i in range(3):
        ext_ref[i, 0:LEAD, :] = jnp.zeros((LEAD, CHANNELS), F32)
        ext_ref[i, LEAD:, :] = raw_ref[i].astype(F32)
    blank = jnp.zeros((HEAD, CHANNELS), F32)
    for q in range(CHUNKS):
        feature = []
        for i in range(3):
            total = None
            for j in range(KW):
                term = weight_ref[i, j : j + 1, :] * ext_ref[i, pl.ds(LEAD - j + q * CHUNK, CHUNK), :]
                total = term if total is None else total + term
            feature.append(total)
        rows = pl.ds(q * CHUNK, CHUNK)
        lanes = slice(q * CHANNELS, (q + 1) * CHANNELS)
        signal = signal_ref[rows, :].astype(F32)
        kv_ref[0, rows, :] = feature[1]
        kv_ref[1, rows, :] = feature[2]
        gi_ref[:, lanes] = feature[1] * feature[2]
        gl_ref[:, lanes] = signal * feature[0]
        if q == 0:
            for i in range(3):
                head_ref[i] = feature[i][0:HEAD, :]
            head_ref[3] = signal[0:HEAD, :]
            gi_ref[0:HEAD, lanes] = blank
            gl_ref[0:HEAD, lanes] = blank
    ends = compact(dot3(descending, split(gi_ref[...])))
    leads = compact(dot3(ascending, split(gl_ref[...])))
    state = jnp.zeros((MODES, CHANNELS), F32)
    for q in range(CHUNKS):
        part = chunk_lanes(ends, q)
        states_ref[0, :, q * CHANNELS : (q + 1) * CHANNELS] = part
        state = chunk_decay * state + part
    back = jnp.zeros((MODES, CHANNELS), F32)
    for q in reversed(range(CHUNKS)):
        part = one_step * chunk_lanes(leads, q)
        states_ref[1, :, q * CHANNELS : (q + 1) * CHANNELS] = part
        back = chunk_decay * back + part
    ends_ref[0] = state
    ends_ref[1] = back


def patch_kernel(me_ref, before_ref, weight_ref, head_ref, power_ref, ends_ref,
                 patch_ref, delta_ref, send_ref, ext_ref):
    me = me_ref[0]
    feature = []
    for i in range(3):
        ext_ref[0:LEAD, :] = before_ref[i].astype(F32)
        ext_ref[LEAD:, :] = jnp.zeros((HEAD, CHANNELS), F32)
        total = head_ref[i]
        for j in range(1, KW):
            total = total + weight_ref[i, j : j + 1, :] * ext_ref[pl.ds(LEAD - j, HEAD), :]
        feature.append(total)
    gi = feature[1] * feature[2]
    gl = head_ref[3] * feature[0]
    for at, value in enumerate((feature[1], feature[2], gi, gl)):
        patch_ref[at] = value
    state_part, back_part = None, None
    for r in range(HEAD):
        ahead = power_ref[0, r] * gi[r : r + 1, :]
        behind = power_ref[1, r] * gl[r : r + 1, :]
        state_part = ahead if r == 0 else state_part + ahead
        back_part = behind if r == 0 else back_part + behind
    delta_ref[0] = state_part
    delta_ref[1] = back_part
    state = ends_ref[0] + power_ref[2, 0] * state_part
    back = ends_ref[1] + back_part
    for d in range(send_ref.shape[0]):
        send_ref[d] = jnp.where(d > me, state, back).astype(send_ref.dtype)


def spliced(wide_ref, patch):
    top = jnp.concatenate([patch, wide_ref[0:HEAD, CHANNELS:]], axis=1)
    return jnp.concatenate([top, wide_ref[HEAD:, :]], axis=0)


def middle_kernel(table_ref, pair_ref, states_ref, patch_ref, delta_ref,
                  near_ref, lag_ref):
    long_ref, gated_ref, small_ref = near_parts(near_ref)
    gi_ref, gl_ref = pair_ref.at[0], pair_ref.at[1]
    rates = table_ref[0]
    row = mode_row(rates)
    column = mode_column(row)
    lag = iota((CHANNELS, CHUNK), 1)
    back_lag = lax.rem(CHUNK - lag, CHUNK)
    ascending = jnp.exp(-column * lag.astype(F32))
    descending = jnp.exp(-column * (CHUNK - 1 - lag).astype(F32))
    turned = jnp.exp(-column * back_lag.astype(F32))
    residue_row = mode_row(table_ref[1]) * lane_group(GROUPS)
    filters = lax.dot_general(residue_row, ascending, MM, precision=EXACT, preferred_element_type=F32)
    turned_filters = lax.dot_general(residue_row, turned, MM, precision=EXACT, preferred_element_type=F32)
    gi = split(spliced(gi_ref, patch_ref[2]))
    gl = split(spliced(gl_ref, patch_ref[3]))
    down = iota((CHUNK, CHUNK), 0)
    across = iota((CHUNK, CHUNK), 1)
    mirror = (down + across == CHUNK - 1).astype(F32).astype(BF16)
    mirrored = [
        lax.dot_general(mirror, part, MM, preferred_element_type=F32).astype(BF16) for part in gl
    ]
    wide_group = (iota((1, ROWS), 1) % CHANNELS) // WIDTH
    lane_of = iota((CHUNK, CHANNELS), 1) // WIDTH
    for g in range(GROUPS):
        straight = jnp.broadcast_to(turned_filters[g : g + 1, :], (CHUNK, CHUNK))
        straight = pltpu.roll(straight, 0, 1, stride=1, stride_axis=0)
        straight = split(jnp.where(across <= down, straight, 0.0))
        flipped = jnp.broadcast_to(filters[g : g + 1, :], (CHUNK, CHUNK))
        flipped = pltpu.roll(flipped, 0, 1, stride=1, stride_axis=0)
        flipped = split(jnp.where(across >= down, flipped, 0.0))
        forward = dot3(straight, gi)
        backward = dot3(flipped, gl)
        for q in range(CHUNKS):
            rows = pl.ds(q * CHUNK, CHUNK)
            if g == 0:
                long_ref[rows, :] = chunk_lanes(forward, q)
                gated_ref[rows, :] = chunk_lanes(backward, q)
            else:
                long_ref[rows, :] = jnp.where(lane_of == g, chunk_lanes(forward, q), long_ref[rows, :])
                gated_ref[rows, :] = jnp.where(lane_of == g, chunk_lanes(backward, q), gated_ref[rows, :])
        own = (wide_group == g).astype(F32).astype(BF16)
        products = dot3((mirrored[0] * own, mirrored[1] * own), gi, NT)
        products = jnp.where(across + down <= CHUNK - 1, products, 0.0)
        sheared = pltpu.roll(products, 1, 1, stride=1, stride_axis=0)
        lag_ref[g : g + 1, :] = jnp.sum(sheared, axis=0, keepdims=True)
    lag_grad = lag_ref[...]
    down_lag = lax.rem(CHUNK - down, CHUNK).astype(F32)
    powers = jnp.exp(-row * down_lag)
    residue_sums = lax.dot_general(lag_grad, powers, MM, precision=EXACT, preferred_element_type=F32)
    moment_sums = lax.dot_general(lag_grad, powers * down_lag, MM, precision=EXACT, preferred_element_type=F32)
    own_group = lane_group(GROUPS)
    small_ref[LOCAL : LOCAL + 1, :] = jnp.sum(residue_sums * own_group, axis=0, keepdims=True)
    small_ref[LOCAL + 1 : LOCAL + 2, :] = jnp.sum(moment_sums * own_group, axis=0, keepdims=True)
    small_rates = mode_compact(rates)
    chunk_decay = jnp.exp(-small_rates * CHUNK)
    lag_value = lag.astype(F32)
    end_moments = compact(dot3(split(descending * (CHUNK - 1 - lag_value)), gi))
    lead_moments = compact(dot3(split(ascending * (jnp.exp(-column) * (lag_value + 1.0))), gl))
    zero = jnp.zeros((MODES, CHANNELS), F32)
    leads = []
    state, moment = zero, zero
    residue_part, moment_part, lead_moment = zero, zero, zero
    offset_decay = jnp.ones((MODES, CHANNELS), F32)
    for q in range(CHUNKS):
        lead = chunk_lanes(states_ref[1], q)
        end = chunk_lanes(states_ref[0], q)
        if q == 0:
            end, lead = end + delta_ref[0], lead + delta_ref[1]
        leads.append(lead)
        lead_here = chunk_lanes(lead_moments, q)
        small_ref[piece(q), :] = state
        residue_part = residue_part + lead * state
        moment_part = moment_part + lead_here * state + lead * moment
        lead_moment = lead_moment + offset_decay * (lead_here + float(q * CHUNK) * lead)
        offset_decay = offset_decay * chunk_decay
        moment = chunk_decay * (moment + float(CHUNK) * state) + chunk_lanes(end_moments, q)
        state = chunk_decay * state + end
    back = zero
    for q in reversed(range(CHUNKS)):
        small_ref[piece(CHUNKS + q), :] = back
        back = chunk_decay * back + leads[q]
    for at, value in enumerate((residue_part, moment_part, lead_moment, moment, back)):
        small_ref[piece(2 * CHUNKS + at), :] = value


def finish_kernel(me_ref, arrived_ref, table_ref, near_ref,
                  kv_ref, patch_ref, out_grad_ref, proj_ref, before_ref, feature_ref, stats_ref, ext_ref):
    for i in range(3):
        ext_ref[i, 0:LEAD, :] = before_ref[i].astype(F32)
        ext_ref[i, LEAD:, :] = proj_ref[i].astype(F32)
    long_ref, gated_ref, small_ref = near_parts(near_ref)
    me = me_ref[0]
    rates, residues = table_ref[0], table_ref[1]
    row = mode_row(rates)
    small_rates = mode_compact(rates)
    small_residues = mode_compact(residues)
    chunk_decay = jnp.exp(-small_rates * CHUNK)
    zero = jnp.zeros((MODES, CHANNELS), F32)
    state_in, late_in, back_in = zero, zero, zero
    for d in range(arrived_ref.shape[0]):
        away = (jnp.abs(me - d) - 1).astype(F32) * float(ROWS)
        term = jnp.exp(-small_rates * away) * arrived_ref[d].astype(F32)
        state_in = state_in + jnp.where(d < me, term, 0.0)
        late_in = late_in + jnp.where(d < me, term * away, 0.0)
        back_in = back_in + jnp.where(d > me, term, 0.0)
    states, backs = [], []
    carried = state_in
    for q in range(CHUNKS):
        states.append(small_residues * (small_ref[piece(q), :] + carried))
        carried = carried * chunk_decay
    carried = back_in
    for q in reversed(range(CHUNKS)):
        backs.insert(0, small_residues * (small_ref[piece(CHUNKS + q), :] + carried))
        carried = carried * chunk_decay
    down = iota((CHUNK, CHANNELS), 0).astype(F32)
    long_far = dot3(split(jnp.exp(-row * (down + 1.0))), expand(jnp.concatenate(states, axis=1)))
    gated_far = dot3(split(jnp.exp(-row * (CHUNK - 1 - down))), expand(jnp.concatenate(backs, axis=1)))
    sums = [jnp.zeros((8, CHANNELS), F32) for _ in range(3 * KW)]
    for q in range(CHUNKS):
        rows = pl.ds(q * CHUNK, CHUNK)
        signal = out_grad_ref[rows, :].astype(F32)
        grad_gated = gated_ref[rows, :] + chunk_lanes(gated_far, q)
        keyed, valued = kv_ref[0, rows, :], kv_ref[1, rows, :]
        if q == 0:
            keyed = jnp.concatenate([patch_ref[0], keyed[HEAD:, :]], axis=0)
            valued = jnp.concatenate([patch_ref[1], valued[HEAD:, :]], axis=0)
        parts = (
            signal * (long_ref[rows, :] + chunk_lanes(long_far, q)),
            grad_gated * valued,
            grad_gated * keyed,
        )
        for i in range(3):
            feature_ref[i, rows, :] = parts[i]
            for j in range(KW):
                product = parts[i] * ext_ref[i, pl.ds(LEAD - j + q * CHUNK, CHUNK), :]
                sums[i * KW + j] = sums[i * KW + j] + jnp.sum(
                    product.reshape(CHUNK // 8, 8, CHANNELS), axis=0
                )
    residue_part, moment_part, lead_moment, end_moment, lead = (
        small_ref[piece(2 * CHUNKS + at), :] for at in range(5)
    )
    residue_part = residue_part + lead * state_in
    moment_part = moment_part + lead_moment * state_in + lead * late_in + end_moment * back_in
    same = (iota((CHANNELS, CHANNELS), 0) // WIDTH == iota((CHANNELS, CHANNELS), 1) // MODES).astype(F32)
    pick = (iota((MODES, CHANNELS), 1) % MODES == iota((MODES, CHANNELS), 0)).astype(F32)

    def by_mode(part):
        spread = lax.dot_general(part, same, MM, precision=EXACT, preferred_element_type=F32)
        return jnp.sum(spread * pick, axis=0, keepdims=True)

    residue_row = small_ref[LOCAL : LOCAL + 1, :] + by_mode(residue_part)
    moment_row = small_ref[LOCAL + 1 : LOCAL + 2, :] + by_mode(moment_part)
    rate_row = -row * mode_row(residues) * moment_row
    lines = [jnp.sum(part, axis=0, keepdims=True) for part in sums]
    stats = jnp.concatenate(lines + [residue_row, rate_row, jnp.zeros((1, CHANNELS), F32)], axis=0)
    largest = jnp.max(jnp.abs(stats), axis=0, keepdims=True)
    exponent = jnp.ceil(jnp.log2(jnp.maximum(largest, 1e-30))) - 15.0
    last = iota((STATS, CHANNELS), 0) == STATS - 1
    stats_ref[...] = jnp.where(last, exponent, stats * jnp.exp2(-exponent))


def inputs_kernel(feature_ref, after_ref, weight_ref, out_ref, ext_ref):
    for i in range(3):
        ext_ref[0:ROWS, :] = feature_ref[i]
        ext_ref[ROWS:, :] = after_ref[i]
        for q in range(CHUNKS):
            total = None
            for j in range(KW):
                term = weight_ref[i, j : j + 1, :] * ext_ref[pl.ds(j + q * CHUNK, CHUNK), :]
                total = term if total is None else total + term
            out_ref[i, pl.ds(q * CHUNK, CHUNK), :] = total.astype(BF16)


def total_kernel(stats_ref, total_ref, square_ref):
    total = jnp.zeros((STATS, CHANNELS), F32)
    for d in range(stats_ref.shape[0]):
        total = total + stats_ref[d] * jnp.exp2(stats_ref[d, STATS - 1 :, :])
    total = jnp.where(iota((STATS, CHANNELS), 0) == STATS - 1, 0.0, total)
    total_ref[...] = total
    square = jnp.sum(total * total, axis=0, keepdims=True)
    for d in range(square_ref.shape[0]):
        square_ref[d] = jnp.broadcast_to(square, square_ref.shape[1:])


def scale_kernel(square_ref, total_ref, conv_ref, residue_ref, rate_ref):
    squares = jnp.sum(jnp.sum(square_ref[:, 0, :], axis=0, keepdims=True), axis=1, keepdims=True)
    factor = jnp.minimum(1.0, lax.rsqrt(squares / (3 * KW * D + 2 * G * MODES) + 1e-6))
    total = total_ref[...] * factor
    for i in range(3):
        conv_ref[i] = total[i * KW : (i + 1) * KW, :]
    pick = (iota((MODES, CHANNELS), 1) % MODES == iota((MODES, CHANNELS), 0)).astype(F32)
    own = lane_group(GROUPS)
    at = 3 * KW
    residue_ref[...] = lax.dot_general(
        total[at : at + 1, :] * own, pick, NT, precision=EXACT, preferred_element_type=F32
    )
    rate_ref[...] = lax.dot_general(
        total[at + 1 : at + 2, :] * own, pick, NT, precision=EXACT, preferred_element_type=F32
    )


def shape(*dims, dtype=F32):
    return jax.ShapeDtypeStruct(dims, dtype)


VMEM = pl.BlockSpec(memory_space=pltpu.VMEM)
SMEM = pl.BlockSpec(memory_space=pltpu.SMEM)


HBM = pl.BlockSpec(memory_space=pltpu.HBM)


def call(kernel, name, out_shape, specs, cost_us, scratch=()):
    return pl.pallas_call(
        kernel,
        out_shape=out_shape,
        in_specs=specs,
        out_specs=jax.tree.map(lambda _: VMEM, out_shape),
        scratch_shapes=list(scratch),
        compiler_params=pltpu.CompilerParams(vmem_limit_bytes=12 * 2**20),
        cost_estimate=pl.CostEstimate(
            flops=int(cost_us * 1e9), bytes_accessed=int(cost_us * 3e6), transcendentals=0
        ),
        name=name,
    )


def shards(projected, conv_weight, residues, decay_rates, grad_out):
    ctx = lax.axis_size("ctx")
    planes = lax.axis_size("ch")
    me = lax.axis_index("ctx").astype(jnp.int32).reshape(1)
    before = lax.ppermute(
        projected[:, ROWS - LEAD :, :], "ctx", [(source, source + 1) for source in range(ctx - 1)]
    )
    kv, pair, states, ends, head, powers, table = call(
        prepare_kernel, "prepare",
        (shape(2, ROWS, CHANNELS), shape(2, CHUNK, CHUNKS * CHANNELS), shape(2, MODES, CHUNKS * CHANNELS),
         shape(2, MODES, CHANNELS), shape(4, HEAD, CHANNELS), shape(3, HEAD, MODES, CHANNELS),
         shape(2, GROUPS, MODES)),
        [VMEM] * 3 + [HBM] * 2, 3,
        scratch=[pltpu.VMEM((3, ROWS, CHANNELS), BF16), pltpu.VMEM((ROWS, CHANNELS), BF16),
                 pltpu.VMEM((3, LEAD + ROWS, CHANNELS), F32), pltpu.SemaphoreType.DMA((2,))],
    )(conv_weight, decay_rates, residues,
      *(pltpu.with_memory_space_constraint(part, pltpu.HBM) for part in (projected, grad_out)))
    patch, delta, send = call(
        patch_kernel, "patch",
        (shape(4, HEAD, CHANNELS), shape(2, MODES, CHANNELS), shape(ctx, MODES, CHANNELS)),
        [SMEM] + [VMEM] * 5, 1,
        scratch=[pltpu.VMEM((LEAD + HEAD, CHANNELS), F32)],
    )(me, before, conv_weight, head, powers, ends)
    arrived = lax.all_to_all(send, "ctx", 0, 0)
    near = call(
        middle_kernel, "within",
        shape(2 * ROWS + LOCAL + 8, CHANNELS),
        [VMEM] * 5, 8,
        scratch=[pltpu.VMEM((GROUPS, CHANNELS), F32)],
    )(table, pair, states, patch, delta)
    grad_feature, stats = call(
        finish_kernel, "across",
        (shape(3, ROWS, CHANNELS), shape(STATS, CHANNELS)),
        [SMEM] + [VMEM] * 8, 4,
        scratch=[pltpu.VMEM((3, LEAD + ROWS, CHANNELS), F32)],
    )(me, arrived, table, near, kv, patch, grad_out, projected, before)
    after = lax.ppermute(
        grad_feature[:, :8, :], "ctx", [(source + 1, source) for source in range(ctx - 1)]
    )
    stats = jnp.broadcast_to(stats.astype(F16), (ctx, STATS, CHANNELS))
    gathered = lax.all_to_all(stats, "ctx", 0, 0).astype(F32)
    grad_projected = call(
        inputs_kernel, "inputs", shape(3, ROWS, CHANNELS, dtype=BF16), [VMEM] * 3, 2,
        scratch=[pltpu.VMEM((ROWS + 8, CHANNELS), F32)],
    )(grad_feature, after, conv_weight)
    total, square = call(
        total_kernel, "total", (shape(STATS, CHANNELS), shape(planes, 1, CHANNELS)), [VMEM], 1,
    )(gathered)
    squares = lax.all_to_all(square, "ch", 0, 0)
    grad_conv, grad_residues, grad_log_rates = call(
        scale_kernel, "scale",
        (shape(3, KW, CHANNELS), shape(GROUPS, MODES), shape(GROUPS, MODES)), [VMEM] * 2, 1,
    )(squares, total)
    return grad_projected, grad_conv, grad_residues, grad_log_rates


def solution(mesh):
    in_specs = (
        P(None, "ctx", "ch"),
        P(None, None, "ch"),
        P("ch", None),
        P("ch", None),
        P("ctx", "ch"),
    )
    out_specs = (P(None, "ctx", "ch"), P(None, None, "ch"), P("ch", None), P("ch", None))
    return jax.shard_map(shards, mesh=mesh, in_specs=in_specs, out_specs=out_specs, check_vma=False)
```

```python
import jax
import jax.numpy as jnp
from jax import lax
from jax.experimental import pallas as pl
from jax.experimental.pallas import tpu as pltpu
from jax.sharding import PartitionSpec as P

D = 4096
G = 256
MODES = 16
KW = 7

ROWS = 512
CHANNELS = 128
GROUPS = 8
WIDTH = 16
CHUNK = 128
CHUNKS = ROWS // CHUNK
LEAD = 16
HEAD = 8
STATS = 24
LOCAL = (2 * CHUNKS + 5) * MODES

F32 = jnp.float32
BF16 = jnp.bfloat16
F16 = jnp.float16
EXACT = lax.Precision.HIGHEST
MM = (((1,), (0,)), ((), ()))
NT = (((1,), (1,)), ((), ()))


def split(value):
    high = value.astype(BF16)
    low = (value - high.astype(F32)).astype(BF16)
    return high, low


def dot3(left, right, dims=MM):
    lh, ll = left
    rh, rl = right

    def product(a, b):
        return lax.dot_general(a, b, dims, preferred_element_type=F32)

    return product(lh, rh) + (product(lh, rl) + product(ll, rh))


def iota(shape, axis):
    return lax.broadcasted_iota(jnp.int32, shape, axis)


def lane_group(rows):
    return (iota((rows, CHANNELS), 1) // WIDTH == iota((rows, CHANNELS), 0)).astype(F32)


def mode_row(table):
    pick = (iota((MODES, CHANNELS), 1) % MODES == iota((MODES, CHANNELS), 0)).astype(F32)
    spread = lax.dot_general(table, pick, MM, precision=EXACT, preferred_element_type=F32)
    return jnp.sum(spread * lane_group(GROUPS), axis=0, keepdims=True)


def mode_column(row):
    eye = iota((CHANNELS, CHANNELS), 0) == iota((CHANNELS, CHANNELS), 1)
    return jnp.sum(jnp.where(eye, row, 0.0), axis=1, keepdims=True)


def mode_compact(table):
    return lax.dot_general(
        table, lane_group(GROUPS), (((0,), (0,)), ((), ())), precision=EXACT, preferred_element_type=F32
    )


def compact(full):
    lanes = full.shape[1]
    total = None
    for g in range(GROUPS):
        own = (iota((MODES, lanes), 1) % CHANNELS) // WIDTH == g
        part = jnp.where(own, full[g * MODES : (g + 1) * MODES, :], 0.0)
        total = part if total is None else total + part
    return total


def expand(small):
    lanes = small.shape[1]
    own = (iota((CHANNELS, lanes), 0) // MODES == (iota((CHANNELS, lanes), 1) % CHANNELS) // WIDTH).astype(F32)
    return split(jnp.concatenate([small] * GROUPS, axis=0) * own)


def near_parts(near_ref):
    return near_ref.at[0:ROWS, :], near_ref.at[ROWS : 2 * ROWS, :], near_ref.at[2 * ROWS :, :]


def piece(at):
    return slice(at * MODES, (at + 1) * MODES)


def chunk_lanes(value, q):
    return value[:, q * CHANNELS : (q + 1) * CHANNELS]


def prepare_kernel(weight_ref, rate_ref, residue_ref, proj_ref, out_grad_ref,
                   kv_ref, pair_ref, states_ref, ends_ref, head_ref, power_ref, table_ref,
                   raw_ref, signal_ref, ext_ref, sem_ref):
    gi_ref, gl_ref = pair_ref.at[0], pair_ref.at[1]
    copies = [
        pltpu.make_async_copy(proj_ref, raw_ref, sem_ref.at[0]),
        pltpu.make_async_copy(out_grad_ref, signal_ref, sem_ref.at[1]),
    ]
    for copy in copies:
        copy.start()
    rates = rate_ref[...]
    table_ref[0] = rates
    table_ref[1] = residue_ref[...]
    column = mode_column(mode_row(rates))
    lag = iota((CHANNELS, CHUNK), 1).astype(F32)
    ascending = split(jnp.exp(-column * lag))
    descending = split(jnp.exp(-column * (CHUNK - 1 - lag)))
    small_rates = mode_compact(rates)
    one_step = jnp.exp(-small_rates)
    chunk_decay = jnp.exp(-small_rates * CHUNK)
    for r in range(HEAD):
        power_ref[0, r] = jnp.exp(-small_rates * float(CHUNK - 1 - r))
        power_ref[1, r] = jnp.exp(-small_rates * float(r + 1))
    power_ref[2, 0] = jnp.exp(-small_rates * float(ROWS - CHUNK))
    for r in range(1, HEAD):
        power_ref[2, r] = jnp.zeros((MODES, CHANNELS), F32)
    for copy in copies:
        copy.wait()
    for i in range(3):
        ext_ref[i, 0:LEAD, :] = jnp.zeros((LEAD, CHANNELS), F32)
        ext_ref[i, LEAD:, :] = raw_ref[i].astype(F32)
    blank = jnp.zeros((HEAD, CHANNELS), F32)
    for q in range(CHUNKS):
        feature = []
        for i in range(3):
            total = None
            for j in range(KW):
                term = weight_ref[i, j : j + 1, :] * ext_ref[i, pl.ds(LEAD - j + q * CHUNK, CHUNK), :]
                total = term if total is None else total + term
            feature.append(total)
        rows = pl.ds(q * CHUNK, CHUNK)
        lanes = slice(q * CHANNELS, (q + 1) * CHANNELS)
        signal = signal_ref[rows, :].astype(F32)
        kv_ref[0, rows, :] = feature[1]
        kv_ref[1, rows, :] = feature[2]
        gi_ref[:, lanes] = feature[1] * feature[2]
        gl_ref[:, lanes] = signal * feature[0]
        if q == 0:
            for i in range(3):
                head_ref[i] = feature[i][0:HEAD, :]
            head_ref[3] = signal[0:HEAD, :]
            gi_ref[0:HEAD, lanes] = blank
            gl_ref[0:HEAD, lanes] = blank
    ends = compact(dot3(descending, split(gi_ref[...])))
    leads = compact(dot3(ascending, split(gl_ref[...])))
    state = jnp.zeros((MODES, CHANNELS), F32)
    for q in range(CHUNKS):
        part = chunk_lanes(ends, q)
        states_ref[0, :, q * CHANNELS : (q + 1) * CHANNELS] = part
        state = chunk_decay * state + part
    back = jnp.zeros((MODES, CHANNELS), F32)
    for q in reversed(range(CHUNKS)):
        part = one_step * chunk_lanes(leads, q)
        states_ref[1, :, q * CHANNELS : (q + 1) * CHANNELS] = part
        back = chunk_decay * back + part
    ends_ref[0] = state
    ends_ref[1] = back


def scaled_columns(value):
    largest = jnp.max(jnp.abs(value), axis=0, keepdims=True)
    exponent = jnp.ceil(jnp.log2(jnp.maximum(largest, 1e-30))) - 15.0
    return value * jnp.exp2(-exponent), exponent


def patch_kernel(before_ref, weight_ref, head_ref, power_ref, ends_ref,
                 patch_ref, delta_ref, send_ref, ext_ref):
    feature = []
    for i in range(3):
        ext_ref[0:LEAD, :] = before_ref[i].astype(F32)
        ext_ref[LEAD:, :] = jnp.zeros((HEAD, CHANNELS), F32)
        total = head_ref[i]
        for j in range(1, KW):
            total = total + weight_ref[i, j : j + 1, :] * ext_ref[pl.ds(LEAD - j, HEAD), :]
        feature.append(total)
    gi = feature[1] * feature[2]
    gl = head_ref[3] * feature[0]
    for at, value in enumerate((feature[1], feature[2], gi, gl)):
        patch_ref[at] = value
    state_part, back_part = None, None
    for r in range(HEAD):
        ahead = power_ref[0, r] * gi[r : r + 1, :]
        behind = power_ref[1, r] * gl[r : r + 1, :]
        state_part = ahead if r == 0 else state_part + ahead
        back_part = behind if r == 0 else back_part + behind
    delta_ref[0] = state_part
    delta_ref[1] = back_part
    state = ends_ref[0] + power_ref[2, 0] * state_part
    back = ends_ref[1] + back_part
    for at, value in enumerate((back, state)):
        scaled, exponent = scaled_columns(value)
        send_ref[at, 0:MODES, :] = scaled
        send_ref[at, MODES:, :] = jnp.broadcast_to(exponent, (8, CHANNELS))


def spliced(wide_ref, patch):
    top = jnp.concatenate([patch, wide_ref[0:HEAD, CHANNELS:]], axis=1)
    return jnp.concatenate([top, wide_ref[HEAD:, :]], axis=0)


def middle_kernel(table_ref, pair_ref, states_ref, patch_ref, delta_ref,
                  near_ref, lag_ref):
    long_ref, gated_ref, small_ref = near_parts(near_ref)
    gi_ref, gl_ref = pair_ref.at[0], pair_ref.at[1]
    rates = table_ref[0]
    row = mode_row(rates)
    column = mode_column(row)
    lag = iota((CHANNELS, CHUNK), 1)
    back_lag = lax.rem(CHUNK - lag, CHUNK)
    ascending = jnp.exp(-column * lag.astype(F32))
    descending = jnp.exp(-column * (CHUNK - 1 - lag).astype(F32))
    turned = jnp.exp(-column * back_lag.astype(F32))
    residue_row = mode_row(table_ref[1]) * lane_group(GROUPS)
    filters = lax.dot_general(residue_row, ascending, MM, precision=EXACT, preferred_element_type=F32)
    turned_filters = lax.dot_general(residue_row, turned, MM, precision=EXACT, preferred_element_type=F32)
    gi = split(spliced(gi_ref, patch_ref[2]))
    gl = split(spliced(gl_ref, patch_ref[3]))
    down = iota((CHUNK, CHUNK), 0)
    across = iota((CHUNK, CHUNK), 1)
    mirror = (down + across == CHUNK - 1).astype(F32).astype(BF16)
    mirrored = [
        lax.dot_general(mirror, part, MM, preferred_element_type=F32).astype(BF16) for part in gl
    ]
    wide_group = (iota((1, ROWS), 1) % CHANNELS) // WIDTH
    lane_of = iota((CHUNK, CHANNELS), 1) // WIDTH
    for g in range(GROUPS):
        straight = jnp.broadcast_to(turned_filters[g : g + 1, :], (CHUNK, CHUNK))
        straight = pltpu.roll(straight, 0, 1, stride=1, stride_axis=0)
        straight = split(jnp.where(across <= down, straight, 0.0))
        flipped = jnp.broadcast_to(filters[g : g + 1, :], (CHUNK, CHUNK))
        flipped = pltpu.roll(flipped, 0, 1, stride=1, stride_axis=0)
        flipped = split(jnp.where(across >= down, flipped, 0.0))
        forward = dot3(straight, gi)
        backward = dot3(flipped, gl)
        for q in range(CHUNKS):
            rows = pl.ds(q * CHUNK, CHUNK)
            if g == 0:
                long_ref[rows, :] = chunk_lanes(forward, q)
                gated_ref[rows, :] = chunk_lanes(backward, q)
            else:
                long_ref[rows, :] = jnp.where(lane_of == g, chunk_lanes(forward, q), long_ref[rows, :])
                gated_ref[rows, :] = jnp.where(lane_of == g, chunk_lanes(backward, q), gated_ref[rows, :])
        own = (wide_group == g).astype(F32).astype(BF16)
        products = dot3((mirrored[0] * own, mirrored[1] * own), gi, NT)
        products = jnp.where(across + down <= CHUNK - 1, products, 0.0)
        sheared = pltpu.roll(products, 1, 1, stride=1, stride_axis=0)
        lag_ref[g : g + 1, :] = jnp.sum(sheared, axis=0, keepdims=True)
    lag_grad = lag_ref[...]
    down_lag = lax.rem(CHUNK - down, CHUNK).astype(F32)
    powers = jnp.exp(-row * down_lag)
    residue_sums = lax.dot_general(lag_grad, powers, MM, precision=EXACT, preferred_element_type=F32)
    moment_sums = lax.dot_general(lag_grad, powers * down_lag, MM, precision=EXACT, preferred_element_type=F32)
    own_group = lane_group(GROUPS)
    small_ref[LOCAL : LOCAL + 1, :] = jnp.sum(residue_sums * own_group, axis=0, keepdims=True)
    small_ref[LOCAL + 1 : LOCAL + 2, :] = jnp.sum(moment_sums * own_group, axis=0, keepdims=True)
    small_rates = mode_compact(rates)
    chunk_decay = jnp.exp(-small_rates * CHUNK)
    lag_value = lag.astype(F32)
    end_moments = compact(dot3(split(descending * (CHUNK - 1 - lag_value)), gi))
    lead_moments = compact(dot3(split(ascending * (jnp.exp(-column) * (lag_value + 1.0))), gl))
    zero = jnp.zeros((MODES, CHANNELS), F32)
    leads = []
    state, moment = zero, zero
    residue_part, moment_part, lead_moment = zero, zero, zero
    offset_decay = jnp.ones((MODES, CHANNELS), F32)
    for q in range(CHUNKS):
        lead = chunk_lanes(states_ref[1], q)
        end = chunk_lanes(states_ref[0], q)
        if q == 0:
            end, lead = end + delta_ref[0], lead + delta_ref[1]
        leads.append(lead)
        lead_here = chunk_lanes(lead_moments, q)
        small_ref[piece(q), :] = state
        residue_part = residue_part + lead * state
        moment_part = moment_part + lead_here * state + lead * moment
        lead_moment = lead_moment + offset_decay * (lead_here + float(q * CHUNK) * lead)
        offset_decay = offset_decay * chunk_decay
        moment = chunk_decay * (moment + float(CHUNK) * state) + chunk_lanes(end_moments, q)
        state = chunk_decay * state + end
    back = zero
    for q in reversed(range(CHUNKS)):
        small_ref[piece(CHUNKS + q), :] = back
        back = chunk_decay * back + leads[q]
    for at, value in enumerate((residue_part, moment_part, lead_moment, moment, back)):
        small_ref[piece(2 * CHUNKS + at), :] = value


def finish_kernel(me_ref, arrived_ref, table_ref, near_ref,
                  kv_ref, patch_ref, out_grad_ref, proj_ref, before_ref, feature_ref, stats_ref, ext_ref):
    for i in range(3):
        ext_ref[i, 0:LEAD, :] = before_ref[i].astype(F32)
        ext_ref[i, LEAD:, :] = proj_ref[i].astype(F32)
    long_ref, gated_ref, small_ref = near_parts(near_ref)
    me = me_ref[0]
    rates, residues = table_ref[0], table_ref[1]
    row = mode_row(rates)
    small_rates = mode_compact(rates)
    small_residues = mode_compact(residues)
    chunk_decay = jnp.exp(-small_rates * CHUNK)
    zero = jnp.zeros((MODES, CHANNELS), F32)
    state_in, late_in, back_in = zero, zero, zero
    for d in range(arrived_ref.shape[0]):
        away = (jnp.abs(me - d) - 1).astype(F32) * float(ROWS)
        scale = jnp.exp2(arrived_ref[d, MODES : MODES + 1, :])
        term = jnp.exp(-small_rates * away) * (arrived_ref[d, 0:MODES, :] * scale)
        state_in = state_in + jnp.where(d < me, term, 0.0)
        late_in = late_in + jnp.where(d < me, term * away, 0.0)
        back_in = back_in + jnp.where(d > me, term, 0.0)
    states, backs = [], []
    carried = state_in
    for q in range(CHUNKS):
        states.append(small_residues * (small_ref[piece(q), :] + carried))
        carried = carried * chunk_decay
    carried = back_in
    for q in reversed(range(CHUNKS)):
        backs.insert(0, small_residues * (small_ref[piece(CHUNKS + q), :] + carried))
        carried = carried * chunk_decay
    down = iota((CHUNK, CHANNELS), 0).astype(F32)
    long_far = dot3(split(jnp.exp(-row * (down + 1.0))), expand(jnp.concatenate(states, axis=1)))
    gated_far = dot3(split(jnp.exp(-row * (CHUNK - 1 - down))), expand(jnp.concatenate(backs, axis=1)))
    sums = [jnp.zeros((8, CHANNELS), F32) for _ in range(3 * KW)]
    for q in range(CHUNKS):
        rows = pl.ds(q * CHUNK, CHUNK)
        signal = out_grad_ref[rows, :].astype(F32)
        grad_gated = gated_ref[rows, :] + chunk_lanes(gated_far, q)
        keyed, valued = kv_ref[0, rows, :], kv_ref[1, rows, :]
        if q == 0:
            keyed = jnp.concatenate([patch_ref[0], keyed[HEAD:, :]], axis=0)
            valued = jnp.concatenate([patch_ref[1], valued[HEAD:, :]], axis=0)
        parts = (
            signal * (long_ref[rows, :] + chunk_lanes(long_far, q)),
            grad_gated * valued,
            grad_gated * keyed,
        )
        for i in range(3):
            feature_ref[i, rows, :] = parts[i]
            for j in range(KW):
                product = parts[i] * ext_ref[i, pl.ds(LEAD - j + q * CHUNK, CHUNK), :]
                sums[i * KW + j] = sums[i * KW + j] + jnp.sum(
                    product.reshape(CHUNK // 8, 8, CHANNELS), axis=0
                )
    residue_part, moment_part, lead_moment, end_moment, lead = (
        small_ref[piece(2 * CHUNKS + at), :] for at in range(5)
    )
    residue_part = residue_part + lead * state_in
    moment_part = moment_part + lead_moment * state_in + lead * late_in + end_moment * back_in
    same = (iota((CHANNELS, CHANNELS), 0) // WIDTH == iota((CHANNELS, CHANNELS), 1) // MODES).astype(F32)
    pick = (iota((MODES, CHANNELS), 1) % MODES == iota((MODES, CHANNELS), 0)).astype(F32)

    def by_mode(part):
        spread = lax.dot_general(part, same, MM, precision=EXACT, preferred_element_type=F32)
        return jnp.sum(spread * pick, axis=0, keepdims=True)

    residue_row = small_ref[LOCAL : LOCAL + 1, :] + by_mode(residue_part)
    moment_row = small_ref[LOCAL + 1 : LOCAL + 2, :] + by_mode(moment_part)
    rate_row = -row * mode_row(residues) * moment_row
    lines = [jnp.sum(part, axis=0, keepdims=True) for part in sums]
    stats = jnp.concatenate(lines + [residue_row, rate_row, jnp.zeros((1, CHANNELS), F32)], axis=0)
    scaled, exponent = scaled_columns(stats)
    last = iota((STATS, CHANNELS), 0) == STATS - 1
    stats_ref[...] = jnp.where(last, exponent, scaled)


def inputs_kernel(feature_ref, after_ref, weight_ref, out_ref, ext_ref):
    for i in range(3):
        ext_ref[0:ROWS, :] = feature_ref[i]
        ext_ref[ROWS:, :] = after_ref[i]
        for q in range(CHUNKS):
            total = None
            for j in range(KW):
                term = weight_ref[i, j : j + 1, :] * ext_ref[pl.ds(j + q * CHUNK, CHUNK), :]
                total = term if total is None else total + term
            out_ref[i, pl.ds(q * CHUNK, CHUNK), :] = total.astype(BF16)


def total_kernel(stats_ref, total_ref, square_ref):
    total = jnp.zeros((STATS, CHANNELS), F32)
    for d in range(stats_ref.shape[0]):
        total = total + stats_ref[d] * jnp.exp2(stats_ref[d, STATS - 1 :, :])
    total = jnp.where(iota((STATS, CHANNELS), 0) == STATS - 1, 0.0, total)
    total_ref[...] = total
    square = jnp.sum(total * total, axis=0, keepdims=True)
    for d in range(square_ref.shape[0]):
        square_ref[d] = jnp.broadcast_to(square, square_ref.shape[1:])


def scale_kernel(square_ref, total_ref, conv_ref, residue_ref, rate_ref):
    squares = jnp.sum(jnp.sum(square_ref[:, 0, :], axis=0, keepdims=True), axis=1, keepdims=True)
    factor = jnp.minimum(1.0, lax.rsqrt(squares / (3 * KW * D + 2 * G * MODES) + 1e-6))
    total = total_ref[...] * factor
    for i in range(3):
        conv_ref[i] = total[i * KW : (i + 1) * KW, :]
    pick = (iota((MODES, CHANNELS), 1) % MODES == iota((MODES, CHANNELS), 0)).astype(F32)
    own = lane_group(GROUPS)
    at = 3 * KW
    residue_ref[...] = lax.dot_general(
        total[at : at + 1, :] * own, pick, NT, precision=EXACT, preferred_element_type=F32
    )
    rate_ref[...] = lax.dot_general(
        total[at + 1 : at + 2, :] * own, pick, NT, precision=EXACT, preferred_element_type=F32
    )


def shape(*dims, dtype=F32):
    return jax.ShapeDtypeStruct(dims, dtype)


VMEM = pl.BlockSpec(memory_space=pltpu.VMEM)
SMEM = pl.BlockSpec(memory_space=pltpu.SMEM)


HBM = pl.BlockSpec(memory_space=pltpu.HBM)


def call(kernel, name, out_shape, specs, cost_us, scratch=()):
    return pl.pallas_call(
        kernel,
        out_shape=out_shape,
        in_specs=specs,
        out_specs=jax.tree.map(lambda _: VMEM, out_shape),
        scratch_shapes=list(scratch),
        compiler_params=pltpu.CompilerParams(vmem_limit_bytes=12 * 2**20),
        cost_estimate=pl.CostEstimate(
            flops=int(cost_us * 1e9), bytes_accessed=int(cost_us * 3e6), transcendentals=0
        ),
        name=name,
    )


def shards(projected, conv_weight, residues, decay_rates, grad_out):
    ctx = lax.axis_size("ctx")
    planes = lax.axis_size("ch")
    me = lax.axis_index("ctx").astype(jnp.int32).reshape(1)
    before = lax.ppermute(
        projected[:, ROWS - LEAD :, :], "ctx", [(source, source + 1) for source in range(ctx - 1)]
    )
    kv, pair, states, ends, head, powers, table = call(
        prepare_kernel, "prepare",
        (shape(2, ROWS, CHANNELS), shape(2, CHUNK, CHUNKS * CHANNELS), shape(2, MODES, CHUNKS * CHANNELS),
         shape(2, MODES, CHANNELS), shape(4, HEAD, CHANNELS), shape(3, HEAD, MODES, CHANNELS),
         shape(2, GROUPS, MODES)),
        [VMEM] * 3 + [HBM] * 2, 3,
        scratch=[pltpu.VMEM((3, ROWS, CHANNELS), BF16), pltpu.VMEM((ROWS, CHANNELS), BF16),
                 pltpu.VMEM((3, LEAD + ROWS, CHANNELS), F32), pltpu.SemaphoreType.DMA((2,))],
    )(conv_weight, decay_rates, residues,
      *(pltpu.with_memory_space_constraint(part, pltpu.HBM) for part in (projected, grad_out)))
    patch, delta, send = call(
        patch_kernel, "patch",
        (shape(4, HEAD, CHANNELS), shape(2, MODES, CHANNELS), shape(2, MODES + 8, CHANNELS)),
        [VMEM] * 5, 1,
        scratch=[pltpu.VMEM((LEAD + HEAD, CHANNELS), F32)],
    )(before, conv_weight, head, powers, ends)
    later = lax.broadcasted_iota(jnp.int32, (ctx, 1, 1), 0) > me.reshape(1, 1, 1)
    send = jnp.where(later, send[1], send[0]).astype(F16)
    arrived = lax.all_to_all(send, "ctx", 0, 0).astype(F32)
    near = call(
        middle_kernel, "within",
        shape(2 * ROWS + LOCAL + 8, CHANNELS),
        [VMEM] * 5, 8,
        scratch=[pltpu.VMEM((GROUPS, CHANNELS), F32)],
    )(table, pair, states, patch, delta)
    grad_feature, stats = call(
        finish_kernel, "across",
        (shape(3, ROWS, CHANNELS), shape(STATS, CHANNELS)),
        [SMEM] + [VMEM] * 8, 4,
        scratch=[pltpu.VMEM((3, LEAD + ROWS, CHANNELS), F32)],
    )(me, arrived, table, near, kv, patch, grad_out, projected, before)
    after = lax.ppermute(
        grad_feature[:, :8, :], "ctx", [(source + 1, source) for source in range(ctx - 1)]
    )
    stats = jnp.broadcast_to(stats.astype(F16), (ctx, STATS, CHANNELS))
    gathered = lax.all_to_all(stats, "ctx", 0, 0).astype(F32)
    grad_projected = call(
        inputs_kernel, "inputs", shape(3, ROWS, CHANNELS, dtype=BF16), [VMEM] * 3, 2,
        scratch=[pltpu.VMEM((ROWS + 8, CHANNELS), F32)],
    )(grad_feature, after, conv_weight)
    total, square = call(
        total_kernel, "total", (shape(STATS, CHANNELS), shape(planes, 1, CHANNELS)), [VMEM], 1,
    )(gathered)
    squares = lax.all_to_all(square, "ch", 0, 0)
    grad_conv, grad_residues, grad_log_rates = call(
        scale_kernel, "scale",
        (shape(3, KW, CHANNELS), shape(GROUPS, MODES), shape(GROUPS, MODES)), [VMEM] * 2, 1,
    )(squares, total)
    return grad_projected, grad_conv, grad_residues, grad_log_rates


def solution(mesh):
    in_specs = (
        P(None, "ctx", "ch"),
        P(None, None, "ch"),
        P("ch", None),
        P("ch", None),
        P("ctx", "ch"),
    )
    out_specs = (P(None, "ctx", "ch"), P(None, None, "ch"), P("ch", None), P("ch", None))
    return jax.shard_map(shards, mesh=mesh, in_specs=in_specs, out_specs=out_specs, check_vma=False)
```

```python
import jax
import jax.numpy as jnp
from jax import lax
from jax.experimental import pallas as pl
from jax.experimental.pallas import tpu as pltpu
from jax.sharding import PartitionSpec as P

D = 4096
G = 256
MODES = 16
KW = 7

ROWS = 512
CHANNELS = 128
GROUPS = 8
WIDTH = 16
CHUNK = 128
CHUNKS = ROWS // CHUNK
LEAD = 16
HEAD = 8
STATS = 24
LOCAL = (2 * CHUNKS + 5) * MODES

F32 = jnp.float32
BF16 = jnp.bfloat16
F16 = jnp.float16
EXACT = lax.Precision.HIGHEST
MM = (((1,), (0,)), ((), ()))
NT = (((1,), (1,)), ((), ()))


def split(value):
    high = value.astype(BF16)
    low = (value - high.astype(F32)).astype(BF16)
    return high, low


def dot3(left, right, dims=MM):
    lh, ll = left
    rh, rl = right

    def product(a, b):
        return lax.dot_general(a, b, dims, preferred_element_type=F32)

    return product(lh, rh) + (product(lh, rl) + product(ll, rh))


def iota(shape, axis):
    return lax.broadcasted_iota(jnp.int32, shape, axis)


def lane_group(rows):
    return (iota((rows, CHANNELS), 1) // WIDTH == iota((rows, CHANNELS), 0)).astype(F32)


def mode_row(table):
    pick = (iota((MODES, CHANNELS), 1) % MODES == iota((MODES, CHANNELS), 0)).astype(F32)
    spread = lax.dot_general(table, pick, MM, precision=EXACT, preferred_element_type=F32)
    return jnp.sum(spread * lane_group(GROUPS), axis=0, keepdims=True)


def mode_column(row):
    eye = iota((CHANNELS, CHANNELS), 0) == iota((CHANNELS, CHANNELS), 1)
    return jnp.sum(jnp.where(eye, row, 0.0), axis=1, keepdims=True)


def mode_compact(table):
    return lax.dot_general(
        table, lane_group(GROUPS), (((0,), (0,)), ((), ())), precision=EXACT, preferred_element_type=F32
    )


def compact(full):
    lanes = full.shape[1]
    total = None
    for g in range(GROUPS):
        own = (iota((MODES, lanes), 1) % CHANNELS) // WIDTH == g
        part = jnp.where(own, full[g * MODES : (g + 1) * MODES, :], 0.0)
        total = part if total is None else total + part
    return total


def expand(small):
    lanes = small.shape[1]
    own = (iota((CHANNELS, lanes), 0) // MODES == (iota((CHANNELS, lanes), 1) % CHANNELS) // WIDTH).astype(F32)
    return split(jnp.concatenate([small] * GROUPS, axis=0) * own)


def near_parts(near_ref):
    return near_ref.at[0:ROWS, :], near_ref.at[ROWS : 2 * ROWS, :], near_ref.at[2 * ROWS :, :]


def member(position, count):
    return (position + count // 2) % count


def piece(at):
    return slice(at * MODES, (at + 1) * MODES)


def chunk_lanes(value, q):
    return value[:, q * CHANNELS : (q + 1) * CHANNELS]


def prepare_kernel(weight_ref, rate_ref, residue_ref, proj_ref, out_grad_ref,
                   kv_ref, pair_ref, states_ref, ends_ref, head_ref, power_ref, table_ref,
                   raw_ref, signal_ref, ext_ref, sem_ref):
    gi_ref, gl_ref = pair_ref.at[0], pair_ref.at[1]
    copies = [
        pltpu.make_async_copy(proj_ref, raw_ref, sem_ref.at[0]),
        pltpu.make_async_copy(out_grad_ref, signal_ref, sem_ref.at[1]),
    ]
    for copy in copies:
        copy.start()
    rates = rate_ref[...]
    table_ref[0] = rates
    table_ref[1] = residue_ref[...]
    column = mode_column(mode_row(rates))
    lag = iota((CHANNELS, CHUNK), 1).astype(F32)
    ascending = split(jnp.exp(-column * lag))
    descending = split(jnp.exp(-column * (CHUNK - 1 - lag)))
    small_rates = mode_compact(rates)
    one_step = jnp.exp(-small_rates)
    chunk_decay = jnp.exp(-small_rates * CHUNK)
    for r in range(HEAD):
        power_ref[0, r] = jnp.exp(-small_rates * float(CHUNK - 1 - r))
        power_ref[1, r] = jnp.exp(-small_rates * float(r + 1))
    power_ref[2, 0] = jnp.exp(-small_rates * float(ROWS - CHUNK))
    for r in range(1, HEAD):
        power_ref[2, r] = jnp.zeros((MODES, CHANNELS), F32)
    for copy in copies:
        copy.wait()
    for i in range(3):
        ext_ref[i, 0:LEAD, :] = jnp.zeros((LEAD, CHANNELS), F32)
        ext_ref[i, LEAD:, :] = raw_ref[i].astype(F32)
    blank = jnp.zeros((HEAD, CHANNELS), F32)
    for q in range(CHUNKS):
        feature = []
        for i in range(3):
            total = None
            for j in range(KW):
                term = weight_ref[i, j : j + 1, :] * ext_ref[i, pl.ds(LEAD - j + q * CHUNK, CHUNK), :]
                total = term if total is None else total + term
            feature.append(total)
        rows = pl.ds(q * CHUNK, CHUNK)
        lanes = slice(q * CHANNELS, (q + 1) * CHANNELS)
        signal = signal_ref[rows, :].astype(F32)
        kv_ref[0, rows, :] = feature[1]
        kv_ref[1, rows, :] = feature[2]
        gi_ref[:, lanes] = feature[1] * feature[2]
        gl_ref[:, lanes] = signal * feature[0]
        if q == 0:
            for i in range(3):
                head_ref[i] = feature[i][0:HEAD, :]
            head_ref[3] = signal[0:HEAD, :]
            gi_ref[0:HEAD, lanes] = blank
            gl_ref[0:HEAD, lanes] = blank
    ends = compact(dot3(descending, split(gi_ref[...])))
    leads = compact(dot3(ascending, split(gl_ref[...])))
    state = jnp.zeros((MODES, CHANNELS), F32)
    for q in range(CHUNKS):
        part = chunk_lanes(ends, q)
        states_ref[0, :, q * CHANNELS : (q + 1) * CHANNELS] = part
        state = chunk_decay * state + part
    back = jnp.zeros((MODES, CHANNELS), F32)
    for q in reversed(range(CHUNKS)):
        part = one_step * chunk_lanes(leads, q)
        states_ref[1, :, q * CHANNELS : (q + 1) * CHANNELS] = part
        back = chunk_decay * back + part
    ends_ref[0] = state
    ends_ref[1] = back


def scaled_columns(value):
    largest = jnp.max(jnp.abs(value), axis=0, keepdims=True)
    exponent = jnp.ceil(jnp.log2(jnp.maximum(largest, 1e-30))) - 15.0
    return value * jnp.exp2(-exponent), exponent


def patch_kernel(before_ref, weight_ref, head_ref, power_ref, ends_ref,
                 patch_ref, delta_ref, send_ref, ext_ref):
    feature = []
    for i in range(3):
        ext_ref[0:LEAD, :] = before_ref[i].astype(F32)
        ext_ref[LEAD:, :] = jnp.zeros((HEAD, CHANNELS), F32)
        total = head_ref[i]
        for j in range(1, KW):
            total = total + weight_ref[i, j : j + 1, :] * ext_ref[pl.ds(LEAD - j, HEAD), :]
        feature.append(total)
    gi = feature[1] * feature[2]
    gl = head_ref[3] * feature[0]
    for at, value in enumerate((feature[1], feature[2], gi, gl)):
        patch_ref[at] = value
    state_part, back_part = None, None
    for r in range(HEAD):
        ahead = power_ref[0, r] * gi[r : r + 1, :]
        behind = power_ref[1, r] * gl[r : r + 1, :]
        state_part = ahead if r == 0 else state_part + ahead
        back_part = behind if r == 0 else back_part + behind
    delta_ref[0] = state_part
    delta_ref[1] = back_part
    state = ends_ref[0] + power_ref[2, 0] * state_part
    back = ends_ref[1] + back_part
    for at, value in enumerate((back, state)):
        scaled, exponent = scaled_columns(value)
        send_ref[at, 0:MODES, :] = scaled
        send_ref[at, MODES:, :] = jnp.broadcast_to(exponent, (8, CHANNELS))


def spliced(wide_ref, patch):
    top = jnp.concatenate([patch, wide_ref[0:HEAD, CHANNELS:]], axis=1)
    return jnp.concatenate([top, wide_ref[HEAD:, :]], axis=0)


def middle_kernel(table_ref, pair_ref, states_ref, patch_ref, delta_ref,
                  near_ref, lag_ref):
    long_ref, gated_ref, small_ref = near_parts(near_ref)
    gi_ref, gl_ref = pair_ref.at[0], pair_ref.at[1]
    rates = table_ref[0]
    row = mode_row(rates)
    column = mode_column(row)
    lag = iota((CHANNELS, CHUNK), 1)
    back_lag = lax.rem(CHUNK - lag, CHUNK)
    ascending = jnp.exp(-column * lag.astype(F32))
    descending = jnp.exp(-column * (CHUNK - 1 - lag).astype(F32))
    turned = jnp.exp(-column * back_lag.astype(F32))
    residue_row = mode_row(table_ref[1]) * lane_group(GROUPS)
    filters = lax.dot_general(residue_row, ascending, MM, precision=EXACT, preferred_element_type=F32)
    turned_filters = lax.dot_general(residue_row, turned, MM, precision=EXACT, preferred_element_type=F32)
    gi = split(spliced(gi_ref, patch_ref[2]))
    gl = split(spliced(gl_ref, patch_ref[3]))
    down = iota((CHUNK, CHUNK), 0)
    across = iota((CHUNK, CHUNK), 1)
    mirror = (down + across == CHUNK - 1).astype(F32).astype(BF16)
    mirrored = [
        lax.dot_general(mirror, part, MM, preferred_element_type=F32).astype(BF16) for part in gl
    ]
    wide_group = (iota((1, ROWS), 1) % CHANNELS) // WIDTH
    lane_of = iota((CHUNK, CHANNELS), 1) // WIDTH
    for g in range(GROUPS):
        straight = jnp.broadcast_to(turned_filters[g : g + 1, :], (CHUNK, CHUNK))
        straight = pltpu.roll(straight, 0, 1, stride=1, stride_axis=0)
        straight = split(jnp.where(across <= down, straight, 0.0))
        flipped = jnp.broadcast_to(filters[g : g + 1, :], (CHUNK, CHUNK))
        flipped = pltpu.roll(flipped, 0, 1, stride=1, stride_axis=0)
        flipped = split(jnp.where(across >= down, flipped, 0.0))
        forward = dot3(straight, gi)
        backward = dot3(flipped, gl)
        for q in range(CHUNKS):
            rows = pl.ds(q * CHUNK, CHUNK)
            if g == 0:
                long_ref[rows, :] = chunk_lanes(forward, q)
                gated_ref[rows, :] = chunk_lanes(backward, q)
            else:
                long_ref[rows, :] = jnp.where(lane_of == g, chunk_lanes(forward, q), long_ref[rows, :])
                gated_ref[rows, :] = jnp.where(lane_of == g, chunk_lanes(backward, q), gated_ref[rows, :])
        own = (wide_group == g).astype(F32).astype(BF16)
        products = dot3((mirrored[0] * own, mirrored[1] * own), gi, NT)
        products = jnp.where(across + down <= CHUNK - 1, products, 0.0)
        sheared = pltpu.roll(products, 1, 1, stride=1, stride_axis=0)
        lag_ref[g : g + 1, :] = jnp.sum(sheared, axis=0, keepdims=True)
    lag_grad = lag_ref[...]
    down_lag = lax.rem(CHUNK - down, CHUNK).astype(F32)
    powers = jnp.exp(-row * down_lag)
    residue_sums = lax.dot_general(lag_grad, powers, MM, precision=EXACT, preferred_element_type=F32)
    moment_sums = lax.dot_general(lag_grad, powers * down_lag, MM, precision=EXACT, preferred_element_type=F32)
    own_group = lane_group(GROUPS)
    small_ref[LOCAL : LOCAL + 1, :] = jnp.sum(residue_sums * own_group, axis=0, keepdims=True)
    small_ref[LOCAL + 1 : LOCAL + 2, :] = jnp.sum(moment_sums * own_group, axis=0, keepdims=True)
    small_rates = mode_compact(rates)
    chunk_decay = jnp.exp(-small_rates * CHUNK)
    lag_value = lag.astype(F32)
    end_moments = compact(dot3(split(descending * (CHUNK - 1 - lag_value)), gi))
    lead_moments = compact(dot3(split(ascending * (jnp.exp(-column) * (lag_value + 1.0))), gl))
    zero = jnp.zeros((MODES, CHANNELS), F32)
    leads = []
    state, moment = zero, zero
    residue_part, moment_part, lead_moment = zero, zero, zero
    offset_decay = jnp.ones((MODES, CHANNELS), F32)
    for q in range(CHUNKS):
        lead = chunk_lanes(states_ref[1], q)
        end = chunk_lanes(states_ref[0], q)
        if q == 0:
            end, lead = end + delta_ref[0], lead + delta_ref[1]
        leads.append(lead)
        lead_here = chunk_lanes(lead_moments, q)
        small_ref[piece(q), :] = state
        residue_part = residue_part + lead * state
        moment_part = moment_part + lead_here * state + lead * moment
        lead_moment = lead_moment + offset_decay * (lead_here + float(q * CHUNK) * lead)
        offset_decay = offset_decay * chunk_decay
        moment = chunk_decay * (moment + float(CHUNK) * state) + chunk_lanes(end_moments, q)
        state = chunk_decay * state + end
    back = zero
    for q in reversed(range(CHUNKS)):
        small_ref[piece(CHUNKS + q), :] = back
        back = chunk_decay * back + leads[q]
    for at, value in enumerate((residue_part, moment_part, lead_moment, moment, back)):
        small_ref[piece(2 * CHUNKS + at), :] = value


def finish_kernel(me_ref, arrived_ref, table_ref, near_ref,
                  kv_ref, patch_ref, out_grad_ref, proj_ref, before_ref, feature_ref, stats_ref, ext_ref):
    for i in range(3):
        ext_ref[i, 0:LEAD, :] = before_ref[i].astype(F32)
        ext_ref[i, LEAD:, :] = proj_ref[i].astype(F32)
    long_ref, gated_ref, small_ref = near_parts(near_ref)
    me = me_ref[0]
    rates, residues = table_ref[0], table_ref[1]
    row = mode_row(rates)
    small_rates = mode_compact(rates)
    small_residues = mode_compact(residues)
    chunk_decay = jnp.exp(-small_rates * CHUNK)
    zero = jnp.zeros((MODES, CHANNELS), F32)
    state_in, late_in, back_in = zero, zero, zero
    for at in range(arrived_ref.shape[0]):
        d = member(at, arrived_ref.shape[0])
        away = (jnp.abs(me - d) - 1).astype(F32) * float(ROWS)
        scale = jnp.exp2(arrived_ref[at, MODES : MODES + 1, :])
        term = jnp.exp(-small_rates * away) * (arrived_ref[at, 0:MODES, :] * scale)
        state_in = state_in + jnp.where(d < me, term, 0.0)
        late_in = late_in + jnp.where(d < me, term * away, 0.0)
        back_in = back_in + jnp.where(d > me, term, 0.0)
    states, backs = [], []
    carried = state_in
    for q in range(CHUNKS):
        states.append(small_residues * (small_ref[piece(q), :] + carried))
        carried = carried * chunk_decay
    carried = back_in
    for q in reversed(range(CHUNKS)):
        backs.insert(0, small_residues * (small_ref[piece(CHUNKS + q), :] + carried))
        carried = carried * chunk_decay
    down = iota((CHUNK, CHANNELS), 0).astype(F32)
    long_far = dot3(split(jnp.exp(-row * (down + 1.0))), expand(jnp.concatenate(states, axis=1)))
    gated_far = dot3(split(jnp.exp(-row * (CHUNK - 1 - down))), expand(jnp.concatenate(backs, axis=1)))
    sums = [jnp.zeros((8, CHANNELS), F32) for _ in range(3 * KW)]
    for q in range(CHUNKS):
        rows = pl.ds(q * CHUNK, CHUNK)
        signal = out_grad_ref[rows, :].astype(F32)
        grad_gated = gated_ref[rows, :] + chunk_lanes(gated_far, q)
        keyed, valued = kv_ref[0, rows, :], kv_ref[1, rows, :]
        if q == 0:
            keyed = jnp.concatenate([patch_ref[0], keyed[HEAD:, :]], axis=0)
            valued = jnp.concatenate([patch_ref[1], valued[HEAD:, :]], axis=0)
        parts = (
            signal * (long_ref[rows, :] + chunk_lanes(long_far, q)),
            grad_gated * valued,
            grad_gated * keyed,
        )
        for i in range(3):
            feature_ref[i, rows, :] = parts[i]
            for j in range(KW):
                product = parts[i] * ext_ref[i, pl.ds(LEAD - j + q * CHUNK, CHUNK), :]
                sums[i * KW + j] = sums[i * KW + j] + jnp.sum(
                    product.reshape(CHUNK // 8, 8, CHANNELS), axis=0
                )
    residue_part, moment_part, lead_moment, end_moment, lead = (
        small_ref[piece(2 * CHUNKS + at), :] for at in range(5)
    )
    residue_part = residue_part + lead * state_in
    moment_part = moment_part + lead_moment * state_in + lead * late_in + end_moment * back_in
    same = (iota((CHANNELS, CHANNELS), 0) // WIDTH == iota((CHANNELS, CHANNELS), 1) // MODES).astype(F32)
    pick = (iota((MODES, CHANNELS), 1) % MODES == iota((MODES, CHANNELS), 0)).astype(F32)

    def by_mode(part):
        spread = lax.dot_general(part, same, MM, precision=EXACT, preferred_element_type=F32)
        return jnp.sum(spread * pick, axis=0, keepdims=True)

    residue_row = small_ref[LOCAL : LOCAL + 1, :] + by_mode(residue_part)
    moment_row = small_ref[LOCAL + 1 : LOCAL + 2, :] + by_mode(moment_part)
    rate_row = -row * mode_row(residues) * moment_row
    lines = [jnp.sum(part, axis=0, keepdims=True) for part in sums]
    stats = jnp.concatenate(lines + [residue_row, rate_row, jnp.zeros((1, CHANNELS), F32)], axis=0)
    scaled, exponent = scaled_columns(stats)
    last = iota((STATS, CHANNELS), 0) == STATS - 1
    stats_ref[...] = jnp.where(last, exponent, scaled)


def inputs_kernel(feature_ref, after_ref, weight_ref, out_ref, ext_ref):
    for i in range(3):
        ext_ref[0:ROWS, :] = feature_ref[i]
        ext_ref[ROWS:, :] = after_ref[i]
        for q in range(CHUNKS):
            total = None
            for j in range(KW):
                term = weight_ref[i, j : j + 1, :] * ext_ref[pl.ds(j + q * CHUNK, CHUNK), :]
                total = term if total is None else total + term
            out_ref[i, pl.ds(q * CHUNK, CHUNK), :] = total.astype(BF16)


def total_kernel(stats_ref, total_ref, square_ref):
    total = jnp.zeros((STATS, CHANNELS), F32)
    for d in range(stats_ref.shape[0]):
        total = total + stats_ref[d] * jnp.exp2(stats_ref[d, STATS - 1 :, :])
    total = jnp.where(iota((STATS, CHANNELS), 0) == STATS - 1, 0.0, total)
    total_ref[...] = total
    square = jnp.sum(total * total, axis=0, keepdims=True)
    for d in range(square_ref.shape[0]):
        square_ref[d] = jnp.broadcast_to(square, square_ref.shape[1:])


def scale_kernel(square_ref, total_ref, conv_ref, residue_ref, rate_ref):
    squares = jnp.sum(jnp.sum(square_ref[:, 0, :], axis=0, keepdims=True), axis=1, keepdims=True)
    factor = jnp.minimum(1.0, lax.rsqrt(squares / (3 * KW * D + 2 * G * MODES) + 1e-6))
    total = total_ref[...] * factor
    for i in range(3):
        conv_ref[i] = total[i * KW : (i + 1) * KW, :]
    pick = (iota((MODES, CHANNELS), 1) % MODES == iota((MODES, CHANNELS), 0)).astype(F32)
    own = lane_group(GROUPS)
    at = 3 * KW
    residue_ref[...] = lax.dot_general(
        total[at : at + 1, :] * own, pick, NT, precision=EXACT, preferred_element_type=F32
    )
    rate_ref[...] = lax.dot_general(
        total[at + 1 : at + 2, :] * own, pick, NT, precision=EXACT, preferred_element_type=F32
    )


def shape(*dims, dtype=F32):
    return jax.ShapeDtypeStruct(dims, dtype)


VMEM = pl.BlockSpec(memory_space=pltpu.VMEM)
SMEM = pl.BlockSpec(memory_space=pltpu.SMEM)


HBM = pl.BlockSpec(memory_space=pltpu.HBM)


def call(kernel, name, out_shape, specs, cost_us, scratch=()):
    return pl.pallas_call(
        kernel,
        out_shape=out_shape,
        in_specs=specs,
        out_specs=jax.tree.map(lambda _: VMEM, out_shape),
        scratch_shapes=list(scratch),
        compiler_params=pltpu.CompilerParams(vmem_limit_bytes=12 * 2**20),
        cost_estimate=pl.CostEstimate(
            flops=int(cost_us * 1e9), bytes_accessed=int(cost_us * 3e6), transcendentals=0
        ),
        name=name,
    )


def exchange(blocks):
    count = blocks.shape[0]
    return lax.all_to_all(blocks, "ctx", 0, 0, axis_index_groups=[[member(p, count) for p in range(count)]])


def shards(projected, conv_weight, residues, decay_rates, grad_out):
    ctx = lax.axis_size("ctx")
    planes = lax.axis_size("ch")
    me = lax.axis_index("ctx").astype(jnp.int32).reshape(1)
    before = lax.ppermute(
        projected[:, ROWS - LEAD :, :], "ctx", [(source, source + 1) for source in range(ctx - 1)]
    )
    kv, pair, states, ends, head, powers, table = call(
        prepare_kernel, "prepare",
        (shape(2, ROWS, CHANNELS), shape(2, CHUNK, CHUNKS * CHANNELS), shape(2, MODES, CHUNKS * CHANNELS),
         shape(2, MODES, CHANNELS), shape(4, HEAD, CHANNELS), shape(3, HEAD, MODES, CHANNELS),
         shape(2, GROUPS, MODES)),
        [VMEM] * 3 + [HBM] * 2, 3,
        scratch=[pltpu.VMEM((3, ROWS, CHANNELS), BF16), pltpu.VMEM((ROWS, CHANNELS), BF16),
                 pltpu.VMEM((3, LEAD + ROWS, CHANNELS), F32), pltpu.SemaphoreType.DMA((2,))],
    )(conv_weight, decay_rates, residues,
      *(pltpu.with_memory_space_constraint(part, pltpu.HBM) for part in (projected, grad_out)))
    patch, delta, send = call(
        patch_kernel, "patch",
        (shape(4, HEAD, CHANNELS), shape(2, MODES, CHANNELS), shape(2, MODES + 8, CHANNELS)),
        [VMEM] * 5, 1,
        scratch=[pltpu.VMEM((LEAD + HEAD, CHANNELS), F32)],
    )(before, conv_weight, head, powers, ends)
    later = member(lax.broadcasted_iota(jnp.int32, (ctx, 1, 1), 0), ctx) > me.reshape(1, 1, 1)
    send = jnp.where(later, send[1], send[0]).astype(F16)
    arrived = exchange(send).astype(F32)
    near = call(
        middle_kernel, "within",
        shape(2 * ROWS + LOCAL + 8, CHANNELS),
        [VMEM] * 5, 8,
        scratch=[pltpu.VMEM((GROUPS, CHANNELS), F32)],
    )(table, pair, states, patch, delta)
    grad_feature, stats = call(
        finish_kernel, "across",
        (shape(3, ROWS, CHANNELS), shape(STATS, CHANNELS)),
        [SMEM] + [VMEM] * 8, 4,
        scratch=[pltpu.VMEM((3, LEAD + ROWS, CHANNELS), F32)],
    )(me, arrived, table, near, kv, patch, grad_out, projected, before)
    after = lax.ppermute(
        grad_feature[:, :8, :], "ctx", [(source + 1, source) for source in range(ctx - 1)]
    )
    stats = jnp.broadcast_to(stats.astype(F16), (ctx, STATS, CHANNELS))
    gathered = exchange(stats).astype(F32)
    grad_projected = call(
        inputs_kernel, "inputs", shape(3, ROWS, CHANNELS, dtype=BF16), [VMEM] * 3, 2,
        scratch=[pltpu.VMEM((ROWS + 8, CHANNELS), F32)],
    )(grad_feature, after, conv_weight)
    total, square = call(
        total_kernel, "total", (shape(STATS, CHANNELS), shape(planes, 1, CHANNELS)), [VMEM], 1,
    )(gathered)
    squares = lax.all_to_all(square, "ch", 0, 0)
    grad_conv, grad_residues, grad_log_rates = call(
        scale_kernel, "scale",
        (shape(3, KW, CHANNELS), shape(GROUPS, MODES), shape(GROUPS, MODES)), [VMEM] * 2, 1,
    )(squares, total)
    return grad_projected, grad_conv, grad_residues, grad_log_rates


def solution(mesh):
    in_specs = (
        P(None, "ctx", "ch"),
        P(None, None, "ch"),
        P("ch", None),
        P("ch", None),
        P("ctx", "ch"),
    )
    out_specs = (P(None, "ctx", "ch"), P(None, None, "ch"), P("ch", None), P("ch", None))
    return jax.shard_map(shards, mesh=mesh, in_specs=in_specs, out_specs=out_specs, check_vma=False)
```

```python
import jax
import jax.numpy as jnp
from jax import lax
from jax.experimental import pallas as pl
from jax.experimental.pallas import tpu as pltpu
from jax.sharding import PartitionSpec as P

D = 4096
G = 256
MODES = 16
KW = 7

ROWS = 512
CHANNELS = 128
GROUPS = 8
WIDTH = 16
CHUNK = 128
CHUNKS = ROWS // CHUNK
LEAD = 16
HEAD = 8
STATS = 24
LOCAL = (2 * CHUNKS + 5) * MODES

F32 = jnp.float32
BF16 = jnp.bfloat16
F16 = jnp.float16
EXACT = lax.Precision.HIGHEST
MM = (((1,), (0,)), ((), ()))
NT = (((1,), (1,)), ((), ()))


def split(value):
    high = value.astype(BF16)
    low = (value - high.astype(F32)).astype(BF16)
    return high, low


def dot3(left, right, dims=MM):
    lh, ll = left
    rh, rl = right

    def product(a, b):
        return lax.dot_general(a, b, dims, preferred_element_type=F32)

    return product(lh, rh) + (product(lh, rl) + product(ll, rh))


def iota(shape, axis):
    return lax.broadcasted_iota(jnp.int32, shape, axis)


def lane_group(rows):
    return (iota((rows, CHANNELS), 1) // WIDTH == iota((rows, CHANNELS), 0)).astype(F32)


def mode_row(table):
    pick = (iota((MODES, CHANNELS), 1) % MODES == iota((MODES, CHANNELS), 0)).astype(F32)
    spread = lax.dot_general(table, pick, MM, precision=EXACT, preferred_element_type=F32)
    return jnp.sum(spread * lane_group(GROUPS), axis=0, keepdims=True)


def mode_column(row):
    eye = iota((CHANNELS, CHANNELS), 0) == iota((CHANNELS, CHANNELS), 1)
    return jnp.sum(jnp.where(eye, row, 0.0), axis=1, keepdims=True)


def mode_compact(table):
    return lax.dot_general(
        table, lane_group(GROUPS), (((0,), (0,)), ((), ())), precision=EXACT, preferred_element_type=F32
    )


def compact(full):
    lanes = full.shape[1]
    total = None
    for g in range(GROUPS):
        own = (iota((MODES, lanes), 1) % CHANNELS) // WIDTH == g
        part = jnp.where(own, full[g * MODES : (g + 1) * MODES, :], 0.0)
        total = part if total is None else total + part
    return total


def expand(small):
    lanes = small.shape[1]
    own = (iota((CHANNELS, lanes), 0) // MODES == (iota((CHANNELS, lanes), 1) % CHANNELS) // WIDTH).astype(F32)
    return split(jnp.concatenate([small] * GROUPS, axis=0) * own)


def near_parts(near_ref):
    return near_ref.at[0:ROWS, :], near_ref.at[ROWS : 2 * ROWS, :], near_ref.at[2 * ROWS :, :]


def member(position, count):
    return (position + count // 2) % count


def piece(at):
    return slice(at * MODES, (at + 1) * MODES)


def chunk_lanes(value, q):
    return value[:, q * CHANNELS : (q + 1) * CHANNELS]


def prepare_kernel(weight_ref, rate_ref, residue_ref, proj_ref, out_grad_ref,
                   kv_ref, pair_ref, states_ref, ends_ref, head_ref, power_ref, table_ref,
                   raw_ref, signal_ref, ext_ref, sem_ref):
    gi_ref, gl_ref = pair_ref.at[0], pair_ref.at[1]
    copies = [
        pltpu.make_async_copy(proj_ref, raw_ref, sem_ref.at[0]),
        pltpu.make_async_copy(out_grad_ref, signal_ref, sem_ref.at[1]),
    ]
    for copy in copies:
        copy.start()
    rates = rate_ref[...]
    table_ref[0] = rates
    table_ref[1] = residue_ref[...]
    column = mode_column(mode_row(rates))
    lag = iota((CHANNELS, CHUNK), 1).astype(F32)
    ascending = split(jnp.exp(-column * lag))
    descending = split(jnp.exp(-column * (CHUNK - 1 - lag)))
    small_rates = mode_compact(rates)
    one_step = jnp.exp(-small_rates)
    chunk_decay = jnp.exp(-small_rates * CHUNK)
    for r in range(HEAD):
        power_ref[0, r] = jnp.exp(-small_rates * float(CHUNK - 1 - r))
        power_ref[1, r] = jnp.exp(-small_rates * float(r + 1))
    power_ref[2, 0] = jnp.exp(-small_rates * float(ROWS - CHUNK))
    for r in range(1, HEAD):
        power_ref[2, r] = jnp.zeros((MODES, CHANNELS), F32)
    for copy in copies:
        copy.wait()
    for i in range(3):
        ext_ref[i, 0:LEAD, :] = jnp.zeros((LEAD, CHANNELS), F32)
        ext_ref[i, LEAD:, :] = raw_ref[i].astype(F32)
    blank = jnp.zeros((HEAD, CHANNELS), F32)
    for q in range(CHUNKS):
        feature = []
        for i in range(3):
            total = None
            for j in range(KW):
                term = weight_ref[i, j : j + 1, :] * ext_ref[i, pl.ds(LEAD - j + q * CHUNK, CHUNK), :]
                total = term if total is None else total + term
            feature.append(total)
        rows = pl.ds(q * CHUNK, CHUNK)
        lanes = slice(q * CHANNELS, (q + 1) * CHANNELS)
        signal = signal_ref[rows, :].astype(F32)
        kv_ref[0, rows, :] = feature[1]
        kv_ref[1, rows, :] = feature[2]
        gi_ref[:, lanes] = feature[1] * feature[2]
        gl_ref[:, lanes] = signal * feature[0]
        if q == 0:
            for i in range(3):
                head_ref[i] = feature[i][0:HEAD, :]
            head_ref[3] = signal[0:HEAD, :]
            gi_ref[0:HEAD, lanes] = blank
            gl_ref[0:HEAD, lanes] = blank
    ends = compact(dot3(descending, split(gi_ref[...])))
    leads = compact(dot3(ascending, split(gl_ref[...])))
    state = jnp.zeros((MODES, CHANNELS), F32)
    for q in range(CHUNKS):
        part = chunk_lanes(ends, q)
        states_ref[0, :, q * CHANNELS : (q + 1) * CHANNELS] = part
        state = chunk_decay * state + part
    back = jnp.zeros((MODES, CHANNELS), F32)
    for q in reversed(range(CHUNKS)):
        part = one_step * chunk_lanes(leads, q)
        states_ref[1, :, q * CHANNELS : (q + 1) * CHANNELS] = part
        back = chunk_decay * back + part
    ends_ref[0] = state
    ends_ref[1] = back


def scaled_columns(value):
    largest = jnp.max(jnp.abs(value), axis=0, keepdims=True)
    exponent = jnp.ceil(jnp.log2(jnp.maximum(largest, 1e-30))) - 15.0
    return value * jnp.exp2(-exponent), exponent


def patch_kernel(before_ref, weight_ref, head_ref, power_ref, ends_ref,
                 patch_ref, delta_ref, send_ref, ext_ref):
    feature = []
    for i in range(3):
        ext_ref[0:LEAD, :] = before_ref[i].astype(F32)
        ext_ref[LEAD:, :] = jnp.zeros((HEAD, CHANNELS), F32)
        total = head_ref[i]
        for j in range(1, KW):
            total = total + weight_ref[i, j : j + 1, :] * ext_ref[pl.ds(LEAD - j, HEAD), :]
        feature.append(total)
    gi = feature[1] * feature[2]
    gl = head_ref[3] * feature[0]
    for at, value in enumerate((feature[1], feature[2], gi, gl)):
        patch_ref[at] = value
    state_part, back_part = None, None
    for r in range(HEAD):
        ahead = power_ref[0, r] * gi[r : r + 1, :]
        behind = power_ref[1, r] * gl[r : r + 1, :]
        state_part = ahead if r == 0 else state_part + ahead
        back_part = behind if r == 0 else back_part + behind
    delta_ref[0] = state_part
    delta_ref[1] = back_part
    state = ends_ref[0] + power_ref[2, 0] * state_part
    back = ends_ref[1] + back_part
    for at, value in enumerate((back, state)):
        scaled, exponent = scaled_columns(value)
        send_ref[at, 0:MODES, :] = scaled
        send_ref[at, MODES:, :] = jnp.broadcast_to(exponent, (8, CHANNELS))


def spliced(wide_ref, patch):
    top = jnp.concatenate([patch, wide_ref[0:HEAD, CHANNELS:]], axis=1)
    return jnp.concatenate([top, wide_ref[HEAD:, :]], axis=0)


def middle_kernel(table_ref, pair_ref, states_ref, patch_ref, delta_ref,
                  near_ref, lag_ref):
    long_ref, gated_ref, small_ref = near_parts(near_ref)
    gi_ref, gl_ref = pair_ref.at[0], pair_ref.at[1]
    rates = table_ref[0]
    row = mode_row(rates)
    column = mode_column(row)
    lag = iota((CHANNELS, CHUNK), 1)
    back_lag = lax.rem(CHUNK - lag, CHUNK)
    ascending = jnp.exp(-column * lag.astype(F32))
    descending = jnp.exp(-column * (CHUNK - 1 - lag).astype(F32))
    turned = jnp.exp(-column * back_lag.astype(F32))
    residue_row = mode_row(table_ref[1]) * lane_group(GROUPS)
    filters = lax.dot_general(residue_row, ascending, MM, precision=EXACT, preferred_element_type=F32)
    turned_filters = lax.dot_general(residue_row, turned, MM, precision=EXACT, preferred_element_type=F32)
    gi = split(spliced(gi_ref, patch_ref[2]))
    gl = split(spliced(gl_ref, patch_ref[3]))
    down = iota((CHUNK, CHUNK), 0)
    across = iota((CHUNK, CHUNK), 1)
    mirror = (down + across == CHUNK - 1).astype(F32).astype(BF16)
    mirrored = [
        lax.dot_general(mirror, part, MM, preferred_element_type=F32).astype(BF16) for part in gl
    ]
    wide_group = (iota((1, ROWS), 1) % CHANNELS) // WIDTH
    lane_of = iota((CHUNK, CHANNELS), 1) // WIDTH
    for g in range(GROUPS):
        straight = jnp.broadcast_to(turned_filters[g : g + 1, :], (CHUNK, CHUNK))
        straight = pltpu.roll(straight, 0, 1, stride=1, stride_axis=0)
        straight = split(jnp.where(across <= down, straight, 0.0))
        flipped = jnp.broadcast_to(filters[g : g + 1, :], (CHUNK, CHUNK))
        flipped = pltpu.roll(flipped, 0, 1, stride=1, stride_axis=0)
        flipped = split(jnp.where(across >= down, flipped, 0.0))
        forward = dot3(straight, gi)
        backward = dot3(flipped, gl)
        for q in range(CHUNKS):
            rows = pl.ds(q * CHUNK, CHUNK)
            if g == 0:
                long_ref[rows, :] = chunk_lanes(forward, q)
                gated_ref[rows, :] = chunk_lanes(backward, q)
            else:
                long_ref[rows, :] = jnp.where(lane_of == g, chunk_lanes(forward, q), long_ref[rows, :])
                gated_ref[rows, :] = jnp.where(lane_of == g, chunk_lanes(backward, q), gated_ref[rows, :])
        own = (wide_group == g).astype(F32).astype(BF16)
        products = dot3((mirrored[0] * own, mirrored[1] * own), gi, NT)
        products = jnp.where(across + down <= CHUNK - 1, products, 0.0)
        sheared = pltpu.roll(products, 1, 1, stride=1, stride_axis=0)
        lag_ref[g : g + 1, :] = jnp.sum(sheared, axis=0, keepdims=True)
    lag_grad = lag_ref[...]
    down_lag = lax.rem(CHUNK - down, CHUNK).astype(F32)
    powers = jnp.exp(-row * down_lag)
    residue_sums = lax.dot_general(lag_grad, powers, MM, precision=EXACT, preferred_element_type=F32)
    moment_sums = lax.dot_general(lag_grad, powers * down_lag, MM, precision=EXACT, preferred_element_type=F32)
    own_group = lane_group(GROUPS)
    small_ref[LOCAL : LOCAL + 1, :] = jnp.sum(residue_sums * own_group, axis=0, keepdims=True)
    small_ref[LOCAL + 1 : LOCAL + 2, :] = jnp.sum(moment_sums * own_group, axis=0, keepdims=True)
    small_rates = mode_compact(rates)
    chunk_decay = jnp.exp(-small_rates * CHUNK)
    lag_value = lag.astype(F32)
    end_moments = compact(dot3(split(descending * (CHUNK - 1 - lag_value)), gi))
    lead_moments = compact(dot3(split(ascending * (jnp.exp(-column) * (lag_value + 1.0))), gl))
    zero = jnp.zeros((MODES, CHANNELS), F32)
    leads = []
    state, moment = zero, zero
    residue_part, moment_part, lead_moment = zero, zero, zero
    offset_decay = jnp.ones((MODES, CHANNELS), F32)
    for q in range(CHUNKS):
        lead = chunk_lanes(states_ref[1], q)
        end = chunk_lanes(states_ref[0], q)
        if q == 0:
            end, lead = end + delta_ref[0], lead + delta_ref[1]
        leads.append(lead)
        lead_here = chunk_lanes(lead_moments, q)
        small_ref[piece(q), :] = state
        residue_part = residue_part + lead * state
        moment_part = moment_part + lead_here * state + lead * moment
        lead_moment = lead_moment + offset_decay * (lead_here + float(q * CHUNK) * lead)
        offset_decay = offset_decay * chunk_decay
        moment = chunk_decay * (moment + float(CHUNK) * state) + chunk_lanes(end_moments, q)
        state = chunk_decay * state + end
    back = zero
    for q in reversed(range(CHUNKS)):
        small_ref[piece(CHUNKS + q), :] = back
        back = chunk_decay * back + leads[q]
    for at, value in enumerate((residue_part, moment_part, lead_moment, moment, back)):
        small_ref[piece(2 * CHUNKS + at), :] = value


def finish_kernel(me_ref, arrived_ref, table_ref, near_ref,
                  kv_ref, patch_ref, out_grad_ref, proj_ref, before_ref, feature_ref, stats_ref, ext_ref):
    for i in range(3):
        ext_ref[i, 0:LEAD, :] = before_ref[i].astype(F32)
        ext_ref[i, LEAD:, :] = proj_ref[i].astype(F32)
    long_ref, gated_ref, small_ref = near_parts(near_ref)
    me = me_ref[0]
    rates, residues = table_ref[0], table_ref[1]
    row = mode_row(rates)
    small_rates = mode_compact(rates)
    small_residues = mode_compact(residues)
    chunk_decay = jnp.exp(-small_rates * CHUNK)
    zero = jnp.zeros((MODES, CHANNELS), F32)
    state_in, late_in, back_in = zero, zero, zero
    for at in range(arrived_ref.shape[0]):
        d = member(at, arrived_ref.shape[0])
        away = (jnp.abs(me - d) - 1).astype(F32) * float(ROWS)
        scale = jnp.exp2(arrived_ref[at, MODES : MODES + 1, :])
        term = jnp.exp(-small_rates * away) * (arrived_ref[at, 0:MODES, :] * scale)
        state_in = state_in + jnp.where(d < me, term, 0.0)
        late_in = late_in + jnp.where(d < me, term * away, 0.0)
        back_in = back_in + jnp.where(d > me, term, 0.0)
    states, backs = [], []
    carried = state_in
    for q in range(CHUNKS):
        states.append(small_residues * (small_ref[piece(q), :] + carried))
        carried = carried * chunk_decay
    carried = back_in
    for q in reversed(range(CHUNKS)):
        backs.insert(0, small_residues * (small_ref[piece(CHUNKS + q), :] + carried))
        carried = carried * chunk_decay
    down = iota((CHUNK, CHANNELS), 0).astype(F32)
    long_far = dot3(split(jnp.exp(-row * (down + 1.0))), expand(jnp.concatenate(states, axis=1)))
    gated_far = dot3(split(jnp.exp(-row * (CHUNK - 1 - down))), expand(jnp.concatenate(backs, axis=1)))
    sums = [jnp.zeros((8, CHANNELS), F32) for _ in range(3 * KW)]
    for q in range(CHUNKS):
        rows = pl.ds(q * CHUNK, CHUNK)
        signal = out_grad_ref[rows, :].astype(F32)
        grad_gated = gated_ref[rows, :] + chunk_lanes(gated_far, q)
        keyed, valued = kv_ref[0, rows, :], kv_ref[1, rows, :]
        if q == 0:
            keyed = jnp.concatenate([patch_ref[0], keyed[HEAD:, :]], axis=0)
            valued = jnp.concatenate([patch_ref[1], valued[HEAD:, :]], axis=0)
        parts = (
            signal * (long_ref[rows, :] + chunk_lanes(long_far, q)),
            grad_gated * valued,
            grad_gated * keyed,
        )
        for i in range(3):
            feature_ref[i, rows, :] = parts[i]
            for j in range(KW):
                product = parts[i] * ext_ref[i, pl.ds(LEAD - j + q * CHUNK, CHUNK), :]
                sums[i * KW + j] = sums[i * KW + j] + jnp.sum(
                    product.reshape(CHUNK // 8, 8, CHANNELS), axis=0
                )
    residue_part, moment_part, lead_moment, end_moment, lead = (
        small_ref[piece(2 * CHUNKS + at), :] for at in range(5)
    )
    residue_part = residue_part + lead * state_in
    moment_part = moment_part + lead_moment * state_in + lead * late_in + end_moment * back_in
    same = (iota((CHANNELS, CHANNELS), 0) // WIDTH == iota((CHANNELS, CHANNELS), 1) // MODES).astype(F32)
    pick = (iota((MODES, CHANNELS), 1) % MODES == iota((MODES, CHANNELS), 0)).astype(F32)

    def by_mode(part):
        spread = lax.dot_general(part, same, MM, precision=EXACT, preferred_element_type=F32)
        return jnp.sum(spread * pick, axis=0, keepdims=True)

    residue_row = small_ref[LOCAL : LOCAL + 1, :] + by_mode(residue_part)
    moment_row = small_ref[LOCAL + 1 : LOCAL + 2, :] + by_mode(moment_part)
    rate_row = -row * mode_row(residues) * moment_row
    lines = [jnp.sum(part, axis=0, keepdims=True) for part in sums]
    stats = jnp.concatenate(lines + [residue_row, rate_row, jnp.zeros((1, CHANNELS), F32)], axis=0)
    scaled, exponent = scaled_columns(stats)
    last = iota((STATS, CHANNELS), 0) == STATS - 1
    stats_ref[...] = jnp.where(last, exponent, scaled)


def inputs_kernel(feature_ref, after_ref, weight_ref, out_ref, ext_ref):
    for i in range(3):
        ext_ref[0:ROWS, :] = feature_ref[i]
        ext_ref[ROWS:, :] = after_ref[i]
        for q in range(CHUNKS):
            total = None
            for j in range(KW):
                term = weight_ref[i, j : j + 1, :] * ext_ref[pl.ds(j + q * CHUNK, CHUNK), :]
                total = term if total is None else total + term
            out_ref[i, pl.ds(q * CHUNK, CHUNK), :] = total.astype(BF16)


def total_kernel(stats_ref, total_ref, square_ref):
    total = jnp.zeros((STATS, CHANNELS), F32)
    for d in range(stats_ref.shape[0]):
        total = total + stats_ref[d] * jnp.exp2(stats_ref[d, STATS - 1 :, :])
    total = jnp.where(iota((STATS, CHANNELS), 0) == STATS - 1, 0.0, total)
    total_ref[...] = total
    square = jnp.sum(total * total, axis=0, keepdims=True)
    for d in range(square_ref.shape[0]):
        square_ref[d] = jnp.broadcast_to(square, square_ref.shape[1:])


def scale_kernel(square_ref, total_ref, conv_ref, residue_ref, rate_ref):
    squares = jnp.sum(jnp.sum(square_ref[:, 0, :], axis=0, keepdims=True), axis=1, keepdims=True)
    factor = jnp.minimum(1.0, lax.rsqrt(squares / (3 * KW * D + 2 * G * MODES) + 1e-6))
    total = total_ref[...] * factor
    for i in range(3):
        conv_ref[i] = total[i * KW : (i + 1) * KW, :]
    pick = (iota((MODES, CHANNELS), 1) % MODES == iota((MODES, CHANNELS), 0)).astype(F32)
    own = lane_group(GROUPS)
    at = 3 * KW
    residue_ref[...] = lax.dot_general(
        total[at : at + 1, :] * own, pick, NT, precision=EXACT, preferred_element_type=F32
    )
    rate_ref[...] = lax.dot_general(
        total[at + 1 : at + 2, :] * own, pick, NT, precision=EXACT, preferred_element_type=F32
    )


def shape(*dims, dtype=F32):
    return jax.ShapeDtypeStruct(dims, dtype)


VMEM = pl.BlockSpec(memory_space=pltpu.VMEM)
SMEM = pl.BlockSpec(memory_space=pltpu.SMEM)


HBM = pl.BlockSpec(memory_space=pltpu.HBM)


def call(kernel, name, out_shape, specs, cost_us, scratch=()):
    return pl.pallas_call(
        kernel,
        out_shape=out_shape,
        in_specs=specs,
        out_specs=jax.tree.map(lambda _: VMEM, out_shape),
        scratch_shapes=list(scratch),
        compiler_params=pltpu.CompilerParams(vmem_limit_bytes=12 * 2**20),
        cost_estimate=pl.CostEstimate(
            flops=int(cost_us * 1e9), bytes_accessed=int(cost_us * 3e6), transcendentals=0
        ),
        name=name,
    )


def exchange(blocks, axis, first):
    count = blocks.shape[0]
    return lax.all_to_all(blocks, axis, 0, 0, axis_index_groups=[[(first + p) % count for p in range(count)]])


def shards(projected, conv_weight, residues, decay_rates, grad_out):
    ctx = lax.axis_size("ctx")
    planes = lax.axis_size("ch")
    me = lax.axis_index("ctx").astype(jnp.int32).reshape(1)
    before = lax.ppermute(
        projected[:, ROWS - LEAD :, :], "ctx", [(source, source + 1) for source in range(ctx - 1)]
    )
    kv, pair, states, ends, head, powers, table = call(
        prepare_kernel, "prepare",
        (shape(2, ROWS, CHANNELS), shape(2, CHUNK, CHUNKS * CHANNELS), shape(2, MODES, CHUNKS * CHANNELS),
         shape(2, MODES, CHANNELS), shape(4, HEAD, CHANNELS), shape(3, HEAD, MODES, CHANNELS),
         shape(2, GROUPS, MODES)),
        [VMEM] * 3 + [HBM] * 2, 3,
        scratch=[pltpu.VMEM((3, ROWS, CHANNELS), BF16), pltpu.VMEM((ROWS, CHANNELS), BF16),
                 pltpu.VMEM((3, LEAD + ROWS, CHANNELS), F32), pltpu.SemaphoreType.DMA((2,))],
    )(conv_weight, decay_rates, residues,
      *(pltpu.with_memory_space_constraint(part, pltpu.HBM) for part in (projected, grad_out)))
    patch, delta, send = call(
        patch_kernel, "patch",
        (shape(4, HEAD, CHANNELS), shape(2, MODES, CHANNELS), shape(2, MODES + 8, CHANNELS)),
        [VMEM] * 5, 1,
        scratch=[pltpu.VMEM((LEAD + HEAD, CHANNELS), F32)],
    )(before, conv_weight, head, powers, ends)
    later = member(lax.broadcasted_iota(jnp.int32, (ctx, 1, 1), 0), ctx) > me.reshape(1, 1, 1)
    send = jnp.where(later, send[1], send[0]).astype(F16)
    arrived = exchange(send, "ctx", ctx // 2).astype(F32)
    near = call(
        middle_kernel, "within",
        shape(2 * ROWS + LOCAL + 8, CHANNELS),
        [VMEM] * 5, 8,
        scratch=[pltpu.VMEM((GROUPS, CHANNELS), F32)],
    )(table, pair, states, patch, delta)
    grad_feature, stats = call(
        finish_kernel, "across",
        (shape(3, ROWS, CHANNELS), shape(STATS, CHANNELS)),
        [SMEM] + [VMEM] * 8, 4,
        scratch=[pltpu.VMEM((3, LEAD + ROWS, CHANNELS), F32)],
    )(me, arrived, table, near, kv, patch, grad_out, projected, before)
    after = lax.ppermute(
        grad_feature[:, :8, :], "ctx", [(source + 1, source) for source in range(ctx - 1)]
    )
    stats = jnp.broadcast_to(stats.astype(F16), (ctx, STATS, CHANNELS))
    gathered = exchange(stats, "ctx", ctx // 2).astype(F32)
    grad_projected = call(
        inputs_kernel, "inputs", shape(3, ROWS, CHANNELS, dtype=BF16), [VMEM] * 3, 2,
        scratch=[pltpu.VMEM((ROWS + 8, CHANNELS), F32)],
    )(grad_feature, after, conv_weight)
    total, square = call(
        total_kernel, "total", (shape(STATS, CHANNELS), shape(planes, 1, CHANNELS)), [VMEM], 1,
    )(gathered)
    squares = exchange(square, "ch", planes // 2 + planes // 8)
    grad_conv, grad_residues, grad_log_rates = call(
        scale_kernel, "scale",
        (shape(3, KW, CHANNELS), shape(GROUPS, MODES), shape(GROUPS, MODES)), [VMEM] * 2, 1,
    )(squares, total)
    return grad_projected, grad_conv, grad_residues, grad_log_rates


def solution(mesh):
    in_specs = (
        P(None, "ctx", "ch"),
        P(None, None, "ch"),
        P("ch", None),
        P("ch", None),
        P("ctx", "ch"),
    )
    out_specs = (P(None, "ctx", "ch"), P(None, None, "ch"), P("ch", None), P("ch", None))
    return jax.shard_map(shards, mesh=mesh, in_specs=in_specs, out_specs=out_specs, check_vma=False)
```

```python
import jax
import jax.numpy as jnp
from jax import lax
from jax.experimental import pallas as pl
from jax.experimental.pallas import tpu as pltpu
from jax.sharding import PartitionSpec as P

D = 4096
G = 256
MODES = 16
KW = 7

ROWS = 512
CHANNELS = 128
GROUPS = 8
WIDTH = 16
CHUNK = 128
CHUNKS = ROWS // CHUNK
LEAD = 16
HEAD = 8
STATS = 24
FACTOR = 2 * CHUNKS + 5
LOCAL = (FACTOR + CHUNKS) * MODES
POWER = FACTOR + CHUNKS + 1

F32 = jnp.float32
BF16 = jnp.bfloat16
F16 = jnp.float16
EXACT = lax.Precision.HIGHEST
MM = (((1,), (0,)), ((), ()))
NT = (((1,), (1,)), ((), ()))


def split(value):
    high = value.astype(BF16)
    low = (value - high.astype(F32)).astype(BF16)
    return high, low


def dot3(left, right, dims=MM):
    lh, ll = left
    rh, rl = right

    def product(a, b):
        return lax.dot_general(a, b, dims, preferred_element_type=F32)

    return product(lh, rh) + (product(lh, rl) + product(ll, rh))


def iota(shape, axis):
    return lax.broadcasted_iota(jnp.int32, shape, axis)


def lane_group(rows):
    return (iota((rows, CHANNELS), 1) // WIDTH == iota((rows, CHANNELS), 0)).astype(F32)


def mode_row(table):
    pick = (iota((MODES, CHANNELS), 1) % MODES == iota((MODES, CHANNELS), 0)).astype(F32)
    spread = lax.dot_general(table, pick, MM, precision=EXACT, preferred_element_type=F32)
    return jnp.sum(spread * lane_group(GROUPS), axis=0, keepdims=True)


def mode_column(row):
    eye = iota((CHANNELS, CHANNELS), 0) == iota((CHANNELS, CHANNELS), 1)
    return jnp.sum(jnp.where(eye, row, 0.0), axis=1, keepdims=True)


def mode_compact(table):
    return lax.dot_general(
        table, lane_group(GROUPS), (((0,), (0,)), ((), ())), precision=EXACT, preferred_element_type=F32
    )


def compact(full):
    lanes = full.shape[1]
    total = None
    for g in range(GROUPS):
        own = (iota((MODES, lanes), 1) % CHANNELS) // WIDTH == g
        part = jnp.where(own, full[g * MODES : (g + 1) * MODES, :], 0.0)
        total = part if total is None else total + part
    return total


def expand(small):
    lanes = small.shape[1]
    own = (iota((CHANNELS, lanes), 0) // MODES == (iota((CHANNELS, lanes), 1) % CHANNELS) // WIDTH).astype(F32)
    return split(jnp.concatenate([small] * GROUPS, axis=0) * own)


def near_parts(near_ref):
    return near_ref.at[0:ROWS, :], near_ref.at[ROWS : 2 * ROWS, :], near_ref.at[2 * ROWS :, :]


def member(position, count):
    return (position + count // 2) % count


def piece(at):
    return slice(at * MODES, (at + 1) * MODES)


def chunk_lanes(value, q):
    return value[:, q * CHANNELS : (q + 1) * CHANNELS]


def prepare_kernel(weight_ref, rate_ref, residue_ref, proj_ref, out_grad_ref,
                   kv_ref, pair_ref, states_ref, ends_ref, head_ref, power_ref, table_ref,
                   raw_ref, signal_ref, ext_ref, sem_ref):
    gi_ref, gl_ref = pair_ref.at[0], pair_ref.at[1]
    copies = [
        pltpu.make_async_copy(proj_ref, raw_ref, sem_ref.at[0]),
        pltpu.make_async_copy(out_grad_ref, signal_ref, sem_ref.at[1]),
    ]
    for copy in copies:
        copy.start()
    rates = rate_ref[...]
    table_ref[0] = rates
    table_ref[1] = residue_ref[...]
    column = mode_column(mode_row(rates))
    lag = iota((CHANNELS, CHUNK), 1).astype(F32)
    ascending = split(jnp.exp(-column * lag))
    descending = split(jnp.exp(-column * (CHUNK - 1 - lag)))
    small_rates = mode_compact(rates)
    one_step = jnp.exp(-small_rates)
    chunk_decay = jnp.exp(-small_rates * CHUNK)
    for r in range(HEAD):
        power_ref[0, r] = jnp.exp(-small_rates * float(CHUNK - 1 - r))
        power_ref[1, r] = jnp.exp(-small_rates * float(r + 1))
    power_ref[2, 0] = jnp.exp(-small_rates * float(ROWS - CHUNK))
    for r in range(1, HEAD):
        power_ref[2, r] = jnp.zeros((MODES, CHANNELS), F32)
    for copy in copies:
        copy.wait()
    for i in range(3):
        ext_ref[i, 0:LEAD, :] = jnp.zeros((LEAD, CHANNELS), F32)
        ext_ref[i, LEAD:, :] = raw_ref[i].astype(F32)
    blank = jnp.zeros((HEAD, CHANNELS), F32)
    for q in range(CHUNKS):
        feature = []
        for i in range(3):
            total = None
            for j in range(KW):
                term = weight_ref[i, j : j + 1, :] * ext_ref[i, pl.ds(LEAD - j + q * CHUNK, CHUNK), :]
                total = term if total is None else total + term
            feature.append(total)
        rows = pl.ds(q * CHUNK, CHUNK)
        lanes = slice(q * CHANNELS, (q + 1) * CHANNELS)
        signal = signal_ref[rows, :].astype(F32)
        kv_ref[0, rows, :] = feature[1]
        kv_ref[1, rows, :] = feature[2]
        gi_ref[:, lanes] = feature[1] * feature[2]
        gl_ref[:, lanes] = signal * feature[0]
        if q == 0:
            for i in range(3):
                head_ref[i] = feature[i][0:HEAD, :]
            head_ref[3] = signal[0:HEAD, :]
            gi_ref[0:HEAD, lanes] = blank
            gl_ref[0:HEAD, lanes] = blank
    ends = compact(dot3(descending, split(gi_ref[...])))
    leads = compact(dot3(ascending, split(gl_ref[...])))
    state = jnp.zeros((MODES, CHANNELS), F32)
    for q in range(CHUNKS):
        part = chunk_lanes(ends, q)
        states_ref[0, :, q * CHANNELS : (q + 1) * CHANNELS] = part
        state = chunk_decay * state + part
    back = jnp.zeros((MODES, CHANNELS), F32)
    for q in reversed(range(CHUNKS)):
        part = one_step * chunk_lanes(leads, q)
        states_ref[1, :, q * CHANNELS : (q + 1) * CHANNELS] = part
        back = chunk_decay * back + part
    ends_ref[0] = state
    ends_ref[1] = back


def scaled_columns(value):
    largest = jnp.max(jnp.abs(value), axis=0, keepdims=True)
    exponent = jnp.ceil(jnp.log2(jnp.maximum(largest, 1e-30))) - 15.0
    return value * jnp.exp2(-exponent), exponent


def patch_kernel(before_ref, weight_ref, head_ref, power_ref, ends_ref,
                 patch_ref, delta_ref, send_ref, ext_ref):
    feature = []
    for i in range(3):
        ext_ref[0:LEAD, :] = before_ref[i].astype(F32)
        ext_ref[LEAD:, :] = jnp.zeros((HEAD, CHANNELS), F32)
        total = head_ref[i]
        for j in range(1, KW):
            total = total + weight_ref[i, j : j + 1, :] * ext_ref[pl.ds(LEAD - j, HEAD), :]
        feature.append(total)
    gi = feature[1] * feature[2]
    gl = head_ref[3] * feature[0]
    for at, value in enumerate((feature[1], feature[2], gi, gl)):
        patch_ref[at] = value
    state_part, back_part = None, None
    for r in range(HEAD):
        ahead = power_ref[0, r] * gi[r : r + 1, :]
        behind = power_ref[1, r] * gl[r : r + 1, :]
        state_part = ahead if r == 0 else state_part + ahead
        back_part = behind if r == 0 else back_part + behind
    delta_ref[0] = state_part
    delta_ref[1] = back_part
    state = ends_ref[0] + power_ref[2, 0] * state_part
    back = ends_ref[1] + back_part
    for at, value in enumerate((back, state)):
        scaled, exponent = scaled_columns(value)
        send_ref[at, 0:MODES, :] = scaled
        send_ref[at, MODES:, :] = jnp.broadcast_to(exponent, (8, CHANNELS))


def spliced(wide_ref, patch):
    top = jnp.concatenate([patch, wide_ref[0:HEAD, CHANNELS:]], axis=1)
    return jnp.concatenate([top, wide_ref[HEAD:, :]], axis=0)


def middle_kernel(me_ref, table_ref, pair_ref, states_ref, patch_ref, delta_ref,
                  near_ref, halves_ref, lag_ref):
    long_ref, gated_ref, small_ref = near_parts(near_ref)
    gi_ref, gl_ref = pair_ref.at[0], pair_ref.at[1]
    rates = table_ref[0]
    row = mode_row(rates)
    column = mode_column(row)
    lag = iota((CHANNELS, CHUNK), 1)
    back_lag = lax.rem(CHUNK - lag, CHUNK)
    ascending = jnp.exp(-column * lag.astype(F32))
    descending = jnp.exp(-column * (CHUNK - 1 - lag).astype(F32))
    turned = jnp.exp(-column * back_lag.astype(F32))
    residue_row = mode_row(table_ref[1]) * lane_group(GROUPS)
    filters = lax.dot_general(residue_row, ascending, MM, precision=EXACT, preferred_element_type=F32)
    turned_filters = lax.dot_general(residue_row, turned, MM, precision=EXACT, preferred_element_type=F32)
    gi = split(spliced(gi_ref, patch_ref[2]))
    gl = split(spliced(gl_ref, patch_ref[3]))
    down = iota((CHUNK, CHUNK), 0)
    across = iota((CHUNK, CHUNK), 1)
    mirror = (down + across == CHUNK - 1).astype(F32).astype(BF16)
    mirrored = [
        lax.dot_general(mirror, part, MM, preferred_element_type=F32).astype(BF16) for part in gl
    ]
    wide_group = (iota((1, ROWS), 1) % CHANNELS) // WIDTH
    lane_of = iota((CHUNK, CHANNELS), 1) // WIDTH
    for g in range(GROUPS):
        straight = jnp.broadcast_to(turned_filters[g : g + 1, :], (CHUNK, CHUNK))
        straight = pltpu.roll(straight, 0, 1, stride=1, stride_axis=0)
        straight = split(jnp.where(across <= down, straight, 0.0))
        flipped = jnp.broadcast_to(filters[g : g + 1, :], (CHUNK, CHUNK))
        flipped = pltpu.roll(flipped, 0, 1, stride=1, stride_axis=0)
        flipped = split(jnp.where(across >= down, flipped, 0.0))
        forward = dot3(straight, gi)
        backward = dot3(flipped, gl)
        for q in range(CHUNKS):
            rows = pl.ds(q * CHUNK, CHUNK)
            if g == 0:
                long_ref[rows, :] = chunk_lanes(forward, q)
                gated_ref[rows, :] = chunk_lanes(backward, q)
            else:
                long_ref[rows, :] = jnp.where(lane_of == g, chunk_lanes(forward, q), long_ref[rows, :])
                gated_ref[rows, :] = jnp.where(lane_of == g, chunk_lanes(backward, q), gated_ref[rows, :])
        own = (wide_group == g).astype(F32).astype(BF16)
        products = dot3((mirrored[0] * own, mirrored[1] * own), gi, NT)
        products = jnp.where(across + down <= CHUNK - 1, products, 0.0)
        sheared = pltpu.roll(products, 1, 1, stride=1, stride_axis=0)
        lag_ref[g : g + 1, :] = jnp.sum(sheared, axis=0, keepdims=True)
    lag_grad = lag_ref[...]
    down_lag = lax.rem(CHUNK - down, CHUNK).astype(F32)
    powers = jnp.exp(-row * down_lag)
    residue_sums = lax.dot_general(lag_grad, powers, MM, precision=EXACT, preferred_element_type=F32)
    moment_sums = lax.dot_general(lag_grad, powers * down_lag, MM, precision=EXACT, preferred_element_type=F32)
    own_group = lane_group(GROUPS)
    small_ref[LOCAL + 2 : LOCAL + 3, :] = -row * mode_row(table_ref[1])
    small_ref[LOCAL : LOCAL + 1, :] = jnp.sum(residue_sums * own_group, axis=0, keepdims=True)
    small_ref[LOCAL + 1 : LOCAL + 2, :] = jnp.sum(moment_sums * own_group, axis=0, keepdims=True)
    small_rates = mode_compact(rates)
    small_residues = mode_compact(table_ref[1])
    chunk_decay = jnp.exp(-small_rates * CHUNK)
    lag_value = lag.astype(F32)
    end_moments = compact(dot3(split(descending * (CHUNK - 1 - lag_value)), gi))
    lead_moments = compact(dot3(split(ascending * (jnp.exp(-column) * (lag_value + 1.0))), gl))
    zero = jnp.zeros((MODES, CHANNELS), F32)
    leads = []
    state, moment = zero, zero
    residue_part, moment_part, lead_moment = zero, zero, zero
    offset_decay = jnp.ones((MODES, CHANNELS), F32)
    for q in range(CHUNKS):
        lead = chunk_lanes(states_ref[1], q)
        end = chunk_lanes(states_ref[0], q)
        if q == 0:
            end, lead = end + delta_ref[0], lead + delta_ref[1]
        leads.append(lead)
        lead_here = chunk_lanes(lead_moments, q)
        small_ref[piece(q), :] = small_residues * state
        residue_part = residue_part + lead * state
        moment_part = moment_part + lead_here * state + lead * moment
        lead_moment = lead_moment + offset_decay * (lead_here + float(q * CHUNK) * lead)
        offset_decay = offset_decay * chunk_decay
        moment = chunk_decay * (moment + float(CHUNK) * state) + chunk_lanes(end_moments, q)
        state = chunk_decay * state + end
    back = zero
    for q in reversed(range(CHUNKS)):
        small_ref[piece(CHUNKS + q), :] = small_residues * back
        back = chunk_decay * back + leads[q]
    for at, value in enumerate((residue_part, moment_part, lead_moment, moment, back)):
        small_ref[piece(2 * CHUNKS + at), :] = value
    factor = small_residues
    for q in range(CHUNKS):
        small_ref[piece(FACTOR + q), :] = factor
        factor = factor * chunk_decay
    count = small_ref.shape[0] // MODES - POWER
    for at in range(count):
        away = jnp.maximum(jnp.abs(me_ref[0] - member(at, count)) - 1, 0).astype(F32) * float(ROWS)
        small_ref[piece(POWER + at), :] = jnp.exp(-small_rates * away)
    steps = down.astype(F32)
    halves_ref[0], halves_ref[1] = split(jnp.exp(-row * (steps + 1.0)))
    halves_ref[2], halves_ref[3] = split(jnp.exp(-row * (CHUNK - 1 - steps)))


def finish_kernel(me_ref, arrived_ref, near_ref, halves_ref,
                  kv_ref, patch_ref, out_grad_ref, proj_ref, before_ref, feature_ref, stats_ref, ext_ref):
    for i in range(3):
        ext_ref[i, 0:LEAD, :] = before_ref[i].astype(F32)
        ext_ref[i, LEAD:, :] = proj_ref[i].astype(F32)
    long_ref, gated_ref, small_ref = near_parts(near_ref)
    me = me_ref[0]
    zero = jnp.zeros((MODES, CHANNELS), F32)
    state_in, late_in, back_in = zero, zero, zero
    for at in range(arrived_ref.shape[0]):
        d = member(at, arrived_ref.shape[0])
        away = (jnp.abs(me - d) - 1).astype(F32) * float(ROWS)
        scale = jnp.exp2(arrived_ref[at, MODES : MODES + 1, :])
        term = small_ref[piece(POWER + at), :] * (arrived_ref[at, 0:MODES, :] * scale)
        state_in = state_in + jnp.where(d < me, term, 0.0)
        late_in = late_in + jnp.where(d < me, term * away, 0.0)
        back_in = back_in + jnp.where(d > me, term, 0.0)
    states, backs = [], []
    for q in range(CHUNKS):
        states.append(small_ref[piece(q), :] + small_ref[piece(FACTOR + q), :] * state_in)
        backs.append(small_ref[piece(CHUNKS + q), :] + small_ref[piece(FACTOR + CHUNKS - 1 - q), :] * back_in)
    long_far = dot3((halves_ref[0], halves_ref[1]), expand(jnp.concatenate(states, axis=1)))
    gated_far = dot3((halves_ref[2], halves_ref[3]), expand(jnp.concatenate(backs, axis=1)))
    sums = [jnp.zeros((8, CHANNELS), F32) for _ in range(3 * KW)]
    for q in range(CHUNKS):
        rows = pl.ds(q * CHUNK, CHUNK)
        signal = out_grad_ref[rows, :].astype(F32)
        grad_gated = gated_ref[rows, :] + chunk_lanes(gated_far, q)
        keyed, valued = kv_ref[0, rows, :], kv_ref[1, rows, :]
        if q == 0:
            keyed = jnp.concatenate([patch_ref[0], keyed[HEAD:, :]], axis=0)
            valued = jnp.concatenate([patch_ref[1], valued[HEAD:, :]], axis=0)
        parts = (
            signal * (long_ref[rows, :] + chunk_lanes(long_far, q)),
            grad_gated * valued,
            grad_gated * keyed,
        )
        for i in range(3):
            feature_ref[i, rows, :] = parts[i]
            for j in range(KW):
                product = parts[i] * ext_ref[i, pl.ds(LEAD - j + q * CHUNK, CHUNK), :]
                sums[i * KW + j] = sums[i * KW + j] + jnp.sum(
                    product.reshape(CHUNK // 8, 8, CHANNELS), axis=0
                )
    residue_part, moment_part, lead_moment, end_moment, lead = (
        small_ref[piece(2 * CHUNKS + at), :] for at in range(5)
    )
    residue_part = residue_part + lead * state_in
    moment_part = moment_part + lead_moment * state_in + lead * late_in + end_moment * back_in
    same = (iota((CHANNELS, CHANNELS), 0) // WIDTH == iota((CHANNELS, CHANNELS), 1) // MODES).astype(F32)
    pick = (iota((MODES, CHANNELS), 1) % MODES == iota((MODES, CHANNELS), 0)).astype(F32)

    def by_mode(part):
        spread = lax.dot_general(part, same, MM, precision=EXACT, preferred_element_type=F32)
        return jnp.sum(spread * pick, axis=0, keepdims=True)

    residue_row = small_ref[LOCAL : LOCAL + 1, :] + by_mode(residue_part)
    moment_row = small_ref[LOCAL + 1 : LOCAL + 2, :] + by_mode(moment_part)
    rate_row = small_ref[LOCAL + 2 : LOCAL + 3, :] * moment_row
    lines = [jnp.sum(part, axis=0, keepdims=True) for part in sums]
    stats = jnp.concatenate(lines + [residue_row, rate_row, jnp.zeros((1, CHANNELS), F32)], axis=0)
    scaled, exponent = scaled_columns(stats)
    last = iota((STATS, CHANNELS), 0) == STATS - 1
    stats_ref[...] = jnp.where(last, exponent, scaled)


def inputs_kernel(feature_ref, after_ref, weight_ref, out_ref, ext_ref):
    for i in range(3):
        ext_ref[0:ROWS, :] = feature_ref[i]
        ext_ref[ROWS:, :] = after_ref[i]
        for q in range(CHUNKS):
            total = None
            for j in range(KW):
                term = weight_ref[i, j : j + 1, :] * ext_ref[pl.ds(j + q * CHUNK, CHUNK), :]
                total = term if total is None else total + term
            out_ref[i, pl.ds(q * CHUNK, CHUNK), :] = total.astype(BF16)


def total_kernel(stats_ref, total_ref, square_ref):
    total = jnp.zeros((STATS, CHANNELS), F32)
    for d in range(stats_ref.shape[0]):
        total = total + stats_ref[d] * jnp.exp2(stats_ref[d, STATS - 1 :, :])
    total = jnp.where(iota((STATS, CHANNELS), 0) == STATS - 1, 0.0, total)
    total_ref[...] = total
    square = jnp.sum(total * total, axis=0, keepdims=True)
    for d in range(square_ref.shape[0]):
        square_ref[d] = jnp.broadcast_to(square, square_ref.shape[1:])


def scale_kernel(square_ref, total_ref, conv_ref, residue_ref, rate_ref):
    squares = jnp.sum(jnp.sum(square_ref[:, 0, :], axis=0, keepdims=True), axis=1, keepdims=True)
    factor = jnp.minimum(1.0, lax.rsqrt(squares / (3 * KW * D + 2 * G * MODES) + 1e-6))
    total = total_ref[...] * factor
    for i in range(3):
        conv_ref[i] = total[i * KW : (i + 1) * KW, :]
    pick = (iota((MODES, CHANNELS), 1) % MODES == iota((MODES, CHANNELS), 0)).astype(F32)
    own = lane_group(GROUPS)
    at = 3 * KW
    residue_ref[...] = lax.dot_general(
        total[at : at + 1, :] * own, pick, NT, precision=EXACT, preferred_element_type=F32
    )
    rate_ref[...] = lax.dot_general(
        total[at + 1 : at + 2, :] * own, pick, NT, precision=EXACT, preferred_element_type=F32
    )


def shape(*dims, dtype=F32):
    return jax.ShapeDtypeStruct(dims, dtype)


VMEM = pl.BlockSpec(memory_space=pltpu.VMEM)
SMEM = pl.BlockSpec(memory_space=pltpu.SMEM)


HBM = pl.BlockSpec(memory_space=pltpu.HBM)


def call(kernel, name, out_shape, specs, cost_us, scratch=()):
    return pl.pallas_call(
        kernel,
        out_shape=out_shape,
        in_specs=specs,
        out_specs=jax.tree.map(lambda _: VMEM, out_shape),
        scratch_shapes=list(scratch),
        compiler_params=pltpu.CompilerParams(vmem_limit_bytes=12 * 2**20),
        cost_estimate=pl.CostEstimate(
            flops=int(cost_us * 1e9), bytes_accessed=int(cost_us * 3e6), transcendentals=0
        ),
        name=name,
    )


def exchange(blocks, axis, first):
    count = blocks.shape[0]
    return lax.all_to_all(blocks, axis, 0, 0, axis_index_groups=[[(first + p) % count for p in range(count)]])


def shards(projected, conv_weight, residues, decay_rates, grad_out):
    ctx = lax.axis_size("ctx")
    planes = lax.axis_size("ch")
    me = lax.axis_index("ctx").astype(jnp.int32).reshape(1)
    before = lax.ppermute(
        projected[:, ROWS - LEAD :, :], "ctx", [(source, source + 1) for source in range(ctx - 1)]
    )
    kv, pair, states, ends, head, powers, table = call(
        prepare_kernel, "prepare",
        (shape(2, ROWS, CHANNELS), shape(2, CHUNK, CHUNKS * CHANNELS), shape(2, MODES, CHUNKS * CHANNELS),
         shape(2, MODES, CHANNELS), shape(4, HEAD, CHANNELS), shape(3, HEAD, MODES, CHANNELS),
         shape(2, GROUPS, MODES)),
        [VMEM] * 3 + [HBM] * 2, 3,
        scratch=[pltpu.VMEM((3, ROWS, CHANNELS), BF16), pltpu.VMEM((ROWS, CHANNELS), BF16),
                 pltpu.VMEM((3, LEAD + ROWS, CHANNELS), F32), pltpu.SemaphoreType.DMA((2,))],
    )(conv_weight, decay_rates, residues,
      *(pltpu.with_memory_space_constraint(part, pltpu.HBM) for part in (projected, grad_out)))
    patch, delta, send = call(
        patch_kernel, "patch",
        (shape(4, HEAD, CHANNELS), shape(2, MODES, CHANNELS), shape(2, MODES + 8, CHANNELS)),
        [VMEM] * 5, 1,
        scratch=[pltpu.VMEM((LEAD + HEAD, CHANNELS), F32)],
    )(before, conv_weight, head, powers, ends)
    later = member(lax.broadcasted_iota(jnp.int32, (ctx, 1, 1), 0), ctx) > me.reshape(1, 1, 1)
    send = jnp.where(later, send[1], send[0]).astype(F16)
    arrived = exchange(send, "ctx", ctx // 2).astype(F32)
    near, halves = call(
        middle_kernel, "within",
        (shape(2 * ROWS + (POWER + ctx) * MODES, CHANNELS), shape(4, CHUNK, CHANNELS, dtype=BF16)),
        [SMEM] + [VMEM] * 5, 8,
        scratch=[pltpu.VMEM((GROUPS, CHANNELS), F32)],
    )(me, table, pair, states, patch, delta)
    grad_feature, stats = call(
        finish_kernel, "across",
        (shape(3, ROWS, CHANNELS), shape(STATS, CHANNELS)),
        [SMEM] + [VMEM] * 8, 4,
        scratch=[pltpu.VMEM((3, LEAD + ROWS, CHANNELS), F32)],
    )(me, arrived, near, halves, kv, patch, grad_out, projected, before)
    after = lax.ppermute(
        grad_feature[:, :8, :], "ctx", [(source + 1, source) for source in range(ctx - 1)]
    )
    stats = jnp.broadcast_to(stats.astype(F16), (ctx, STATS, CHANNELS))
    gathered = exchange(stats, "ctx", ctx // 2).astype(F32)
    grad_projected = call(
        inputs_kernel, "inputs", shape(3, ROWS, CHANNELS, dtype=BF16), [VMEM] * 3, 2,
        scratch=[pltpu.VMEM((ROWS + 8, CHANNELS), F32)],
    )(grad_feature, after, conv_weight)
    total, square = call(
        total_kernel, "total", (shape(STATS, CHANNELS), shape(planes, 1, CHANNELS)), [VMEM], 1,
    )(gathered)
    squares = exchange(square, "ch", planes // 2 + planes // 8)
    grad_conv, grad_residues, grad_log_rates = call(
        scale_kernel, "scale",
        (shape(3, KW, CHANNELS), shape(GROUPS, MODES), shape(GROUPS, MODES)), [VMEM] * 2, 1,
    )(squares, total)
    return grad_projected, grad_conv, grad_residues, grad_log_rates


def solution(mesh):
    in_specs = (
        P(None, "ctx", "ch"),
        P(None, None, "ch"),
        P("ch", None),
        P("ch", None),
        P("ctx", "ch"),
    )
    out_specs = (P(None, "ctx", "ch"), P(None, None, "ch"), P("ch", None), P("ch", None))
    return jax.shard_map(shards, mesh=mesh, in_specs=in_specs, out_specs=out_specs, check_vma=False)
```

```python
import jax
import jax.numpy as jnp
from jax import lax
from jax.experimental import pallas as pl
from jax.experimental.pallas import tpu as pltpu
from jax.sharding import PartitionSpec as P

D = 4096
G = 256
MODES = 16
KW = 7

ROWS = 512
CHANNELS = 128
GROUPS = 8
WIDTH = 16
CHUNK = 128
CHUNKS = ROWS // CHUNK
LEAD = 16
HEAD = 8
STATS = 24
FACTOR = 2 * CHUNKS + 5
LOCAL = (FACTOR + CHUNKS) * MODES
POWER = FACTOR + CHUNKS + 1

F32 = jnp.float32
BF16 = jnp.bfloat16
F16 = jnp.float16
EXACT = lax.Precision.HIGHEST
MM = (((1,), (0,)), ((), ()))
NT = (((1,), (1,)), ((), ()))


def split(value):
    high = value.astype(BF16)
    low = (value - high.astype(F32)).astype(BF16)
    return high, low


def dot3(left, right, dims=MM):
    lh, ll = left
    rh, rl = right

    def product(a, b):
        return lax.dot_general(a, b, dims, preferred_element_type=F32)

    return product(lh, rh) + (product(lh, rl) + product(ll, rh))


def iota(shape, axis):
    return lax.broadcasted_iota(jnp.int32, shape, axis)


def lane_group(rows):
    return (iota((rows, CHANNELS), 1) // WIDTH == iota((rows, CHANNELS), 0)).astype(F32)


def mode_row(table):
    pick = (iota((MODES, CHANNELS), 1) % MODES == iota((MODES, CHANNELS), 0)).astype(F32)
    spread = lax.dot_general(table, pick, MM, precision=EXACT, preferred_element_type=F32)
    return jnp.sum(spread * lane_group(GROUPS), axis=0, keepdims=True)


def mode_column(row):
    eye = iota((CHANNELS, CHANNELS), 0) == iota((CHANNELS, CHANNELS), 1)
    return jnp.sum(jnp.where(eye, row, 0.0), axis=1, keepdims=True)


def mode_compact(table):
    return lax.dot_general(
        table, lane_group(GROUPS), (((0,), (0,)), ((), ())), precision=EXACT, preferred_element_type=F32
    )


def compact(full):
    lanes = full.shape[1]
    total = None
    for g in range(GROUPS):
        own = (iota((MODES, lanes), 1) % CHANNELS) // WIDTH == g
        part = jnp.where(own, full[g * MODES : (g + 1) * MODES, :], 0.0)
        total = part if total is None else total + part
    return total


def expand(small):
    lanes = small.shape[1]
    own = (iota((CHANNELS, lanes), 0) // MODES == (iota((CHANNELS, lanes), 1) % CHANNELS) // WIDTH).astype(F32)
    return split(jnp.concatenate([small] * GROUPS, axis=0) * own)


def near_parts(near_ref):
    return near_ref.at[0:ROWS, :], near_ref.at[ROWS : 2 * ROWS, :], near_ref.at[2 * ROWS :, :]


def member(position, count):
    return (position + count // 2) % count


def piece(at):
    return slice(at * MODES, (at + 1) * MODES)


def chunk_lanes(value, q):
    return value[:, q * CHANNELS : (q + 1) * CHANNELS]


def prepare_kernel(weight_ref, rate_ref, residue_ref, proj_ref, out_grad_ref,
                   kv_ref, pair_ref, states_ref, ends_ref, head_ref, power_ref, table_ref,
                   raw_ref, signal_ref, ext_ref, sem_ref):
    gi_ref, gl_ref = pair_ref.at[0], pair_ref.at[1]
    copies = [
        pltpu.make_async_copy(proj_ref, raw_ref, sem_ref.at[0]),
        pltpu.make_async_copy(out_grad_ref, signal_ref, sem_ref.at[1]),
    ]
    for copy in copies:
        copy.start()
    rates = rate_ref[...]
    table_ref[0] = rates
    table_ref[1] = residue_ref[...]
    column = mode_column(mode_row(rates))
    lag = iota((CHANNELS, CHUNK), 1).astype(F32)
    ascending = split(jnp.exp(-column * lag))
    descending = split(jnp.exp(-column * (CHUNK - 1 - lag)))
    small_rates = mode_compact(rates)
    one_step = jnp.exp(-small_rates)
    chunk_decay = jnp.exp(-small_rates * CHUNK)
    for r in range(HEAD):
        power_ref[0, r] = jnp.exp(-small_rates * float(CHUNK - 1 - r))
        power_ref[1, r] = jnp.exp(-small_rates * float(r + 1))
    power_ref[2, 0] = jnp.exp(-small_rates * float(ROWS - CHUNK))
    for r in range(1, HEAD):
        power_ref[2, r] = jnp.zeros((MODES, CHANNELS), F32)
    for copy in copies:
        copy.wait()
    for i in range(3):
        ext_ref[i, 0:LEAD, :] = jnp.zeros((LEAD, CHANNELS), F32)
        ext_ref[i, LEAD:, :] = raw_ref[i].astype(F32)
    blank = jnp.zeros((HEAD, CHANNELS), F32)
    for q in range(CHUNKS):
        feature = []
        for i in range(3):
            total = None
            for j in range(KW):
                term = weight_ref[i, j : j + 1, :] * ext_ref[i, pl.ds(LEAD - j + q * CHUNK, CHUNK), :]
                total = term if total is None else total + term
            feature.append(total)
        rows = pl.ds(q * CHUNK, CHUNK)
        lanes = slice(q * CHANNELS, (q + 1) * CHANNELS)
        signal = signal_ref[rows, :].astype(F32)
        kv_ref[0, rows, :] = feature[1]
        kv_ref[1, rows, :] = feature[2]
        gi_ref[:, lanes] = feature[1] * feature[2]
        gl_ref[:, lanes] = signal * feature[0]
        if q == 0:
            for i in range(3):
                head_ref[i] = feature[i][0:HEAD, :]
            head_ref[3] = signal[0:HEAD, :]
            gi_ref[0:HEAD, lanes] = blank
            gl_ref[0:HEAD, lanes] = blank
    ends = compact(dot3(descending, split(gi_ref[...])))
    leads = compact(dot3(ascending, split(gl_ref[...])))
    state = jnp.zeros((MODES, CHANNELS), F32)
    for q in range(CHUNKS):
        part = chunk_lanes(ends, q)
        states_ref[0, :, q * CHANNELS : (q + 1) * CHANNELS] = part
        state = chunk_decay * state + part
    back = jnp.zeros((MODES, CHANNELS), F32)
    for q in reversed(range(CHUNKS)):
        part = one_step * chunk_lanes(leads, q)
        states_ref[1, :, q * CHANNELS : (q + 1) * CHANNELS] = part
        back = chunk_decay * back + part
    ends_ref[0] = state
    ends_ref[1] = back


def scaled_columns(value):
    largest = jnp.max(jnp.abs(value), axis=0, keepdims=True)
    exponent = jnp.ceil(jnp.log2(jnp.maximum(largest, 1e-30))) - 15.0
    return value * jnp.exp2(-exponent), exponent


def patch_kernel(before_ref, weight_ref, head_ref, power_ref, ends_ref,
                 patch_ref, delta_ref, send_ref, ext_ref):
    feature = []
    for i in range(3):
        ext_ref[0:LEAD, :] = before_ref[i].astype(F32)
        ext_ref[LEAD:, :] = jnp.zeros((HEAD, CHANNELS), F32)
        total = head_ref[i]
        for j in range(1, KW):
            total = total + weight_ref[i, j : j + 1, :] * ext_ref[pl.ds(LEAD - j, HEAD), :]
        feature.append(total)
    gi = feature[1] * feature[2]
    gl = head_ref[3] * feature[0]
    for at, value in enumerate((feature[1], feature[2], gi, gl)):
        patch_ref[at] = value
    state_part, back_part = None, None
    for r in range(HEAD):
        ahead = power_ref[0, r] * gi[r : r + 1, :]
        behind = power_ref[1, r] * gl[r : r + 1, :]
        state_part = ahead if r == 0 else state_part + ahead
        back_part = behind if r == 0 else back_part + behind
    delta_ref[0] = state_part
    delta_ref[1] = back_part
    state = ends_ref[0] + power_ref[2, 0] * state_part
    back = ends_ref[1] + back_part
    for at, value in enumerate((back, state)):
        scaled, exponent = scaled_columns(value)
        send_ref[at, 0:MODES, :] = scaled
        send_ref[at, MODES:, :] = jnp.broadcast_to(exponent, (8, CHANNELS))


def spliced(wide_ref, patch):
    top = jnp.concatenate([patch, wide_ref[0:HEAD, CHANNELS:]], axis=1)
    return jnp.concatenate([top, wide_ref[HEAD:, :]], axis=0)


def middle_kernel(me_ref, table_ref, pair_ref, states_ref, patch_ref, delta_ref,
                  near_ref, halves_ref, lag_ref):
    long_ref, gated_ref, small_ref = near_parts(near_ref)
    gi_ref, gl_ref = pair_ref.at[0], pair_ref.at[1]
    rates = table_ref[0]
    row = mode_row(rates)
    column = mode_column(row)
    lag = iota((CHANNELS, CHUNK), 1)
    back_lag = lax.rem(CHUNK - lag, CHUNK)
    ascending = jnp.exp(-column * lag.astype(F32))
    descending = jnp.exp(-column * (CHUNK - 1 - lag).astype(F32))
    turned = jnp.exp(-column * back_lag.astype(F32))
    residue_row = mode_row(table_ref[1]) * lane_group(GROUPS)
    filters = lax.dot_general(residue_row, ascending, MM, precision=EXACT, preferred_element_type=F32)
    turned_filters = lax.dot_general(residue_row, turned, MM, precision=EXACT, preferred_element_type=F32)
    gi = split(spliced(gi_ref, patch_ref[2]))
    gl = split(spliced(gl_ref, patch_ref[3]))
    down = iota((CHUNK, CHUNK), 0)
    across = iota((CHUNK, CHUNK), 1)
    mirror = (down + across == CHUNK - 1).astype(F32).astype(BF16)
    mirrored = [
        lax.dot_general(mirror, part, MM, preferred_element_type=F32).astype(BF16) for part in gl
    ]
    wide_group = (iota((1, ROWS), 1) % CHANNELS) // WIDTH
    lane_of = iota((CHUNK, CHANNELS), 1) // WIDTH
    for g in range(GROUPS):
        straight = jnp.broadcast_to(turned_filters[g : g + 1, :], (CHUNK, CHUNK))
        straight = pltpu.roll(straight, 0, 1, stride=1, stride_axis=0)
        straight = split(jnp.where(across <= down, straight, 0.0))
        flipped = jnp.broadcast_to(filters[g : g + 1, :], (CHUNK, CHUNK))
        flipped = pltpu.roll(flipped, 0, 1, stride=1, stride_axis=0)
        flipped = split(jnp.where(across >= down, flipped, 0.0))
        forward = dot3(straight, gi)
        backward = dot3(flipped, gl)
        for q in range(CHUNKS):
            rows = pl.ds(q * CHUNK, CHUNK)
            if g == 0:
                long_ref[rows, :] = chunk_lanes(forward, q)
                gated_ref[rows, :] = chunk_lanes(backward, q)
            else:
                long_ref[rows, :] = jnp.where(lane_of == g, chunk_lanes(forward, q), long_ref[rows, :])
                gated_ref[rows, :] = jnp.where(lane_of == g, chunk_lanes(backward, q), gated_ref[rows, :])
        own = (wide_group == g).astype(F32).astype(BF16)
        products = dot3((mirrored[0] * own, mirrored[1] * own), gi, NT)
        products = jnp.where(across + down <= CHUNK - 1, products, 0.0)
        sheared = pltpu.roll(products, 1, 1, stride=1, stride_axis=0)
        lag_ref[g : g + 1, :] = jnp.sum(sheared, axis=0, keepdims=True)
    lag_grad = lag_ref[...]
    down_lag = lax.rem(CHUNK - down, CHUNK).astype(F32)
    powers = jnp.exp(-row * down_lag)
    residue_sums = lax.dot_general(lag_grad, powers, MM, precision=EXACT, preferred_element_type=F32)
    moment_sums = lax.dot_general(lag_grad, powers * down_lag, MM, precision=EXACT, preferred_element_type=F32)
    own_group = lane_group(GROUPS)
    small_ref[LOCAL + 2 : LOCAL + 3, :] = -row * mode_row(table_ref[1])
    small_ref[LOCAL : LOCAL + 1, :] = jnp.sum(residue_sums * own_group, axis=0, keepdims=True)
    small_ref[LOCAL + 1 : LOCAL + 2, :] = jnp.sum(moment_sums * own_group, axis=0, keepdims=True)
    small_rates = mode_compact(rates)
    small_residues = mode_compact(table_ref[1])
    chunk_decay = jnp.exp(-small_rates * CHUNK)
    lag_value = lag.astype(F32)
    end_moments = compact(dot3(split(descending * (CHUNK - 1 - lag_value)), gi))
    lead_moments = compact(dot3(split(ascending * (jnp.exp(-column) * (lag_value + 1.0))), gl))
    zero = jnp.zeros((MODES, CHANNELS), F32)
    leads = []
    state, moment = zero, zero
    residue_part, moment_part, lead_moment = zero, zero, zero
    offset_decay = jnp.ones((MODES, CHANNELS), F32)
    for q in range(CHUNKS):
        lead = chunk_lanes(states_ref[1], q)
        end = chunk_lanes(states_ref[0], q)
        if q == 0:
            end, lead = end + delta_ref[0], lead + delta_ref[1]
        leads.append(lead)
        lead_here = chunk_lanes(lead_moments, q)
        small_ref[piece(q), :] = small_residues * state
        residue_part = residue_part + lead * state
        moment_part = moment_part + lead_here * state + lead * moment
        lead_moment = lead_moment + offset_decay * (lead_here + float(q * CHUNK) * lead)
        offset_decay = offset_decay * chunk_decay
        moment = chunk_decay * (moment + float(CHUNK) * state) + chunk_lanes(end_moments, q)
        state = chunk_decay * state + end
    back = zero
    for q in reversed(range(CHUNKS)):
        small_ref[piece(CHUNKS + q), :] = small_residues * back
        back = chunk_decay * back + leads[q]
    for at, value in enumerate((residue_part, moment_part, lead_moment, moment, back)):
        small_ref[piece(2 * CHUNKS + at), :] = value
    factor = small_residues
    for q in range(CHUNKS):
        small_ref[piece(FACTOR + q), :] = factor
        factor = factor * chunk_decay
    count = small_ref.shape[0] // MODES - POWER
    for at in range(count):
        away = jnp.maximum(jnp.abs(me_ref[0] - member(at, count)) - 1, 0).astype(F32) * float(ROWS)
        small_ref[piece(POWER + at), :] = jnp.exp(-small_rates * away)
    steps = down.astype(F32)
    halves_ref[0], halves_ref[1] = split(jnp.exp(-row * (steps + 1.0)))
    halves_ref[2], halves_ref[3] = split(jnp.exp(-row * (CHUNK - 1 - steps)))


def finish_kernel(me_ref, arrived_ref, near_ref, halves_ref,
                  kv_ref, patch_ref, out_grad_ref, proj_ref, before_ref, feature_ref, stats_ref, ext_ref):
    for i in range(3):
        ext_ref[i, 0:LEAD, :] = before_ref[i].astype(F32)
        ext_ref[i, LEAD:, :] = proj_ref[i].astype(F32)
    long_ref, gated_ref, small_ref = near_parts(near_ref)
    me = me_ref[0]
    zero = jnp.zeros((MODES, CHANNELS), F32)
    state_in, late_in, back_in = zero, zero, zero
    for at in range(arrived_ref.shape[0]):
        d = member(at, arrived_ref.shape[0])
        away = (jnp.abs(me - d) - 1).astype(F32) * float(ROWS)
        scale = jnp.exp2(arrived_ref[at, MODES : MODES + 1, :])
        term = small_ref[piece(POWER + at), :] * (arrived_ref[at, 0:MODES, :] * scale)
        state_in = state_in + jnp.where(d < me, term, 0.0)
        late_in = late_in + jnp.where(d < me, term * away, 0.0)
        back_in = back_in + jnp.where(d > me, term, 0.0)
    states, backs = [], []
    for q in range(CHUNKS):
        states.append(small_ref[piece(q), :] + small_ref[piece(FACTOR + q), :] * state_in)
        backs.append(small_ref[piece(CHUNKS + q), :] + small_ref[piece(FACTOR + CHUNKS - 1 - q), :] * back_in)
    long_far = dot3((halves_ref[0], halves_ref[1]), expand(jnp.concatenate(states, axis=1)))
    gated_far = dot3((halves_ref[2], halves_ref[3]), expand(jnp.concatenate(backs, axis=1)))
    sums = [jnp.zeros((8, CHANNELS), F32) for _ in range(3 * KW)]
    for q in range(CHUNKS):
        rows = pl.ds(q * CHUNK, CHUNK)
        signal = out_grad_ref[rows, :].astype(F32)
        grad_gated = gated_ref[rows, :] + chunk_lanes(gated_far, q)
        keyed, valued = kv_ref[0, rows, :], kv_ref[1, rows, :]
        if q == 0:
            keyed = jnp.concatenate([patch_ref[0], keyed[HEAD:, :]], axis=0)
            valued = jnp.concatenate([patch_ref[1], valued[HEAD:, :]], axis=0)
        parts = (
            signal * (long_ref[rows, :] + chunk_lanes(long_far, q)),
            grad_gated * valued,
            grad_gated * keyed,
        )
        for i in range(3):
            feature_ref[i, rows, :] = parts[i]
            for j in range(KW):
                product = parts[i] * ext_ref[i, pl.ds(LEAD - j + q * CHUNK, CHUNK), :]
                sums[i * KW + j] = sums[i * KW + j] + jnp.sum(
                    product.reshape(CHUNK // 8, 8, CHANNELS), axis=0
                )
    residue_part, moment_part, lead_moment, end_moment, lead = (
        small_ref[piece(2 * CHUNKS + at), :] for at in range(5)
    )
    residue_part = residue_part + lead * state_in
    moment_part = moment_part + lead_moment * state_in + lead * late_in + end_moment * back_in
    same = (iota((CHANNELS, CHANNELS), 0) // WIDTH == iota((CHANNELS, CHANNELS), 1) // MODES).astype(F32)
    pick = (iota((MODES, CHANNELS), 1) % MODES == iota((MODES, CHANNELS), 0)).astype(F32)

    def by_mode(part):
        spread = lax.dot_general(part, same, MM, precision=EXACT, preferred_element_type=F32)
        return jnp.sum(spread * pick, axis=0, keepdims=True)

    residue_row = small_ref[LOCAL : LOCAL + 1, :] + by_mode(residue_part)
    moment_row = small_ref[LOCAL + 1 : LOCAL + 2, :] + by_mode(moment_part)
    rate_row = small_ref[LOCAL + 2 : LOCAL + 3, :] * moment_row
    lines = [jnp.sum(part, axis=0, keepdims=True) for part in sums]
    stats = jnp.concatenate(lines + [residue_row, rate_row, jnp.zeros((1, CHANNELS), F32)], axis=0)
    scaled, exponent = scaled_columns(stats)
    last = iota((STATS, CHANNELS), 0) == STATS - 1
    stats_ref[...] = jnp.where(last, exponent, scaled)


def inputs_kernel(feature_ref, after_ref, weight_ref, total_ref, out_ref, table_ref, ext_ref):
    pick = (iota((MODES, CHANNELS), 1) % MODES == iota((MODES, CHANNELS), 0)).astype(F32)
    for at in range(2):
        line = total_ref[3 * KW + at : 3 * KW + at + 1, :] * lane_group(GROUPS)
        table_ref[at] = lax.dot_general(line, pick, NT, precision=EXACT, preferred_element_type=F32)
    for i in range(3):
        ext_ref[0:ROWS, :] = feature_ref[i]
        ext_ref[ROWS:, :] = after_ref[i]
        for q in range(CHUNKS):
            total = None
            for j in range(KW):
                term = weight_ref[i, j : j + 1, :] * ext_ref[pl.ds(j + q * CHUNK, CHUNK), :]
                total = term if total is None else total + term
            out_ref[i, pl.ds(q * CHUNK, CHUNK), :] = total.astype(BF16)


def total_kernel(stats_ref, total_ref, square_ref):
    total = jnp.zeros((STATS, CHANNELS), F32)
    for d in range(stats_ref.shape[0]):
        total = total + stats_ref[d] * jnp.exp2(stats_ref[d, STATS - 1 :, :])
    total = jnp.where(iota((STATS, CHANNELS), 0) == STATS - 1, 0.0, total)
    total_ref[...] = total
    square = jnp.sum(total * total, axis=0, keepdims=True)
    for d in range(square_ref.shape[0]):
        square_ref[d] = jnp.broadcast_to(square, square_ref.shape[1:])


def scale_kernel(square_ref, total_ref, table_ref, conv_ref, residue_ref, rate_ref):
    squares = jnp.sum(jnp.sum(square_ref[:, 0, :], axis=0, keepdims=True), axis=1, keepdims=True)
    factor = jnp.minimum(1.0, lax.rsqrt(squares / (3 * KW * D + 2 * G * MODES) + 1e-6))
    for i in range(3):
        conv_ref[i] = total_ref[i * KW : (i + 1) * KW, :] * factor
    residue_ref[...] = table_ref[0] * factor
    rate_ref[...] = table_ref[1] * factor


def shape(*dims, dtype=F32):
    return jax.ShapeDtypeStruct(dims, dtype)


VMEM = pl.BlockSpec(memory_space=pltpu.VMEM)
SMEM = pl.BlockSpec(memory_space=pltpu.SMEM)


HBM = pl.BlockSpec(memory_space=pltpu.HBM)


def call(kernel, name, out_shape, specs, cost_us, scratch=()):
    return pl.pallas_call(
        kernel,
        out_shape=out_shape,
        in_specs=specs,
        out_specs=jax.tree.map(lambda _: VMEM, out_shape),
        scratch_shapes=list(scratch),
        compiler_params=pltpu.CompilerParams(vmem_limit_bytes=12 * 2**20),
        cost_estimate=pl.CostEstimate(
            flops=int(cost_us * 1e9), bytes_accessed=int(cost_us * 3e6), transcendentals=0
        ),
        name=name,
    )


def exchange(blocks, axis, first):
    count = blocks.shape[0]
    return lax.all_to_all(blocks, axis, 0, 0, axis_index_groups=[[(first + p) % count for p in range(count)]])


def shards(projected, conv_weight, residues, decay_rates, grad_out):
    ctx = lax.axis_size("ctx")
    planes = lax.axis_size("ch")
    me = lax.axis_index("ctx").astype(jnp.int32).reshape(1)
    before = lax.ppermute(
        projected[:, ROWS - LEAD :, :], "ctx", [(source, source + 1) for source in range(ctx - 1)]
    )
    kv, pair, states, ends, head, powers, table = call(
        prepare_kernel, "prepare",
        (shape(2, ROWS, CHANNELS), shape(2, CHUNK, CHUNKS * CHANNELS), shape(2, MODES, CHUNKS * CHANNELS),
         shape(2, MODES, CHANNELS), shape(4, HEAD, CHANNELS), shape(3, HEAD, MODES, CHANNELS),
         shape(2, GROUPS, MODES)),
        [VMEM] * 3 + [HBM] * 2, 3,
        scratch=[pltpu.VMEM((3, ROWS, CHANNELS), BF16), pltpu.VMEM((ROWS, CHANNELS), BF16),
                 pltpu.VMEM((3, LEAD + ROWS, CHANNELS), F32), pltpu.SemaphoreType.DMA((2,))],
    )(conv_weight, decay_rates, residues,
      *(pltpu.with_memory_space_constraint(part, pltpu.HBM) for part in (projected, grad_out)))
    patch, delta, send = call(
        patch_kernel, "patch",
        (shape(4, HEAD, CHANNELS), shape(2, MODES, CHANNELS), shape(2, MODES + 8, CHANNELS)),
        [VMEM] * 5, 1,
        scratch=[pltpu.VMEM((LEAD + HEAD, CHANNELS), F32)],
    )(before, conv_weight, head, powers, ends)
    later = member(lax.broadcasted_iota(jnp.int32, (ctx, 1, 1), 0), ctx) > me.reshape(1, 1, 1)
    send = jnp.where(later, send[1], send[0]).astype(F16)
    arrived = exchange(send, "ctx", ctx // 2).astype(F32)
    near, halves = call(
        middle_kernel, "within",
        (shape(2 * ROWS + (POWER + ctx) * MODES, CHANNELS), shape(4, CHUNK, CHANNELS, dtype=BF16)),
        [SMEM] + [VMEM] * 5, 8,
        scratch=[pltpu.VMEM((GROUPS, CHANNELS), F32)],
    )(me, table, pair, states, patch, delta)
    grad_feature, stats = call(
        finish_kernel, "across",
        (shape(3, ROWS, CHANNELS), shape(STATS, CHANNELS)),
        [SMEM] + [VMEM] * 8, 4,
        scratch=[pltpu.VMEM((3, LEAD + ROWS, CHANNELS), F32)],
    )(me, arrived, near, halves, kv, patch, grad_out, projected, before)
    after = lax.ppermute(
        grad_feature[:, :8, :], "ctx", [(source + 1, source) for source in range(ctx - 1)]
    )
    stats = jnp.broadcast_to(stats.astype(F16), (ctx, STATS, CHANNELS))
    gathered = exchange(stats, "ctx", ctx // 2 - 1).astype(F32)
    total, square = call(
        total_kernel, "total", (shape(STATS, CHANNELS), shape(planes, 1, CHANNELS)), [VMEM], 1,
    )(gathered)
    squares = exchange(square, "ch", planes // 2 + planes // 8)
    grad_projected, table = call(
        inputs_kernel, "inputs",
        (shape(3, ROWS, CHANNELS, dtype=BF16), shape(2, GROUPS, MODES)), [VMEM] * 4, 2,
        scratch=[pltpu.VMEM((ROWS + 8, CHANNELS), F32)],
    )(grad_feature, after, conv_weight, total)
    grad_conv, grad_residues, grad_log_rates = call(
        scale_kernel, "scale",
        (shape(3, KW, CHANNELS), shape(GROUPS, MODES), shape(GROUPS, MODES)), [VMEM] * 3, 1,
    )(squares, total, table)
    return grad_projected, grad_conv, grad_residues, grad_log_rates


def solution(mesh):
    in_specs = (
        P(None, "ctx", "ch"),
        P(None, None, "ch"),
        P("ch", None),
        P("ch", None),
        P("ctx", "ch"),
    )
    out_specs = (P(None, "ctx", "ch"), P(None, None, "ch"), P("ch", None), P("ch", None))
    return jax.shard_map(shards, mesh=mesh, in_specs=in_specs, out_specs=out_specs, check_vma=False)
```

```python
import jax
import jax.numpy as jnp
from jax import lax
from jax.experimental import pallas as pl
from jax.experimental.pallas import tpu as pltpu
from jax.sharding import PartitionSpec as P

D = 4096
G = 256
MODES = 16
KW = 7

ROWS = 512
CHANNELS = 128
GROUPS = 8
WIDTH = 16
CHUNK = 128
CHUNKS = ROWS // CHUNK
LEAD = 16
HEAD = 8
STATS = 24
FACTOR = 2 * CHUNKS + 5
LOCAL = (FACTOR + CHUNKS) * MODES
POWER = FACTOR + CHUNKS + 1

F32 = jnp.float32
BF16 = jnp.bfloat16
F16 = jnp.float16
EXACT = lax.Precision.HIGHEST
MM = (((1,), (0,)), ((), ()))
NT = (((1,), (1,)), ((), ()))


def split(value):
    high = value.astype(BF16)
    low = (value - high.astype(F32)).astype(BF16)
    return high, low


def dot3(left, right, dims=MM):
    lh, ll = left
    rh, rl = right

    def product(a, b):
        return lax.dot_general(a, b, dims, preferred_element_type=F32)

    return product(lh, rh) + (product(lh, rl) + product(ll, rh))


def iota(shape, axis):
    return lax.broadcasted_iota(jnp.int32, shape, axis)


def lane_group(rows):
    return (iota((rows, CHANNELS), 1) // WIDTH == iota((rows, CHANNELS), 0)).astype(F32)


def mode_row(table):
    pick = (iota((MODES, CHANNELS), 1) % MODES == iota((MODES, CHANNELS), 0)).astype(F32)
    spread = lax.dot_general(table, pick, MM, precision=EXACT, preferred_element_type=F32)
    return jnp.sum(spread * lane_group(GROUPS), axis=0, keepdims=True)


def mode_column(row):
    eye = iota((CHANNELS, CHANNELS), 0) == iota((CHANNELS, CHANNELS), 1)
    return jnp.sum(jnp.where(eye, row, 0.0), axis=1, keepdims=True)


def mode_compact(table):
    return lax.dot_general(
        table, lane_group(GROUPS), (((0,), (0,)), ((), ())), precision=EXACT, preferred_element_type=F32
    )


def compact(full):
    lanes = full.shape[1]
    total = None
    for g in range(GROUPS):
        own = (iota((MODES, lanes), 1) % CHANNELS) // WIDTH == g
        part = jnp.where(own, full[g * MODES : (g + 1) * MODES, :], 0.0)
        total = part if total is None else total + part
    return total


def expand(small):
    lanes = small.shape[1]
    own = (iota((CHANNELS, lanes), 0) // MODES == (iota((CHANNELS, lanes), 1) % CHANNELS) // WIDTH).astype(F32)
    return split(jnp.concatenate([small] * GROUPS, axis=0) * own)


def near_parts(near_ref):
    return near_ref.at[0:ROWS, :], near_ref.at[ROWS : 2 * ROWS, :], near_ref.at[2 * ROWS :, :]


def member(position, count):
    return (position + count // 2) % count


def piece(at):
    return slice(at * MODES, (at + 1) * MODES)


def chunk_lanes(value, q):
    return value[:, q * CHANNELS : (q + 1) * CHANNELS]


def prepare_kernel(weight_ref, rate_ref, residue_ref, proj_ref, out_grad_ref,
                   kv_ref, pair_ref, states_ref, ends_ref, head_ref, power_ref, table_ref,
                   raw_ref, signal_ref, ext_ref, sem_ref):
    gi_ref, gl_ref = pair_ref.at[0], pair_ref.at[1]
    copies = [
        pltpu.make_async_copy(proj_ref, raw_ref, sem_ref.at[0]),
        pltpu.make_async_copy(out_grad_ref, signal_ref, sem_ref.at[1]),
    ]
    for copy in copies:
        copy.start()
    rates = rate_ref[...]
    table_ref[0] = rates
    table_ref[1] = residue_ref[...]
    column = mode_column(mode_row(rates))
    lag = iota((CHANNELS, CHUNK), 1).astype(F32)
    ascending = split(jnp.exp(-column * lag))
    descending = split(jnp.exp(-column * (CHUNK - 1 - lag)))
    small_rates = mode_compact(rates)
    one_step = jnp.exp(-small_rates)
    chunk_decay = jnp.exp(-small_rates * CHUNK)
    for r in range(HEAD):
        power_ref[0, r] = jnp.exp(-small_rates * float(CHUNK - 1 - r))
        power_ref[1, r] = jnp.exp(-small_rates * float(r + 1))
    power_ref[2, 0] = jnp.exp(-small_rates * float(ROWS - CHUNK))
    for r in range(1, HEAD):
        power_ref[2, r] = jnp.zeros((MODES, CHANNELS), F32)
    for copy in copies:
        copy.wait()
    for i in range(3):
        ext_ref[i, 0:LEAD, :] = jnp.zeros((LEAD, CHANNELS), F32)
        ext_ref[i, LEAD:, :] = raw_ref[i].astype(F32)
    blank = jnp.zeros((HEAD, CHANNELS), F32)
    for q in range(CHUNKS):
        feature = []
        for i in range(3):
            total = None
            for j in range(KW):
                term = weight_ref[i, j : j + 1, :] * ext_ref[i, pl.ds(LEAD - j + q * CHUNK, CHUNK), :]
                total = term if total is None else total + term
            feature.append(total)
        rows = pl.ds(q * CHUNK, CHUNK)
        lanes = slice(q * CHANNELS, (q + 1) * CHANNELS)
        signal = signal_ref[rows, :].astype(F32)
        kv_ref[0, rows, :] = feature[1]
        kv_ref[1, rows, :] = feature[2]
        gi_ref[:, lanes] = feature[1] * feature[2]
        gl_ref[:, lanes] = signal * feature[0]
        if q == 0:
            for i in range(3):
                head_ref[i] = feature[i][0:HEAD, :]
            head_ref[3] = signal[0:HEAD, :]
            gi_ref[0:HEAD, lanes] = blank
            gl_ref[0:HEAD, lanes] = blank
    ends = compact(dot3(descending, split(gi_ref[...])))
    leads = compact(dot3(ascending, split(gl_ref[...])))
    state = jnp.zeros((MODES, CHANNELS), F32)
    for q in range(CHUNKS):
        part = chunk_lanes(ends, q)
        states_ref[0, :, q * CHANNELS : (q + 1) * CHANNELS] = part
        state = chunk_decay * state + part
    back = jnp.zeros((MODES, CHANNELS), F32)
    for q in reversed(range(CHUNKS)):
        part = one_step * chunk_lanes(leads, q)
        states_ref[1, :, q * CHANNELS : (q + 1) * CHANNELS] = part
        back = chunk_decay * back + part
    ends_ref[0] = state
    ends_ref[1] = back


def scaled_columns(value):
    largest = jnp.max(jnp.abs(value), axis=0, keepdims=True)
    exponent = jnp.ceil(jnp.log2(jnp.maximum(largest, 1e-30))) - 15.0
    return value * jnp.exp2(-exponent), exponent


def patch_kernel(before_ref, weight_ref, head_ref, power_ref, ends_ref,
                 patch_ref, delta_ref, send_ref, ext_ref):
    feature = []
    for i in range(3):
        ext_ref[0:LEAD, :] = before_ref[i].astype(F32)
        ext_ref[LEAD:, :] = jnp.zeros((HEAD, CHANNELS), F32)
        total = head_ref[i]
        for j in range(1, KW):
            total = total + weight_ref[i, j : j + 1, :] * ext_ref[pl.ds(LEAD - j, HEAD), :]
        feature.append(total)
    gi = feature[1] * feature[2]
    gl = head_ref[3] * feature[0]
    for at, value in enumerate((feature[1], feature[2], gi, gl)):
        patch_ref[at] = value
    state_part, back_part = None, None
    for r in range(HEAD):
        ahead = power_ref[0, r] * gi[r : r + 1, :]
        behind = power_ref[1, r] * gl[r : r + 1, :]
        state_part = ahead if r == 0 else state_part + ahead
        back_part = behind if r == 0 else back_part + behind
    delta_ref[0] = state_part
    delta_ref[1] = back_part
    state = ends_ref[0] + power_ref[2, 0] * state_part
    back = ends_ref[1] + back_part
    for at, value in enumerate((back, state)):
        scaled, exponent = scaled_columns(value)
        send_ref[at, 0:MODES, :] = scaled
        send_ref[at, MODES:, :] = jnp.broadcast_to(exponent, (8, CHANNELS))


def spliced(wide_ref, patch):
    top = jnp.concatenate([patch, wide_ref[0:HEAD, CHANNELS:]], axis=1)
    return jnp.concatenate([top, wide_ref[HEAD:, :]], axis=0)


def middle_kernel(me_ref, table_ref, pair_ref, states_ref, patch_ref, delta_ref,
                  near_ref, halves_ref, lag_ref):
    long_ref, gated_ref, small_ref = near_parts(near_ref)
    gi_ref, gl_ref = pair_ref.at[0], pair_ref.at[1]
    rates = table_ref[0]
    row = mode_row(rates)
    column = mode_column(row)
    lag = iota((CHANNELS, CHUNK), 1)
    back_lag = lax.rem(CHUNK - lag, CHUNK)
    ascending = jnp.exp(-column * lag.astype(F32))
    descending = jnp.exp(-column * (CHUNK - 1 - lag).astype(F32))
    turned = jnp.exp(-column * back_lag.astype(F32))
    residue_row = mode_row(table_ref[1]) * lane_group(GROUPS)
    filters = lax.dot_general(residue_row, ascending, MM, precision=EXACT, preferred_element_type=F32)
    turned_filters = lax.dot_general(residue_row, turned, MM, precision=EXACT, preferred_element_type=F32)
    gi = split(spliced(gi_ref, patch_ref[2]))
    gl = split(spliced(gl_ref, patch_ref[3]))
    down = iota((CHUNK, CHUNK), 0)
    across = iota((CHUNK, CHUNK), 1)
    mirror = (down + across == CHUNK - 1).astype(F32).astype(BF16)
    mirrored = [
        lax.dot_general(mirror, part, MM, preferred_element_type=F32).astype(BF16) for part in gl
    ]
    wide_group = (iota((1, ROWS), 1) % CHANNELS) // WIDTH
    lane_of = iota((CHUNK, CHANNELS), 1) // WIDTH
    for g in range(GROUPS):
        straight = jnp.broadcast_to(turned_filters[g : g + 1, :], (CHUNK, CHUNK))
        straight = pltpu.roll(straight, 0, 1, stride=1, stride_axis=0)
        straight = split(jnp.where(across <= down, straight, 0.0))
        flipped = jnp.broadcast_to(filters[g : g + 1, :], (CHUNK, CHUNK))
        flipped = pltpu.roll(flipped, 0, 1, stride=1, stride_axis=0)
        flipped = split(jnp.where(across >= down, flipped, 0.0))
        forward = dot3(straight, gi)
        backward = dot3(flipped, gl)
        for q in range(CHUNKS):
            rows = pl.ds(q * CHUNK, CHUNK)
            if g == 0:
                long_ref[rows, :] = chunk_lanes(forward, q)
                gated_ref[rows, :] = chunk_lanes(backward, q)
            else:
                long_ref[rows, :] = jnp.where(lane_of == g, chunk_lanes(forward, q), long_ref[rows, :])
                gated_ref[rows, :] = jnp.where(lane_of == g, chunk_lanes(backward, q), gated_ref[rows, :])
        own = (wide_group == g).astype(F32).astype(BF16)
        products = dot3((mirrored[0] * own, mirrored[1] * own), gi, NT)
        products = jnp.where(across + down <= CHUNK - 1, products, 0.0)
        sheared = pltpu.roll(products, 1, 1, stride=1, stride_axis=0)
        lag_ref[g : g + 1, :] = jnp.sum(sheared, axis=0, keepdims=True)
    lag_grad = lag_ref[...]
    down_lag = lax.rem(CHUNK - down, CHUNK).astype(F32)
    powers = jnp.exp(-row * down_lag)
    residue_sums = lax.dot_general(lag_grad, powers, MM, precision=EXACT, preferred_element_type=F32)
    moment_sums = lax.dot_general(lag_grad, powers * down_lag, MM, precision=EXACT, preferred_element_type=F32)
    own_group = lane_group(GROUPS)
    small_ref[LOCAL + 2 : LOCAL + 3, :] = -row * mode_row(table_ref[1])
    small_ref[LOCAL : LOCAL + 1, :] = jnp.sum(residue_sums * own_group, axis=0, keepdims=True)
    small_ref[LOCAL + 1 : LOCAL + 2, :] = jnp.sum(moment_sums * own_group, axis=0, keepdims=True)
    small_rates = mode_compact(rates)
    small_residues = mode_compact(table_ref[1])
    chunk_decay = jnp.exp(-small_rates * CHUNK)
    lag_value = lag.astype(F32)
    end_moments = compact(dot3(split(descending * (CHUNK - 1 - lag_value)), gi))
    lead_moments = compact(dot3(split(ascending * (jnp.exp(-column) * (lag_value + 1.0))), gl))
    zero = jnp.zeros((MODES, CHANNELS), F32)
    leads = []
    state, moment = zero, zero
    residue_part, moment_part, lead_moment = zero, zero, zero
    offset_decay = jnp.ones((MODES, CHANNELS), F32)
    for q in range(CHUNKS):
        lead = chunk_lanes(states_ref[1], q)
        end = chunk_lanes(states_ref[0], q)
        if q == 0:
            end, lead = end + delta_ref[0], lead + delta_ref[1]
        leads.append(lead)
        lead_here = chunk_lanes(lead_moments, q)
        small_ref[piece(q), :] = small_residues * state
        residue_part = residue_part + lead * state
        moment_part = moment_part + lead_here * state + lead * moment
        lead_moment = lead_moment + offset_decay * (lead_here + float(q * CHUNK) * lead)
        offset_decay = offset_decay * chunk_decay
        moment = chunk_decay * (moment + float(CHUNK) * state) + chunk_lanes(end_moments, q)
        state = chunk_decay * state + end
    back = zero
    for q in reversed(range(CHUNKS)):
        small_ref[piece(CHUNKS + q), :] = small_residues * back
        back = chunk_decay * back + leads[q]
    for at, value in enumerate((residue_part, moment_part, lead_moment, moment, back)):
        small_ref[piece(2 * CHUNKS + at), :] = value
    factor = small_residues
    for q in range(CHUNKS):
        small_ref[piece(FACTOR + q), :] = factor
        factor = factor * chunk_decay
    count = small_ref.shape[0] // MODES - POWER
    for at in range(count):
        away = jnp.maximum(jnp.abs(me_ref[0] - member(at, count)) - 1, 0).astype(F32) * float(ROWS)
        small_ref[piece(POWER + at), :] = jnp.exp(-small_rates * away)
    steps = down.astype(F32)
    halves_ref[0], halves_ref[1] = split(jnp.exp(-row * (steps + 1.0)))
    halves_ref[2], halves_ref[3] = split(jnp.exp(-row * (CHUNK - 1 - steps)))


def finish_kernel(me_ref, arrived_ref, near_ref, halves_ref,
                  kv_ref, patch_ref, out_grad_ref, proj_ref, before_ref, feature_ref, stats_ref, ext_ref):
    for i in range(3):
        ext_ref[i, 0:LEAD, :] = before_ref[i].astype(F32)
        ext_ref[i, LEAD:, :] = proj_ref[i].astype(F32)
    long_ref, gated_ref, small_ref = near_parts(near_ref)
    me = me_ref[0]
    zero = jnp.zeros((MODES, CHANNELS), F32)
    state_in, late_in, back_in = zero, zero, zero
    for at in range(arrived_ref.shape[0]):
        d = member(at, arrived_ref.shape[0])
        away = (jnp.abs(me - d) - 1).astype(F32) * float(ROWS)
        scale = jnp.exp2(arrived_ref[at, MODES : MODES + 1, :])
        term = small_ref[piece(POWER + at), :] * (arrived_ref[at, 0:MODES, :] * scale)
        state_in = state_in + jnp.where(d < me, term, 0.0)
        late_in = late_in + jnp.where(d < me, term * away, 0.0)
        back_in = back_in + jnp.where(d > me, term, 0.0)
    states, backs = [], []
    for q in range(CHUNKS):
        states.append(small_ref[piece(q), :] + small_ref[piece(FACTOR + q), :] * state_in)
        backs.append(small_ref[piece(CHUNKS + q), :] + small_ref[piece(FACTOR + CHUNKS - 1 - q), :] * back_in)
    long_far = dot3((halves_ref[0], halves_ref[1]), expand(jnp.concatenate(states, axis=1)))
    gated_far = dot3((halves_ref[2], halves_ref[3]), expand(jnp.concatenate(backs, axis=1)))
    sums = [jnp.zeros((8, CHANNELS), F32) for _ in range(3 * KW)]
    for q in range(CHUNKS):
        rows = pl.ds(q * CHUNK, CHUNK)
        signal = out_grad_ref[rows, :].astype(F32)
        grad_gated = gated_ref[rows, :] + chunk_lanes(gated_far, q)
        keyed, valued = kv_ref[0, rows, :], kv_ref[1, rows, :]
        if q == 0:
            keyed = jnp.concatenate([patch_ref[0], keyed[HEAD:, :]], axis=0)
            valued = jnp.concatenate([patch_ref[1], valued[HEAD:, :]], axis=0)
        parts = (
            signal * (long_ref[rows, :] + chunk_lanes(long_far, q)),
            grad_gated * valued,
            grad_gated * keyed,
        )
        for i in range(3):
            feature_ref[i, rows, :] = parts[i]
            for j in range(KW):
                product = parts[i] * ext_ref[i, pl.ds(LEAD - j + q * CHUNK, CHUNK), :]
                sums[i * KW + j] = sums[i * KW + j] + jnp.sum(
                    product.reshape(CHUNK // 8, 8, CHANNELS), axis=0
                )
    residue_part, moment_part, lead_moment, end_moment, lead = (
        small_ref[piece(2 * CHUNKS + at), :] for at in range(5)
    )
    residue_part = residue_part + lead * state_in
    moment_part = moment_part + lead_moment * state_in + lead * late_in + end_moment * back_in
    same = (iota((CHANNELS, CHANNELS), 0) // WIDTH == iota((CHANNELS, CHANNELS), 1) // MODES).astype(F32)
    pick = (iota((MODES, CHANNELS), 1) % MODES == iota((MODES, CHANNELS), 0)).astype(F32)

    def by_mode(part):
        spread = lax.dot_general(part, same, MM, precision=EXACT, preferred_element_type=F32)
        return jnp.sum(spread * pick, axis=0, keepdims=True)

    residue_row = small_ref[LOCAL : LOCAL + 1, :] + by_mode(residue_part)
    moment_row = small_ref[LOCAL + 1 : LOCAL + 2, :] + by_mode(moment_part)
    rate_row = small_ref[LOCAL + 2 : LOCAL + 3, :] * moment_row
    lines = [jnp.sum(part, axis=0, keepdims=True) for part in sums]
    stats = jnp.concatenate(lines + [residue_row, rate_row, jnp.zeros((1, CHANNELS), F32)], axis=0)
    scaled, exponent = scaled_columns(stats)
    last = iota((STATS, CHANNELS), 0) == STATS - 1
    stats_ref[...] = jnp.where(last, exponent, scaled)


def inputs_kernel(feature_ref, after_ref, weight_ref, total_ref, out_ref, table_ref, ext_ref):
    pick = (iota((MODES, CHANNELS), 1) % MODES == iota((MODES, CHANNELS), 0)).astype(F32)
    for at in range(2):
        line = total_ref[3 * KW + at : 3 * KW + at + 1, :] * lane_group(GROUPS)
        table_ref[at] = lax.dot_general(line, pick, NT, precision=EXACT, preferred_element_type=F32)
    for i in range(3):
        ext_ref[0:ROWS, :] = feature_ref[i]
        ext_ref[ROWS:, :] = after_ref[i]
        for q in range(CHUNKS):
            total = None
            for j in range(KW):
                term = weight_ref[i, j : j + 1, :] * ext_ref[pl.ds(j + q * CHUNK, CHUNK), :]
                total = term if total is None else total + term
            out_ref[i, pl.ds(q * CHUNK, CHUNK), :] = total.astype(BF16)


def total_kernel(stats_ref, total_ref, square_ref):
    total = jnp.zeros((STATS, CHANNELS), F32)
    for d in range(stats_ref.shape[0]):
        total = total + stats_ref[d] * jnp.exp2(stats_ref[d, STATS - 1 :, :])
    total = jnp.where(iota((STATS, CHANNELS), 0) == STATS - 1, 0.0, total)
    total_ref[...] = total
    square = jnp.sum(total * total, axis=0, keepdims=True)
    for d in range(square_ref.shape[0]):
        square_ref[d] = jnp.broadcast_to(square, square_ref.shape[1:])


def scale_kernel(square_ref, total_ref, table_ref, conv_ref, residue_ref, rate_ref):
    squares = jnp.sum(jnp.sum(square_ref[:, 0, :], axis=0, keepdims=True), axis=1, keepdims=True)
    factor = jnp.minimum(1.0, lax.rsqrt(squares / (3 * KW * D + 2 * G * MODES) + 1e-6))
    for i in range(3):
        conv_ref[i] = total_ref[i * KW : (i + 1) * KW, :] * factor
    residue_ref[...] = table_ref[0] * factor
    rate_ref[...] = table_ref[1] * factor


def shape(*dims, dtype=F32):
    return jax.ShapeDtypeStruct(dims, dtype)


VMEM = pl.BlockSpec(memory_space=pltpu.VMEM)
SMEM = pl.BlockSpec(memory_space=pltpu.SMEM)


HBM = pl.BlockSpec(memory_space=pltpu.HBM)


def call(kernel, name, out_shape, specs, cost_us, scratch=()):
    return pl.pallas_call(
        kernel,
        out_shape=out_shape,
        in_specs=specs,
        out_specs=jax.tree.map(lambda _: VMEM, out_shape),
        scratch_shapes=list(scratch),
        compiler_params=pltpu.CompilerParams(vmem_limit_bytes=12 * 2**20),
        cost_estimate=pl.CostEstimate(
            flops=int(cost_us * 1e9), bytes_accessed=int(cost_us * 3e6), transcendentals=0
        ),
        name=name,
    )


def exchange(blocks, axis, first):
    count = blocks.shape[0]
    return lax.all_to_all(blocks, axis, 0, 0, axis_index_groups=[[(first + p) % count for p in range(count)]])


def shards(projected, conv_weight, residues, decay_rates, grad_out):
    ctx = lax.axis_size("ctx")
    planes = lax.axis_size("ch")
    me = lax.axis_index("ctx").astype(jnp.int32).reshape(1)
    before = lax.ppermute(
        projected[:, ROWS - LEAD :, :], "ctx", [(source, source + 1) for source in range(ctx - 1)]
    )
    kv, pair, states, ends, head, powers, table = call(
        prepare_kernel, "prepare",
        (shape(2, ROWS, CHANNELS), shape(2, CHUNK, CHUNKS * CHANNELS), shape(2, MODES, CHUNKS * CHANNELS),
         shape(2, MODES, CHANNELS), shape(4, HEAD, CHANNELS), shape(3, HEAD, MODES, CHANNELS),
         shape(2, GROUPS, MODES)),
        [VMEM] * 3 + [HBM] * 2, 3,
        scratch=[pltpu.VMEM((3, ROWS, CHANNELS), BF16), pltpu.VMEM((ROWS, CHANNELS), BF16),
                 pltpu.VMEM((3, LEAD + ROWS, CHANNELS), F32), pltpu.SemaphoreType.DMA((2,))],
    )(conv_weight, decay_rates, residues,
      *(pltpu.with_memory_space_constraint(part, pltpu.HBM) for part in (projected, grad_out)))
    patch, delta, send = call(
        patch_kernel, "patch",
        (shape(4, HEAD, CHANNELS), shape(2, MODES, CHANNELS), shape(2, MODES + 8, CHANNELS)),
        [VMEM] * 5, 1,
        scratch=[pltpu.VMEM((LEAD + HEAD, CHANNELS), F32)],
    )(before, conv_weight, head, powers, ends)
    later = member(lax.broadcasted_iota(jnp.int32, (ctx, 1, 1), 0), ctx) > me.reshape(1, 1, 1)
    send = jnp.where(later, send[1], send[0]).astype(F16)
    arrived = exchange(send, "ctx", ctx // 2).astype(F32)
    near, halves = call(
        middle_kernel, "within",
        (shape(2 * ROWS + (POWER + ctx) * MODES, CHANNELS), shape(4, CHUNK, CHANNELS, dtype=BF16)),
        [SMEM] + [VMEM] * 5, 8,
        scratch=[pltpu.VMEM((GROUPS, CHANNELS), F32)],
    )(me, table, pair, states, patch, delta)
    grad_feature, stats = call(
        finish_kernel, "across",
        (shape(3, ROWS, CHANNELS), shape(STATS, CHANNELS)),
        [SMEM] + [VMEM] * 8, 4,
        scratch=[pltpu.VMEM((3, LEAD + ROWS, CHANNELS), F32)],
    )(me, arrived, near, halves, kv, patch, grad_out, projected, before)
    after = lax.ppermute(
        grad_feature[:, :8, :], "ctx", [(source + 1, source) for source in range(ctx - 1)]
    )
    stats = jnp.broadcast_to(stats.astype(F16), (ctx, STATS, CHANNELS))
    gathered = exchange(stats, "ctx", ctx // 2).astype(F32)
    total, square = call(
        total_kernel, "total", (shape(STATS, CHANNELS), shape(planes, 1, CHANNELS)), [VMEM], 1,
    )(gathered)
    squares = exchange(square, "ch", planes // 2 + planes // 8)
    grad_projected, table = call(
        inputs_kernel, "inputs",
        (shape(3, ROWS, CHANNELS, dtype=BF16), shape(2, GROUPS, MODES)), [VMEM] * 4, 2,
        scratch=[pltpu.VMEM((ROWS + 8, CHANNELS), F32)],
    )(grad_feature, after, conv_weight, total)
    grad_conv, grad_residues, grad_log_rates = call(
        scale_kernel, "scale",
        (shape(3, KW, CHANNELS), shape(GROUPS, MODES), shape(GROUPS, MODES)), [VMEM] * 3, 1,
    )(squares, total, table)
    return grad_projected, grad_conv, grad_residues, grad_log_rates


def solution(mesh):
    in_specs = (
        P(None, "ctx", "ch"),
        P(None, None, "ch"),
        P("ch", None),
        P("ch", None),
        P("ctx", "ch"),
    )
    out_specs = (P(None, "ctx", "ch"), P(None, None, "ch"), P("ch", None), P("ch", None))
    return jax.shard_map(shards, mesh=mesh, in_specs=in_specs, out_specs=out_specs, check_vma=False)
```

```python
import jax
import jax.numpy as jnp
from jax import lax
from jax.experimental import pallas as pl
from jax.experimental.pallas import tpu as pltpu
from jax.sharding import PartitionSpec as P

D = 4096
G = 256
MODES = 16
KW = 7

ROWS = 512
CHANNELS = 128
GROUPS = 8
WIDTH = 16
CHUNK = 128
CHUNKS = ROWS // CHUNK
LEAD = 16
HEAD = 8
STATS = 24
FACTOR = 2 * CHUNKS + 5
LOCAL = (FACTOR + CHUNKS) * MODES
POWER = FACTOR + CHUNKS + 1

F32 = jnp.float32
BF16 = jnp.bfloat16
F16 = jnp.float16
EXACT = lax.Precision.HIGHEST
MM = (((1,), (0,)), ((), ()))
NT = (((1,), (1,)), ((), ()))


def split(value):
    high = value.astype(BF16)
    low = (value - high.astype(F32)).astype(BF16)
    return high, low


def dot3(left, right, dims=MM):
    lh, ll = left
    rh, rl = right

    def product(a, b):
        return lax.dot_general(a, b, dims, preferred_element_type=F32)

    return product(lh, rh) + (product(lh, rl) + product(ll, rh))


def iota(shape, axis):
    return lax.broadcasted_iota(jnp.int32, shape, axis)


def lane_group(rows):
    return (iota((rows, CHANNELS), 1) // WIDTH == iota((rows, CHANNELS), 0)).astype(F32)


def mode_row(table):
    pick = (iota((MODES, CHANNELS), 1) % MODES == iota((MODES, CHANNELS), 0)).astype(F32)
    spread = lax.dot_general(table, pick, MM, precision=EXACT, preferred_element_type=F32)
    return jnp.sum(spread * lane_group(GROUPS), axis=0, keepdims=True)


def mode_column(row):
    eye = iota((CHANNELS, CHANNELS), 0) == iota((CHANNELS, CHANNELS), 1)
    return jnp.sum(jnp.where(eye, row, 0.0), axis=1, keepdims=True)


def mode_compact(table):
    return lax.dot_general(
        table, lane_group(GROUPS), (((0,), (0,)), ((), ())), precision=EXACT, preferred_element_type=F32
    )


def compact(full):
    lanes = full.shape[1]
    total = None
    for g in range(GROUPS):
        own = (iota((MODES, lanes), 1) % CHANNELS) // WIDTH == g
        part = jnp.where(own, full[g * MODES : (g + 1) * MODES, :], 0.0)
        total = part if total is None else total + part
    return total


def expand(small):
    lanes = small.shape[1]
    own = (iota((CHANNELS, lanes), 0) // MODES == (iota((CHANNELS, lanes), 1) % CHANNELS) // WIDTH).astype(F32)
    return split(jnp.concatenate([small] * GROUPS, axis=0) * own)


def near_parts(near_ref):
    return near_ref.at[0:ROWS, :], near_ref.at[ROWS : 2 * ROWS, :], near_ref.at[2 * ROWS :, :]


def member(position, count):
    return (position + count // 2) % count


def piece(at):
    return slice(at * MODES, (at + 1) * MODES)


def chunk_lanes(value, q):
    return value[:, q * CHANNELS : (q + 1) * CHANNELS]


def prepare_kernel(weight_ref, rate_ref, residue_ref, proj_ref, out_grad_ref,
                   kv_ref, pair_ref, states_ref, ends_ref, head_ref, power_ref, table_ref,
                   raw_ref, signal_ref, ext_ref, sem_ref):
    gi_ref, gl_ref = pair_ref.at[0], pair_ref.at[1]
    copies = [
        pltpu.make_async_copy(proj_ref, raw_ref, sem_ref.at[0]),
        pltpu.make_async_copy(out_grad_ref, signal_ref, sem_ref.at[1]),
    ]
    for copy in copies:
        copy.start()
    rates = rate_ref[...]
    table_ref[0] = rates
    table_ref[1] = residue_ref[...]
    column = mode_column(mode_row(rates))
    lag = iota((CHANNELS, CHUNK), 1).astype(F32)
    ascending = split(jnp.exp(-column * lag))
    descending = split(jnp.exp(-column * (CHUNK - 1 - lag)))
    small_rates = mode_compact(rates)
    one_step = jnp.exp(-small_rates)
    chunk_decay = jnp.exp(-small_rates * CHUNK)
    for r in range(HEAD):
        power_ref[0, r] = jnp.exp(-small_rates * float(CHUNK - 1 - r))
        power_ref[1, r] = jnp.exp(-small_rates * float(r + 1))
    power_ref[2, 0] = jnp.exp(-small_rates * float(ROWS - CHUNK))
    for r in range(1, HEAD):
        power_ref[2, r] = jnp.zeros((MODES, CHANNELS), F32)
    for copy in copies:
        copy.wait()
    for i in range(3):
        ext_ref[i, 0:LEAD, :] = jnp.zeros((LEAD, CHANNELS), F32)
        ext_ref[i, LEAD:, :] = raw_ref[i].astype(F32)
    blank = jnp.zeros((HEAD, CHANNELS), F32)
    for q in range(CHUNKS):
        feature = []
        for i in range(3):
            total = None
            for j in range(KW):
                term = weight_ref[i, j : j + 1, :] * ext_ref[i, pl.ds(LEAD - j + q * CHUNK, CHUNK), :]
                total = term if total is None else total + term
            feature.append(total)
        rows = pl.ds(q * CHUNK, CHUNK)
        lanes = slice(q * CHANNELS, (q + 1) * CHANNELS)
        signal = signal_ref[rows, :].astype(F32)
        kv_ref[0, rows, :] = feature[1]
        kv_ref[1, rows, :] = feature[2]
        gi_ref[:, lanes] = feature[1] * feature[2]
        gl_ref[:, lanes] = signal * feature[0]
        if q == 0:
            for i in range(3):
                head_ref[i] = feature[i][0:HEAD, :]
            head_ref[3] = signal[0:HEAD, :]
            gi_ref[0:HEAD, lanes] = blank
            gl_ref[0:HEAD, lanes] = blank
    ends = compact(dot3(descending, split(gi_ref[...])))
    leads = compact(dot3(ascending, split(gl_ref[...])))
    state = jnp.zeros((MODES, CHANNELS), F32)
    for q in range(CHUNKS):
        part = chunk_lanes(ends, q)
        states_ref[0, :, q * CHANNELS : (q + 1) * CHANNELS] = part
        state = chunk_decay * state + part
    back = jnp.zeros((MODES, CHANNELS), F32)
    for q in reversed(range(CHUNKS)):
        part = one_step * chunk_lanes(leads, q)
        states_ref[1, :, q * CHANNELS : (q + 1) * CHANNELS] = part
        back = chunk_decay * back + part
    ends_ref[0] = state
    ends_ref[1] = back


def scaled_columns(value):
    largest = jnp.max(jnp.abs(value), axis=0, keepdims=True)
    exponent = jnp.ceil(jnp.log2(jnp.maximum(largest, 1e-30))) - 15.0
    return value * jnp.exp2(-exponent), exponent


def patch_kernel(before_ref, weight_ref, head_ref, power_ref, ends_ref,
                 patch_ref, delta_ref, send_ref, ext_ref):
    feature = []
    for i in range(3):
        ext_ref[0:LEAD, :] = before_ref[i].astype(F32)
        ext_ref[LEAD:, :] = jnp.zeros((HEAD, CHANNELS), F32)
        total = head_ref[i]
        for j in range(1, KW):
            total = total + weight_ref[i, j : j + 1, :] * ext_ref[pl.ds(LEAD - j, HEAD), :]
        feature.append(total)
    gi = feature[1] * feature[2]
    gl = head_ref[3] * feature[0]
    for at, value in enumerate((feature[1], feature[2], gi, gl)):
        patch_ref[at] = value
    state_part, back_part = None, None
    for r in range(HEAD):
        ahead = power_ref[0, r] * gi[r : r + 1, :]
        behind = power_ref[1, r] * gl[r : r + 1, :]
        state_part = ahead if r == 0 else state_part + ahead
        back_part = behind if r == 0 else back_part + behind
    delta_ref[0] = state_part
    delta_ref[1] = back_part
    state = ends_ref[0] + power_ref[2, 0] * state_part
    back = ends_ref[1] + back_part
    for at, value in enumerate((back, state)):
        scaled, exponent = scaled_columns(value)
        send_ref[at, 0:MODES, :] = scaled
        send_ref[at, MODES:, :] = jnp.broadcast_to(exponent, (8, CHANNELS))


def spliced(wide_ref, patch):
    top = jnp.concatenate([patch, wide_ref[0:HEAD, CHANNELS:]], axis=1)
    return jnp.concatenate([top, wide_ref[HEAD:, :]], axis=0)


def middle_kernel(me_ref, table_ref, pair_ref, states_ref, patch_ref, delta_ref,
                  near_ref, halves_ref, lag_ref):
    long_ref, gated_ref, small_ref = near_parts(near_ref)
    gi_ref, gl_ref = pair_ref.at[0], pair_ref.at[1]
    rates = table_ref[0]
    row = mode_row(rates)
    column = mode_column(row)
    lag = iota((CHANNELS, CHUNK), 1)
    back_lag = lax.rem(CHUNK - lag, CHUNK)
    ascending = jnp.exp(-column * lag.astype(F32))
    descending = jnp.exp(-column * (CHUNK - 1 - lag).astype(F32))
    turned = jnp.exp(-column * back_lag.astype(F32))
    residue_row = mode_row(table_ref[1]) * lane_group(GROUPS)
    filters = lax.dot_general(residue_row, ascending, MM, precision=EXACT, preferred_element_type=F32)
    turned_filters = lax.dot_general(residue_row, turned, MM, precision=EXACT, preferred_element_type=F32)
    gi = split(spliced(gi_ref, patch_ref[2]))
    gl = split(spliced(gl_ref, patch_ref[3]))
    down = iota((CHUNK, CHUNK), 0)
    across = iota((CHUNK, CHUNK), 1)
    mirror = (down + across == CHUNK - 1).astype(F32).astype(BF16)
    mirrored = [
        lax.dot_general(mirror, part, MM, preferred_element_type=F32).astype(BF16) for part in gl
    ]
    wide_group = (iota((1, ROWS), 1) % CHANNELS) // WIDTH
    lane_of = iota((CHUNK, CHANNELS), 1) // WIDTH
    for g in range(GROUPS):
        straight = jnp.broadcast_to(turned_filters[g : g + 1, :], (CHUNK, CHUNK))
        straight = pltpu.roll(straight, 0, 1, stride=1, stride_axis=0)
        straight = split(jnp.where(across <= down, straight, 0.0))
        flipped = jnp.broadcast_to(filters[g : g + 1, :], (CHUNK, CHUNK))
        flipped = pltpu.roll(flipped, 0, 1, stride=1, stride_axis=0)
        flipped = split(jnp.where(across >= down, flipped, 0.0))
        forward = dot3(straight, gi)
        backward = dot3(flipped, gl)
        for q in range(CHUNKS):
            rows = pl.ds(q * CHUNK, CHUNK)
            if g == 0:
                long_ref[rows, :] = chunk_lanes(forward, q)
                gated_ref[rows, :] = chunk_lanes(backward, q)
            else:
                long_ref[rows, :] = jnp.where(lane_of == g, chunk_lanes(forward, q), long_ref[rows, :])
                gated_ref[rows, :] = jnp.where(lane_of == g, chunk_lanes(backward, q), gated_ref[rows, :])
        own = (wide_group == g).astype(F32).astype(BF16)
        products = dot3((mirrored[0] * own, mirrored[1] * own), gi, NT)
        products = jnp.where(across + down <= CHUNK - 1, products, 0.0)
        sheared = pltpu.roll(products, 1, 1, stride=1, stride_axis=0)
        lag_ref[g : g + 1, :] = jnp.sum(sheared, axis=0, keepdims=True)
    lag_grad = lag_ref[...]
    down_lag = lax.rem(CHUNK - down, CHUNK).astype(F32)
    powers = jnp.exp(-row * down_lag)
    residue_sums = lax.dot_general(lag_grad, powers, MM, precision=EXACT, preferred_element_type=F32)
    moment_sums = lax.dot_general(lag_grad, powers * down_lag, MM, precision=EXACT, preferred_element_type=F32)
    own_group = lane_group(GROUPS)
    small_ref[LOCAL + 2 : LOCAL + 3, :] = -row * mode_row(table_ref[1])
    small_ref[LOCAL : LOCAL + 1, :] = jnp.sum(residue_sums * own_group, axis=0, keepdims=True)
    small_ref[LOCAL + 1 : LOCAL + 2, :] = jnp.sum(moment_sums * own_group, axis=0, keepdims=True)
    small_rates = mode_compact(rates)
    small_residues = mode_compact(table_ref[1])
    chunk_decay = jnp.exp(-small_rates * CHUNK)
    lag_value = lag.astype(F32)
    end_moments = compact(dot3(split(descending * (CHUNK - 1 - lag_value)), gi))
    lead_moments = compact(dot3(split(ascending * (jnp.exp(-column) * (lag_value + 1.0))), gl))
    zero = jnp.zeros((MODES, CHANNELS), F32)
    leads = []
    state, moment = zero, zero
    residue_part, moment_part, lead_moment = zero, zero, zero
    offset_decay = jnp.ones((MODES, CHANNELS), F32)
    for q in range(CHUNKS):
        lead = chunk_lanes(states_ref[1], q)
        end = chunk_lanes(states_ref[0], q)
        if q == 0:
            end, lead = end + delta_ref[0], lead + delta_ref[1]
        leads.append(lead)
        lead_here = chunk_lanes(lead_moments, q)
        small_ref[piece(q), :] = small_residues * state
        residue_part = residue_part + lead * state
        moment_part = moment_part + lead_here * state + lead * moment
        lead_moment = lead_moment + offset_decay * (lead_here + float(q * CHUNK) * lead)
        offset_decay = offset_decay * chunk_decay
        moment = chunk_decay * (moment + float(CHUNK) * state) + chunk_lanes(end_moments, q)
        state = chunk_decay * state + end
    back = zero
    for q in reversed(range(CHUNKS)):
        small_ref[piece(CHUNKS + q), :] = small_residues * back
        back = chunk_decay * back + leads[q]
    for at, value in enumerate((residue_part, moment_part, lead_moment, moment, back)):
        small_ref[piece(2 * CHUNKS + at), :] = value
    factor = small_residues
    for q in range(CHUNKS):
        small_ref[piece(FACTOR + q), :] = factor
        factor = factor * chunk_decay
    count = small_ref.shape[0] // MODES - POWER
    for at in range(count):
        away = jnp.maximum(jnp.abs(me_ref[0] - member(at, count)) - 1, 0).astype(F32) * float(ROWS)
        small_ref[piece(POWER + at), :] = jnp.exp(-small_rates * away)
    steps = down.astype(F32)
    halves_ref[0], halves_ref[1] = split(jnp.exp(-row * (steps + 1.0)))
    halves_ref[2], halves_ref[3] = split(jnp.exp(-row * (CHUNK - 1 - steps)))


def finish_kernel(me_ref, arrived_ref, near_ref, halves_ref,
                  kv_ref, patch_ref, out_grad_ref, proj_ref, before_ref, feature_ref, stats_ref, ext_ref):
    for i in range(3):
        ext_ref[i, 0:LEAD, :] = before_ref[i].astype(F32)
        ext_ref[i, LEAD:, :] = proj_ref[i].astype(F32)
    long_ref, gated_ref, small_ref = near_parts(near_ref)
    me = me_ref[0]
    zero = jnp.zeros((MODES, CHANNELS), F32)
    state_in, late_in, back_in = zero, zero, zero
    for at in range(arrived_ref.shape[0]):
        d = member(at, arrived_ref.shape[0])
        away = (jnp.abs(me - d) - 1).astype(F32) * float(ROWS)
        scale = jnp.exp2(arrived_ref[at, MODES : MODES + 1, :])
        term = small_ref[piece(POWER + at), :] * (arrived_ref[at, 0:MODES, :] * scale)
        state_in = state_in + jnp.where(d < me, term, 0.0)
        late_in = late_in + jnp.where(d < me, term * away, 0.0)
        back_in = back_in + jnp.where(d > me, term, 0.0)
    states, backs = [], []
    for q in range(CHUNKS):
        states.append(small_ref[piece(q), :] + small_ref[piece(FACTOR + q), :] * state_in)
        backs.append(small_ref[piece(CHUNKS + q), :] + small_ref[piece(FACTOR + CHUNKS - 1 - q), :] * back_in)
    long_far = dot3((halves_ref[0], halves_ref[1]), expand(jnp.concatenate(states, axis=1)))
    gated_far = dot3((halves_ref[2], halves_ref[3]), expand(jnp.concatenate(backs, axis=1)))
    sums = [jnp.zeros((8, CHANNELS), F32) for _ in range(3 * KW)]
    for q in range(CHUNKS):
        rows = pl.ds(q * CHUNK, CHUNK)
        signal = out_grad_ref[rows, :].astype(F32)
        grad_gated = gated_ref[rows, :] + chunk_lanes(gated_far, q)
        keyed, valued = kv_ref[0, rows, :], kv_ref[1, rows, :]
        if q == 0:
            keyed = jnp.concatenate([patch_ref[0], keyed[HEAD:, :]], axis=0)
            valued = jnp.concatenate([patch_ref[1], valued[HEAD:, :]], axis=0)
        parts = (
            signal * (long_ref[rows, :] + chunk_lanes(long_far, q)),
            grad_gated * valued,
            grad_gated * keyed,
        )
        for i in range(3):
            feature_ref[i, rows, :] = parts[i]
            for j in range(KW):
                product = parts[i] * ext_ref[i, pl.ds(LEAD - j + q * CHUNK, CHUNK), :]
                sums[i * KW + j] = sums[i * KW + j] + jnp.sum(
                    product.reshape(CHUNK // 8, 8, CHANNELS), axis=0
                )
    residue_part, moment_part, lead_moment, end_moment, lead = (
        small_ref[piece(2 * CHUNKS + at), :] for at in range(5)
    )
    residue_part = residue_part + lead * state_in
    moment_part = moment_part + lead_moment * state_in + lead * late_in + end_moment * back_in
    same = (iota((CHANNELS, CHANNELS), 0) // WIDTH == iota((CHANNELS, CHANNELS), 1) // MODES).astype(F32)
    pick = (iota((MODES, CHANNELS), 1) % MODES == iota((MODES, CHANNELS), 0)).astype(F32)

    def by_mode(part):
        spread = lax.dot_general(part, same, MM, precision=EXACT, preferred_element_type=F32)
        return jnp.sum(spread * pick, axis=0, keepdims=True)

    residue_row = small_ref[LOCAL : LOCAL + 1, :] + by_mode(residue_part)
    moment_row = small_ref[LOCAL + 1 : LOCAL + 2, :] + by_mode(moment_part)
    rate_row = small_ref[LOCAL + 2 : LOCAL + 3, :] * moment_row
    lines = [jnp.sum(part, axis=0, keepdims=True) for part in sums]
    stats = jnp.concatenate(lines + [residue_row, rate_row, jnp.zeros((1, CHANNELS), F32)], axis=0)
    scaled, exponent = scaled_columns(stats)
    last = iota((STATS, CHANNELS), 0) == STATS - 1
    stats_ref[...] = jnp.where(last, exponent, scaled)


def inputs_kernel(feature_ref, after_ref, weight_ref, total_ref, out_ref, table_ref, ext_ref):
    pick = (iota((MODES, CHANNELS), 1) % MODES == iota((MODES, CHANNELS), 0)).astype(F32)
    for at in range(2):
        line = total_ref[3 * KW + at : 3 * KW + at + 1, :] * lane_group(GROUPS)
        table_ref[at] = lax.dot_general(line, pick, NT, precision=EXACT, preferred_element_type=F32)
    for i in range(3):
        ext_ref[0:ROWS, :] = feature_ref[i]
        ext_ref[ROWS:, :] = after_ref[i]
        for q in range(CHUNKS):
            total = None
            for j in range(KW):
                term = weight_ref[i, j : j + 1, :] * ext_ref[pl.ds(j + q * CHUNK, CHUNK), :]
                total = term if total is None else total + term
            out_ref[i, pl.ds(q * CHUNK, CHUNK), :] = total.astype(BF16)


def total_kernel(stats_ref, total_ref, square_ref):
    total = jnp.zeros((STATS, CHANNELS), F32)
    for d in range(stats_ref.shape[0]):
        total = total + stats_ref[d] * jnp.exp2(stats_ref[d, STATS - 1 :, :])
    total = jnp.where(iota((STATS, CHANNELS), 0) == STATS - 1, 0.0, total)
    total_ref[...] = total
    square = jnp.sum(total * total, axis=0, keepdims=True)
    for d in range(square_ref.shape[0]):
        square_ref[d] = jnp.broadcast_to(square, square_ref.shape[1:])


def scale_kernel(square_ref, total_ref, table_ref, conv_ref, residue_ref, rate_ref):
    squares = jnp.sum(jnp.sum(square_ref[:, 0, :], axis=0, keepdims=True), axis=1, keepdims=True)
    factor = jnp.minimum(1.0, lax.rsqrt(squares / (3 * KW * D + 2 * G * MODES) + 1e-6))
    for i in range(3):
        conv_ref[i] = total_ref[i * KW : (i + 1) * KW, :] * factor
    residue_ref[...] = table_ref[0] * factor
    rate_ref[...] = table_ref[1] * factor


def shape(*dims, dtype=F32):
    return jax.ShapeDtypeStruct(dims, dtype)


VMEM = pl.BlockSpec(memory_space=pltpu.VMEM)
SMEM = pl.BlockSpec(memory_space=pltpu.SMEM)


HBM = pl.BlockSpec(memory_space=pltpu.HBM)


def call(kernel, name, out_shape, specs, cost_us, scratch=()):
    return pl.pallas_call(
        kernel,
        out_shape=out_shape,
        in_specs=specs,
        out_specs=jax.tree.map(lambda _: VMEM, out_shape),
        scratch_shapes=list(scratch),
        compiler_params=pltpu.CompilerParams(vmem_limit_bytes=12 * 2**20),
        cost_estimate=pl.CostEstimate(
            flops=int(cost_us * 1e9), bytes_accessed=int(cost_us * 3e6), transcendentals=0
        ),
        name=name,
    )


def exchange(blocks, axis, first):
    count = blocks.shape[0]
    return lax.all_to_all(blocks, axis, 0, 0, axis_index_groups=[[(first + p) % count for p in range(count)]])


def shards(projected, conv_weight, residues, decay_rates, grad_out):
    ctx = lax.axis_size("ctx")
    planes = lax.axis_size("ch")
    me = lax.axis_index("ctx").astype(jnp.int32).reshape(1)
    before = lax.ppermute(
        projected[:, ROWS - LEAD :, :], "ctx", [(source, source + 1) for source in range(ctx - 1)]
    )
    kv, pair, states, ends, head, powers, table = call(
        prepare_kernel, "prepare",
        (shape(2, ROWS, CHANNELS), shape(2, CHUNK, CHUNKS * CHANNELS), shape(2, MODES, CHUNKS * CHANNELS),
         shape(2, MODES, CHANNELS), shape(4, HEAD, CHANNELS), shape(3, HEAD, MODES, CHANNELS),
         shape(2, GROUPS, MODES)),
        [VMEM] * 3 + [HBM] * 2, 3,
        scratch=[pltpu.VMEM((3, ROWS, CHANNELS), BF16), pltpu.VMEM((ROWS, CHANNELS), BF16),
                 pltpu.VMEM((3, LEAD + ROWS, CHANNELS), F32), pltpu.SemaphoreType.DMA((2,))],
    )(conv_weight, decay_rates, residues,
      *(pltpu.with_memory_space_constraint(part, pltpu.HBM) for part in (projected, grad_out)))
    patch, delta, send = call(
        patch_kernel, "patch",
        (shape(4, HEAD, CHANNELS), shape(2, MODES, CHANNELS), shape(2, MODES + 8, CHANNELS)),
        [VMEM] * 5, 1,
        scratch=[pltpu.VMEM((LEAD + HEAD, CHANNELS), F32)],
    )(before, conv_weight, head, powers, ends)
    later = member(lax.broadcasted_iota(jnp.int32, (ctx, 1, 1), 0), ctx) > me.reshape(1, 1, 1)
    send = send[:, : MODES + 2, :].reshape(2, MODES // 2 + 1, 2, CHANNELS)
    send = jnp.where(later[..., None], send[1], send[0]).astype(F16)
    arrived = exchange(send, "ctx", ctx // 2).astype(F32).reshape(ctx, MODES + 2, CHANNELS)
    near, halves = call(
        middle_kernel, "within",
        (shape(2 * ROWS + (POWER + ctx) * MODES, CHANNELS), shape(4, CHUNK, CHANNELS, dtype=BF16)),
        [SMEM] + [VMEM] * 5, 8,
        scratch=[pltpu.VMEM((GROUPS, CHANNELS), F32)],
    )(me, table, pair, states, patch, delta)
    grad_feature, stats = call(
        finish_kernel, "across",
        (shape(3, ROWS, CHANNELS), shape(STATS, CHANNELS)),
        [SMEM] + [VMEM] * 8, 4,
        scratch=[pltpu.VMEM((3, LEAD + ROWS, CHANNELS), F32)],
    )(me, arrived, near, halves, kv, patch, grad_out, projected, before)
    after = lax.ppermute(
        grad_feature[:, :8, :], "ctx", [(source + 1, source) for source in range(ctx - 1)]
    )
    stats = jnp.broadcast_to(stats.astype(F16), (ctx, STATS, CHANNELS))
    gathered = exchange(stats, "ctx", ctx // 2).astype(F32)
    total, square = call(
        total_kernel, "total", (shape(STATS, CHANNELS), shape(planes, 1, CHANNELS)), [VMEM], 1,
    )(gathered)
    squares = exchange(square, "ch", planes // 2 + planes // 8)
    grad_projected, table = call(
        inputs_kernel, "inputs",
        (shape(3, ROWS, CHANNELS, dtype=BF16), shape(2, GROUPS, MODES)), [VMEM] * 4, 2,
        scratch=[pltpu.VMEM((ROWS + 8, CHANNELS), F32)],
    )(grad_feature, after, conv_weight, total)
    grad_conv, grad_residues, grad_log_rates = call(
        scale_kernel, "scale",
        (shape(3, KW, CHANNELS), shape(GROUPS, MODES), shape(GROUPS, MODES)), [VMEM] * 3, 1,
    )(squares, total, table)
    return grad_projected, grad_conv, grad_residues, grad_log_rates


def solution(mesh):
    in_specs = (
        P(None, "ctx", "ch"),
        P(None, None, "ch"),
        P("ch", None),
        P("ch", None),
        P("ctx", "ch"),
    )
    out_specs = (P(None, "ctx", "ch"), P(None, None, "ch"), P("ch", None), P("ch", None))
    return jax.shard_map(shards, mesh=mesh, in_specs=in_specs, out_specs=out_specs, check_vma=False)
```

```python
import jax
import jax.numpy as jnp
from jax import lax
from jax.experimental import pallas as pl
from jax.experimental.pallas import tpu as pltpu
from jax.sharding import PartitionSpec as P

D = 4096
G = 256
MODES = 16
KW = 7

ROWS = 512
CHANNELS = 128
GROUPS = 8
WIDTH = 16
CHUNK = 128
CHUNKS = ROWS // CHUNK
LEAD = 16
HEAD = 8
STATS = 24
FACTOR = 2 * CHUNKS + 5
LOCAL = (FACTOR + CHUNKS) * MODES
POWER = FACTOR + CHUNKS + 1

F32 = jnp.float32
BF16 = jnp.bfloat16
F16 = jnp.float16
EXACT = lax.Precision.HIGHEST
MM = (((1,), (0,)), ((), ()))
NT = (((1,), (1,)), ((), ()))


def split(value):
    high = value.astype(BF16)
    low = (value - high.astype(F32)).astype(BF16)
    return high, low


def dot3(left, right, dims=MM):
    lh, ll = left
    rh, rl = right

    def product(a, b):
        return lax.dot_general(a, b, dims, preferred_element_type=F32)

    return product(lh, rh) + (product(lh, rl) + product(ll, rh))


def iota(shape, axis):
    return lax.broadcasted_iota(jnp.int32, shape, axis)


def lane_group(rows):
    return (iota((rows, CHANNELS), 1) // WIDTH == iota((rows, CHANNELS), 0)).astype(F32)


def mode_row(table):
    pick = (iota((MODES, CHANNELS), 1) % MODES == iota((MODES, CHANNELS), 0)).astype(F32)
    spread = lax.dot_general(table, pick, MM, precision=EXACT, preferred_element_type=F32)
    return jnp.sum(spread * lane_group(GROUPS), axis=0, keepdims=True)


def mode_column(row):
    eye = iota((CHANNELS, CHANNELS), 0) == iota((CHANNELS, CHANNELS), 1)
    return jnp.sum(jnp.where(eye, row, 0.0), axis=1, keepdims=True)


def mode_compact(table):
    return lax.dot_general(
        table, lane_group(GROUPS), (((0,), (0,)), ((), ())), precision=EXACT, preferred_element_type=F32
    )


def compact(full):
    lanes = full.shape[1]
    total = None
    for g in range(GROUPS):
        own = (iota((MODES, lanes), 1) % CHANNELS) // WIDTH == g
        part = jnp.where(own, full[g * MODES : (g + 1) * MODES, :], 0.0)
        total = part if total is None else total + part
    return total


def expand(small):
    lanes = small.shape[1]
    own = (iota((CHANNELS, lanes), 0) // MODES == (iota((CHANNELS, lanes), 1) % CHANNELS) // WIDTH).astype(F32)
    return split(jnp.concatenate([small] * GROUPS, axis=0) * own)


def near_parts(near_ref):
    return near_ref.at[0:ROWS, :], near_ref.at[ROWS : 2 * ROWS, :], near_ref.at[2 * ROWS :, :]


def member(position, count):
    return (position + count // 2) % count


def piece(at):
    return slice(at * MODES, (at + 1) * MODES)


def chunk_lanes(value, q):
    return value[:, q * CHANNELS : (q + 1) * CHANNELS]


def prepare_kernel(weight_ref, rate_ref, residue_ref, proj_ref, out_grad_ref,
                   kv_ref, pair_ref, states_ref, ends_ref, head_ref, power_ref, table_ref,
                   raw_ref, signal_ref, ext_ref, sem_ref):
    gi_ref, gl_ref = pair_ref.at[0], pair_ref.at[1]
    copies = [
        pltpu.make_async_copy(proj_ref, raw_ref, sem_ref.at[0]),
        pltpu.make_async_copy(out_grad_ref, signal_ref, sem_ref.at[1]),
    ]
    for copy in copies:
        copy.start()
    rates = rate_ref[...]
    table_ref[0] = rates
    table_ref[1] = residue_ref[...]
    column = mode_column(mode_row(rates))
    lag = iota((CHANNELS, CHUNK), 1).astype(F32)
    ascending = split(jnp.exp(-column * lag))
    descending = split(jnp.exp(-column * (CHUNK - 1 - lag)))
    small_rates = mode_compact(rates)
    one_step = jnp.exp(-small_rates)
    chunk_decay = jnp.exp(-small_rates * CHUNK)
    for r in range(HEAD):
        power_ref[0, r] = jnp.exp(-small_rates * float(CHUNK - 1 - r))
        power_ref[1, r] = jnp.exp(-small_rates * float(r + 1))
    power_ref[2, 0] = jnp.exp(-small_rates * float(ROWS - CHUNK))
    for r in range(1, HEAD):
        power_ref[2, r] = jnp.zeros((MODES, CHANNELS), F32)
    for copy in copies:
        copy.wait()
    for i in range(3):
        ext_ref[i, 0:LEAD, :] = jnp.zeros((LEAD, CHANNELS), F32)
        ext_ref[i, LEAD:, :] = raw_ref[i].astype(F32)
    blank = jnp.zeros((HEAD, CHANNELS), F32)
    for q in range(CHUNKS):
        feature = []
        for i in range(3):
            total = None
            for j in range(KW):
                term = weight_ref[i, j : j + 1, :] * ext_ref[i, pl.ds(LEAD - j + q * CHUNK, CHUNK), :]
                total = term if total is None else total + term
            feature.append(total)
        rows = pl.ds(q * CHUNK, CHUNK)
        lanes = slice(q * CHANNELS, (q + 1) * CHANNELS)
        signal = signal_ref[rows, :].astype(F32)
        kv_ref[0, rows, :] = feature[1]
        kv_ref[1, rows, :] = feature[2]
        gi_ref[:, lanes] = feature[1] * feature[2]
        gl_ref[:, lanes] = signal * feature[0]
        if q == 0:
            for i in range(3):
                head_ref[i] = feature[i][0:HEAD, :]
            head_ref[3] = signal[0:HEAD, :]
            gi_ref[0:HEAD, lanes] = blank
            gl_ref[0:HEAD, lanes] = blank
    ends = compact(dot3(descending, split(gi_ref[...])))
    leads = compact(dot3(ascending, split(gl_ref[...])))
    state = jnp.zeros((MODES, CHANNELS), F32)
    for q in range(CHUNKS):
        part = chunk_lanes(ends, q)
        states_ref[0, :, q * CHANNELS : (q + 1) * CHANNELS] = part
        state = chunk_decay * state + part
    back = jnp.zeros((MODES, CHANNELS), F32)
    for q in reversed(range(CHUNKS)):
        part = one_step * chunk_lanes(leads, q)
        states_ref[1, :, q * CHANNELS : (q + 1) * CHANNELS] = part
        back = chunk_decay * back + part
    ends_ref[0] = state
    ends_ref[1] = back


def scaled_columns(value):
    largest = jnp.max(jnp.abs(value), axis=0, keepdims=True)
    exponent = jnp.ceil(jnp.log2(jnp.maximum(largest, 1e-30))) - 15.0
    return value * jnp.exp2(-exponent), exponent


def patch_kernel(before_ref, weight_ref, head_ref, power_ref, ends_ref,
                 patch_ref, delta_ref, send_ref, ext_ref):
    feature = []
    for i in range(3):
        ext_ref[0:LEAD, :] = before_ref[i].astype(F32)
        ext_ref[LEAD:, :] = jnp.zeros((HEAD, CHANNELS), F32)
        total = head_ref[i]
        for j in range(1, KW):
            total = total + weight_ref[i, j : j + 1, :] * ext_ref[pl.ds(LEAD - j, HEAD), :]
        feature.append(total)
    gi = feature[1] * feature[2]
    gl = head_ref[3] * feature[0]
    for at, value in enumerate((feature[1], feature[2], gi, gl)):
        patch_ref[at] = value
    state_part, back_part = None, None
    for r in range(HEAD):
        ahead = power_ref[0, r] * gi[r : r + 1, :]
        behind = power_ref[1, r] * gl[r : r + 1, :]
        state_part = ahead if r == 0 else state_part + ahead
        back_part = behind if r == 0 else back_part + behind
    delta_ref[0] = state_part
    delta_ref[1] = back_part
    state = ends_ref[0] + power_ref[2, 0] * state_part
    back = ends_ref[1] + back_part
    for at, value in enumerate((back, state)):
        scaled, exponent = scaled_columns(value)
        send_ref[at, 0:MODES, :] = scaled
        send_ref[at, MODES:, :] = jnp.broadcast_to(exponent, (8, CHANNELS))


def spliced(wide_ref, patch):
    top = jnp.concatenate([patch, wide_ref[0:HEAD, CHANNELS:]], axis=1)
    return jnp.concatenate([top, wide_ref[HEAD:, :]], axis=0)


def middle_kernel(me_ref, table_ref, pair_ref, states_ref, patch_ref, delta_ref,
                  near_ref, halves_ref, lag_ref):
    long_ref, gated_ref, small_ref = near_parts(near_ref)
    gi_ref, gl_ref = pair_ref.at[0], pair_ref.at[1]
    rates = table_ref[0]
    row = mode_row(rates)
    column = mode_column(row)
    lag = iota((CHANNELS, CHUNK), 1)
    back_lag = lax.rem(CHUNK - lag, CHUNK)
    ascending = jnp.exp(-column * lag.astype(F32))
    descending = jnp.exp(-column * (CHUNK - 1 - lag).astype(F32))
    turned = jnp.exp(-column * back_lag.astype(F32))
    residue_row = mode_row(table_ref[1]) * lane_group(GROUPS)
    filters = lax.dot_general(residue_row, ascending, MM, precision=EXACT, preferred_element_type=F32)
    turned_filters = lax.dot_general(residue_row, turned, MM, precision=EXACT, preferred_element_type=F32)
    gi = split(spliced(gi_ref, patch_ref[2]))
    gl = split(spliced(gl_ref, patch_ref[3]))
    down = iota((CHUNK, CHUNK), 0)
    across = iota((CHUNK, CHUNK), 1)
    mirror = (down + across == CHUNK - 1).astype(F32).astype(BF16)
    mirrored = [
        lax.dot_general(mirror, part, MM, preferred_element_type=F32).astype(BF16) for part in gl
    ]
    wide_group = (iota((1, ROWS), 1) % CHANNELS) // WIDTH
    lane_of = iota((CHUNK, CHANNELS), 1) // WIDTH
    for g in range(GROUPS):
        straight = jnp.broadcast_to(turned_filters[g : g + 1, :], (CHUNK, CHUNK))
        straight = pltpu.roll(straight, 0, 1, stride=1, stride_axis=0)
        straight = split(jnp.where(across <= down, straight, 0.0))
        flipped = jnp.broadcast_to(filters[g : g + 1, :], (CHUNK, CHUNK))
        flipped = pltpu.roll(flipped, 0, 1, stride=1, stride_axis=0)
        flipped = split(jnp.where(across >= down, flipped, 0.0))
        forward = dot3(straight, gi)
        backward = dot3(flipped, gl)
        for q in range(CHUNKS):
            rows = pl.ds(q * CHUNK, CHUNK)
            if g == 0:
                long_ref[rows, :] = chunk_lanes(forward, q)
                gated_ref[rows, :] = chunk_lanes(backward, q)
            else:
                long_ref[rows, :] = jnp.where(lane_of == g, chunk_lanes(forward, q), long_ref[rows, :])
                gated_ref[rows, :] = jnp.where(lane_of == g, chunk_lanes(backward, q), gated_ref[rows, :])
        own = (wide_group == g).astype(F32).astype(BF16)
        products = dot3((mirrored[0] * own, mirrored[1] * own), gi, NT)
        products = jnp.where(across + down <= CHUNK - 1, products, 0.0)
        sheared = pltpu.roll(products, 1, 1, stride=1, stride_axis=0)
        lag_ref[g : g + 1, :] = jnp.sum(sheared, axis=0, keepdims=True)
    lag_grad = lag_ref[...]
    down_lag = lax.rem(CHUNK - down, CHUNK).astype(F32)
    powers = jnp.exp(-row * down_lag)
    residue_sums = lax.dot_general(lag_grad, powers, MM, precision=EXACT, preferred_element_type=F32)
    moment_sums = lax.dot_general(lag_grad, powers * down_lag, MM, precision=EXACT, preferred_element_type=F32)
    own_group = lane_group(GROUPS)
    small_ref[LOCAL + 2 : LOCAL + 3, :] = -row * mode_row(table_ref[1])
    small_ref[LOCAL : LOCAL + 1, :] = jnp.sum(residue_sums * own_group, axis=0, keepdims=True)
    small_ref[LOCAL + 1 : LOCAL + 2, :] = jnp.sum(moment_sums * own_group, axis=0, keepdims=True)
    small_rates = mode_compact(rates)
    small_residues = mode_compact(table_ref[1])
    chunk_decay = jnp.exp(-small_rates * CHUNK)
    lag_value = lag.astype(F32)
    end_moments = compact(dot3(split(descending * (CHUNK - 1 - lag_value)), gi))
    lead_moments = compact(dot3(split(ascending * (jnp.exp(-column) * (lag_value + 1.0))), gl))
    zero = jnp.zeros((MODES, CHANNELS), F32)
    leads = []
    state, moment = zero, zero
    residue_part, moment_part, lead_moment = zero, zero, zero
    offset_decay = jnp.ones((MODES, CHANNELS), F32)
    for q in range(CHUNKS):
        lead = chunk_lanes(states_ref[1], q)
        end = chunk_lanes(states_ref[0], q)
        if q == 0:
            end, lead = end + delta_ref[0], lead + delta_ref[1]
        leads.append(lead)
        lead_here = chunk_lanes(lead_moments, q)
        small_ref[piece(q), :] = small_residues * state
        residue_part = residue_part + lead * state
        moment_part = moment_part + lead_here * state + lead * moment
        lead_moment = lead_moment + offset_decay * (lead_here + float(q * CHUNK) * lead)
        offset_decay = offset_decay * chunk_decay
        moment = chunk_decay * (moment + float(CHUNK) * state) + chunk_lanes(end_moments, q)
        state = chunk_decay * state + end
    back = zero
    for q in reversed(range(CHUNKS)):
        small_ref[piece(CHUNKS + q), :] = small_residues * back
        back = chunk_decay * back + leads[q]
    for at, value in enumerate((residue_part, moment_part, lead_moment, moment, back)):
        small_ref[piece(2 * CHUNKS + at), :] = value
    factor = small_residues
    for q in range(CHUNKS):
        small_ref[piece(FACTOR + q), :] = factor
        factor = factor * chunk_decay
    count = small_ref.shape[0] // MODES - POWER
    for at in range(count):
        away = jnp.maximum(jnp.abs(me_ref[0] - member(at, count)) - 1, 0).astype(F32) * float(ROWS)
        small_ref[piece(POWER + at), :] = jnp.exp(-small_rates * away)
    steps = down.astype(F32)
    halves_ref[0], halves_ref[1] = split(jnp.exp(-row * (steps + 1.0)))
    halves_ref[2], halves_ref[3] = split(jnp.exp(-row * (CHUNK - 1 - steps)))


def finish_kernel(me_ref, arrived_ref, near_ref, halves_ref,
                  kv_ref, patch_ref, out_grad_ref, proj_ref, before_ref, feature_ref, stats_ref, ext_ref):
    for i in range(3):
        ext_ref[i, 0:LEAD, :] = before_ref[i].astype(F32)
        ext_ref[i, LEAD:, :] = proj_ref[i].astype(F32)
    long_ref, gated_ref, small_ref = near_parts(near_ref)
    me = me_ref[0]
    zero = jnp.zeros((MODES, CHANNELS), F32)
    state_in, late_in, back_in = zero, zero, zero
    for at in range(arrived_ref.shape[0]):
        d = member(at, arrived_ref.shape[0])
        away = (jnp.abs(me - d) - 1).astype(F32) * float(ROWS)
        scale = jnp.exp2(arrived_ref[at, MODES : MODES + 1, :])
        term = small_ref[piece(POWER + at), :] * (arrived_ref[at, 0:MODES, :] * scale)
        state_in = state_in + jnp.where(d < me, term, 0.0)
        late_in = late_in + jnp.where(d < me, term * away, 0.0)
        back_in = back_in + jnp.where(d > me, term, 0.0)
    states, backs = [], []
    for q in range(CHUNKS):
        states.append(small_ref[piece(q), :] + small_ref[piece(FACTOR + q), :] * state_in)
        backs.append(small_ref[piece(CHUNKS + q), :] + small_ref[piece(FACTOR + CHUNKS - 1 - q), :] * back_in)
    long_far = dot3((halves_ref[0], halves_ref[1]), expand(jnp.concatenate(states, axis=1)))
    gated_far = dot3((halves_ref[2], halves_ref[3]), expand(jnp.concatenate(backs, axis=1)))
    sums = [jnp.zeros((8, CHANNELS), F32) for _ in range(3 * KW)]
    for q in range(CHUNKS):
        rows = pl.ds(q * CHUNK, CHUNK)
        signal = out_grad_ref[rows, :].astype(F32)
        grad_gated = gated_ref[rows, :] + chunk_lanes(gated_far, q)
        keyed, valued = kv_ref[0, rows, :], kv_ref[1, rows, :]
        if q == 0:
            keyed = jnp.concatenate([patch_ref[0], keyed[HEAD:, :]], axis=0)
            valued = jnp.concatenate([patch_ref[1], valued[HEAD:, :]], axis=0)
        parts = (
            signal * (long_ref[rows, :] + chunk_lanes(long_far, q)),
            grad_gated * valued,
            grad_gated * keyed,
        )
        for i in range(3):
            feature_ref[i, rows, :] = parts[i]
            for j in range(KW):
                product = parts[i] * ext_ref[i, pl.ds(LEAD - j + q * CHUNK, CHUNK), :]
                sums[i * KW + j] = sums[i * KW + j] + jnp.sum(
                    product.reshape(CHUNK // 8, 8, CHANNELS), axis=0
                )
    residue_part, moment_part, lead_moment, end_moment, lead = (
        small_ref[piece(2 * CHUNKS + at), :] for at in range(5)
    )
    residue_part = residue_part + lead * state_in
    moment_part = moment_part + lead_moment * state_in + lead * late_in + end_moment * back_in
    same = (iota((CHANNELS, CHANNELS), 0) // WIDTH == iota((CHANNELS, CHANNELS), 1) // MODES).astype(F32)
    pick = (iota((MODES, CHANNELS), 1) % MODES == iota((MODES, CHANNELS), 0)).astype(F32)

    def by_mode(part):
        spread = lax.dot_general(part, same, MM, precision=EXACT, preferred_element_type=F32)
        return jnp.sum(spread * pick, axis=0, keepdims=True)

    residue_row = small_ref[LOCAL : LOCAL + 1, :] + by_mode(residue_part)
    moment_row = small_ref[LOCAL + 1 : LOCAL + 2, :] + by_mode(moment_part)
    rate_row = small_ref[LOCAL + 2 : LOCAL + 3, :] * moment_row
    lines = [jnp.sum(part, axis=0, keepdims=True) for part in sums]
    stats = jnp.concatenate(lines + [residue_row, rate_row, jnp.zeros((1, CHANNELS), F32)], axis=0)
    scaled, exponent = scaled_columns(stats)
    last = iota((STATS, CHANNELS), 0) == STATS - 1
    stats_ref[...] = jnp.where(last, exponent, scaled)


def inputs_kernel(feature_ref, after_ref, weight_ref, total_ref, out_ref, table_ref, ext_ref):
    pick = (iota((MODES, CHANNELS), 1) % MODES == iota((MODES, CHANNELS), 0)).astype(F32)
    for at in range(2):
        line = total_ref[3 * KW + at : 3 * KW + at + 1, :] * lane_group(GROUPS)
        table_ref[at] = lax.dot_general(line, pick, NT, precision=EXACT, preferred_element_type=F32)
    for i in range(3):
        ext_ref[0:ROWS, :] = feature_ref[i]
        ext_ref[ROWS:, :] = after_ref[i]
        for q in range(CHUNKS):
            total = None
            for j in range(KW):
                term = weight_ref[i, j : j + 1, :] * ext_ref[pl.ds(j + q * CHUNK, CHUNK), :]
                total = term if total is None else total + term
            out_ref[i, pl.ds(q * CHUNK, CHUNK), :] = total.astype(BF16)


def total_kernel(stats_ref, total_ref, square_ref):
    total = jnp.zeros((STATS, CHANNELS), F32)
    for d in range(stats_ref.shape[0]):
        total = total + stats_ref[d] * jnp.exp2(stats_ref[d, STATS - 1 :, :])
    total = jnp.where(iota((STATS, CHANNELS), 0) == STATS - 1, 0.0, total)
    total_ref[...] = total
    square = jnp.sum(total * total, axis=0, keepdims=True)
    for d in range(square_ref.shape[0]):
        square_ref[d] = jnp.broadcast_to(square, square_ref.shape[1:])


def scale_kernel(square_ref, total_ref, table_ref, conv_ref, residue_ref, rate_ref):
    squares = jnp.sum(jnp.sum(square_ref[:, 0, :], axis=0, keepdims=True), axis=1, keepdims=True)
    factor = jnp.minimum(1.0, lax.rsqrt(squares / (3 * KW * D + 2 * G * MODES) + 1e-6))
    for i in range(3):
        conv_ref[i] = total_ref[i * KW : (i + 1) * KW, :] * factor
    residue_ref[...] = table_ref[0] * factor
    rate_ref[...] = table_ref[1] * factor


def shape(*dims, dtype=F32):
    return jax.ShapeDtypeStruct(dims, dtype)


VMEM = pl.BlockSpec(memory_space=pltpu.VMEM)
SMEM = pl.BlockSpec(memory_space=pltpu.SMEM)


HBM = pl.BlockSpec(memory_space=pltpu.HBM)


def call(kernel, name, out_shape, specs, cost_us, scratch=()):
    return pl.pallas_call(
        kernel,
        out_shape=out_shape,
        in_specs=specs,
        out_specs=jax.tree.map(lambda _: VMEM, out_shape),
        scratch_shapes=list(scratch),
        compiler_params=pltpu.CompilerParams(vmem_limit_bytes=12 * 2**20),
        cost_estimate=pl.CostEstimate(
            flops=int(cost_us * 1e9), bytes_accessed=int(cost_us * 3e6), transcendentals=0
        ),
        name=name,
    )


def exchange(blocks, axis, first):
    count = blocks.shape[0]
    return lax.all_to_all(blocks, axis, 0, 0, axis_index_groups=[[(first + p) % count for p in range(count)]])


def shards(projected, conv_weight, residues, decay_rates, grad_out):
    ctx = lax.axis_size("ctx")
    planes = lax.axis_size("ch")
    me = lax.axis_index("ctx").astype(jnp.int32).reshape(1)
    before = lax.ppermute(
        projected[:, ROWS - LEAD :, :], "ctx", [(source, source + 1) for source in range(ctx - 1)]
    )
    kv, pair, states, ends, head, powers, table = call(
        prepare_kernel, "prepare",
        (shape(2, ROWS, CHANNELS), shape(2, CHUNK, CHUNKS * CHANNELS), shape(2, MODES, CHUNKS * CHANNELS),
         shape(2, MODES, CHANNELS), shape(4, HEAD, CHANNELS), shape(3, HEAD, MODES, CHANNELS),
         shape(2, GROUPS, MODES)),
        [VMEM] * 3 + [HBM] * 2, 3,
        scratch=[pltpu.VMEM((3, ROWS, CHANNELS), BF16), pltpu.VMEM((ROWS, CHANNELS), BF16),
                 pltpu.VMEM((3, LEAD + ROWS, CHANNELS), F32), pltpu.SemaphoreType.DMA((2,))],
    )(conv_weight, decay_rates, residues,
      *(pltpu.with_memory_space_constraint(part, pltpu.HBM) for part in (projected, grad_out)))
    patch, delta, send = call(
        patch_kernel, "patch",
        (shape(4, HEAD, CHANNELS), shape(2, MODES, CHANNELS), shape(2, MODES + 8, CHANNELS)),
        [VMEM] * 5, 1,
        scratch=[pltpu.VMEM((LEAD + HEAD, CHANNELS), F32)],
    )(before, conv_weight, head, powers, ends)
    later = member(lax.broadcasted_iota(jnp.int32, (ctx, 1, 1), 0), ctx) > me.reshape(1, 1, 1)
    send = jnp.where(later, send[1], send[0]).astype(F16)
    arrived = exchange(send, "ctx", ctx // 2).astype(F32)
    near, halves = call(
        middle_kernel, "within",
        (shape(2 * ROWS + (POWER + ctx) * MODES, CHANNELS), shape(4, CHUNK, CHANNELS, dtype=BF16)),
        [SMEM] + [VMEM] * 5, 8,
        scratch=[pltpu.VMEM((GROUPS, CHANNELS), F32)],
    )(me, table, pair, states, patch, delta)
    grad_feature, stats = call(
        finish_kernel, "across",
        (shape(3, ROWS, CHANNELS), shape(STATS, CHANNELS)),
        [SMEM] + [VMEM] * 8, 4,
        scratch=[pltpu.VMEM((3, LEAD + ROWS, CHANNELS), F32)],
    )(me, arrived, near, halves, kv, patch, grad_out, projected, before)
    after = lax.ppermute(
        grad_feature[:, :8, :], "ctx", [(source + 1, source) for source in range(ctx - 1)]
    )
    stats = jnp.broadcast_to(stats.astype(F16), (ctx, STATS, CHANNELS))
    gathered = exchange(stats, "ctx", ctx // 2).astype(F32)
    total, square = call(
        total_kernel, "total", (shape(STATS, CHANNELS), shape(planes, 1, CHANNELS)), [VMEM], 1,
    )(gathered)
    squares = exchange(square, "ch", planes - 2)
    grad_projected, table = call(
        inputs_kernel, "inputs",
        (shape(3, ROWS, CHANNELS, dtype=BF16), shape(2, GROUPS, MODES)), [VMEM] * 4, 2,
        scratch=[pltpu.VMEM((ROWS + 8, CHANNELS), F32)],
    )(grad_feature, after, conv_weight, total)
    grad_conv, grad_residues, grad_log_rates = call(
        scale_kernel, "scale",
        (shape(3, KW, CHANNELS), shape(GROUPS, MODES), shape(GROUPS, MODES)), [VMEM] * 3, 1,
    )(squares, total, table)
    return grad_projected, grad_conv, grad_residues, grad_log_rates


def solution(mesh):
    in_specs = (
        P(None, "ctx", "ch"),
        P(None, None, "ch"),
        P("ch", None),
        P("ch", None),
        P("ctx", "ch"),
    )
    out_specs = (P(None, "ctx", "ch"), P(None, None, "ch"), P("ch", None), P("ch", None))
    return jax.shard_map(shards, mesh=mesh, in_specs=in_specs, out_specs=out_specs, check_vma=False)
```

```python
import jax
import jax.numpy as jnp
from jax import lax
from jax.experimental import pallas as pl
from jax.experimental.pallas import tpu as pltpu
from jax.sharding import PartitionSpec as P

D = 4096
G = 256
MODES = 16
KW = 7

ROWS = 512
CHANNELS = 128
GROUPS = 8
WIDTH = 16
CHUNK = 128
CHUNKS = ROWS // CHUNK
LEAD = 16
HEAD = 8
STATS = 24
FACTOR = 2 * CHUNKS + 5
LOCAL = (FACTOR + CHUNKS) * MODES
POWER = FACTOR + CHUNKS + 1

F32 = jnp.float32
BF16 = jnp.bfloat16
F16 = jnp.float16
EXACT = lax.Precision.HIGHEST
MM = (((1,), (0,)), ((), ()))
NT = (((1,), (1,)), ((), ()))


def split(value):
    high = value.astype(BF16)
    low = (value - high.astype(F32)).astype(BF16)
    return high, low


def dot3(left, right, dims=MM):
    lh, ll = left
    rh, rl = right

    def product(a, b):
        return lax.dot_general(a, b, dims, preferred_element_type=F32)

    return product(lh, rh) + (product(lh, rl) + product(ll, rh))


def iota(shape, axis):
    return lax.broadcasted_iota(jnp.int32, shape, axis)


def lane_group(rows):
    return (iota((rows, CHANNELS), 1) // WIDTH == iota((rows, CHANNELS), 0)).astype(F32)


def mode_row(table):
    pick = (iota((MODES, CHANNELS), 1) % MODES == iota((MODES, CHANNELS), 0)).astype(F32)
    spread = lax.dot_general(table, pick, MM, precision=EXACT, preferred_element_type=F32)
    return jnp.sum(spread * lane_group(GROUPS), axis=0, keepdims=True)


def mode_column(row):
    eye = iota((CHANNELS, CHANNELS), 0) == iota((CHANNELS, CHANNELS), 1)
    return jnp.sum(jnp.where(eye, row, 0.0), axis=1, keepdims=True)


def mode_compact(table):
    return lax.dot_general(
        table, lane_group(GROUPS), (((0,), (0,)), ((), ())), precision=EXACT, preferred_element_type=F32
    )


def compact(full):
    lanes = full.shape[1]
    total = None
    for g in range(GROUPS):
        own = (iota((MODES, lanes), 1) % CHANNELS) // WIDTH == g
        part = jnp.where(own, full[g * MODES : (g + 1) * MODES, :], 0.0)
        total = part if total is None else total + part
    return total


def expand(small):
    lanes = small.shape[1]
    own = (iota((CHANNELS, lanes), 0) // MODES == (iota((CHANNELS, lanes), 1) % CHANNELS) // WIDTH).astype(F32)
    return split(jnp.concatenate([small] * GROUPS, axis=0) * own)


def near_parts(near_ref):
    return near_ref.at[0:ROWS, :], near_ref.at[ROWS : 2 * ROWS, :], near_ref.at[2 * ROWS :, :]


def member(position, count):
    return (position + count // 2 + 1) % count


def piece(at):
    return slice(at * MODES, (at + 1) * MODES)


def chunk_lanes(value, q):
    return value[:, q * CHANNELS : (q + 1) * CHANNELS]


def prepare_kernel(weight_ref, rate_ref, residue_ref, proj_ref, out_grad_ref,
                   kv_ref, pair_ref, states_ref, ends_ref, head_ref, power_ref, table_ref,
                   raw_ref, signal_ref, ext_ref, sem_ref):
    gi_ref, gl_ref = pair_ref.at[0], pair_ref.at[1]
    copies = [
        pltpu.make_async_copy(proj_ref, raw_ref, sem_ref.at[0]),
        pltpu.make_async_copy(out_grad_ref, signal_ref, sem_ref.at[1]),
    ]
    for copy in copies:
        copy.start()
    rates = rate_ref[...]
    table_ref[0] = rates
    table_ref[1] = residue_ref[...]
    column = mode_column(mode_row(rates))
    lag = iota((CHANNELS, CHUNK), 1).astype(F32)
    ascending = split(jnp.exp(-column * lag))
    descending = split(jnp.exp(-column * (CHUNK - 1 - lag)))
    small_rates = mode_compact(rates)
    one_step = jnp.exp(-small_rates)
    chunk_decay = jnp.exp(-small_rates * CHUNK)
    for r in range(HEAD):
        power_ref[0, r] = jnp.exp(-small_rates * float(CHUNK - 1 - r))
        power_ref[1, r] = jnp.exp(-small_rates * float(r + 1))
    power_ref[2, 0] = jnp.exp(-small_rates * float(ROWS - CHUNK))
    for r in range(1, HEAD):
        power_ref[2, r] = jnp.zeros((MODES, CHANNELS), F32)
    for copy in copies:
        copy.wait()
    for i in range(3):
        ext_ref[i, 0:LEAD, :] = jnp.zeros((LEAD, CHANNELS), F32)
        ext_ref[i, LEAD:, :] = raw_ref[i].astype(F32)
    blank = jnp.zeros((HEAD, CHANNELS), F32)
    for q in range(CHUNKS):
        feature = []
        for i in range(3):
            total = None
            for j in range(KW):
                term = weight_ref[i, j : j + 1, :] * ext_ref[i, pl.ds(LEAD - j + q * CHUNK, CHUNK), :]
                total = term if total is None else total + term
            feature.append(total)
        rows = pl.ds(q * CHUNK, CHUNK)
        lanes = slice(q * CHANNELS, (q + 1) * CHANNELS)
        signal = signal_ref[rows, :].astype(F32)
        kv_ref[0, rows, :] = feature[1]
        kv_ref[1, rows, :] = feature[2]
        gi_ref[:, lanes] = feature[1] * feature[2]
        gl_ref[:, lanes] = signal * feature[0]
        if q == 0:
            for i in range(3):
                head_ref[i] = feature[i][0:HEAD, :]
            head_ref[3] = signal[0:HEAD, :]
            gi_ref[0:HEAD, lanes] = blank
            gl_ref[0:HEAD, lanes] = blank
    ends = compact(dot3(descending, split(gi_ref[...])))
    leads = compact(dot3(ascending, split(gl_ref[...])))
    state = jnp.zeros((MODES, CHANNELS), F32)
    for q in range(CHUNKS):
        part = chunk_lanes(ends, q)
        states_ref[0, :, q * CHANNELS : (q + 1) * CHANNELS] = part
        state = chunk_decay * state + part
    back = jnp.zeros((MODES, CHANNELS), F32)
    for q in reversed(range(CHUNKS)):
        part = one_step * chunk_lanes(leads, q)
        states_ref[1, :, q * CHANNELS : (q + 1) * CHANNELS] = part
        back = chunk_decay * back + part
    ends_ref[0] = state
    ends_ref[1] = back


def scaled_columns(value):
    largest = jnp.max(jnp.abs(value), axis=0, keepdims=True)
    exponent = jnp.ceil(jnp.log2(jnp.maximum(largest, 1e-30))) - 15.0
    return value * jnp.exp2(-exponent), exponent


def patch_kernel(before_ref, weight_ref, head_ref, power_ref, ends_ref,
                 patch_ref, delta_ref, send_ref, ext_ref):
    feature = []
    for i in range(3):
        ext_ref[0:LEAD, :] = before_ref[i].astype(F32)
        ext_ref[LEAD:, :] = jnp.zeros((HEAD, CHANNELS), F32)
        total = head_ref[i]
        for j in range(1, KW):
            total = total + weight_ref[i, j : j + 1, :] * ext_ref[pl.ds(LEAD - j, HEAD), :]
        feature.append(total)
    gi = feature[1] * feature[2]
    gl = head_ref[3] * feature[0]
    for at, value in enumerate((feature[1], feature[2], gi, gl)):
        patch_ref[at] = value
    state_part, back_part = None, None
    for r in range(HEAD):
        ahead = power_ref[0, r] * gi[r : r + 1, :]
        behind = power_ref[1, r] * gl[r : r + 1, :]
        state_part = ahead if r == 0 else state_part + ahead
        back_part = behind if r == 0 else back_part + behind
    delta_ref[0] = state_part
    delta_ref[1] = back_part
    state = ends_ref[0] + power_ref[2, 0] * state_part
    back = ends_ref[1] + back_part
    for at, value in enumerate((back, state)):
        scaled, exponent = scaled_columns(value)
        send_ref[at, 0:MODES, :] = scaled
        send_ref[at, MODES:, :] = jnp.broadcast_to(exponent, (8, CHANNELS))


def spliced(wide_ref, patch):
    top = jnp.concatenate([patch, wide_ref[0:HEAD, CHANNELS:]], axis=1)
    return jnp.concatenate([top, wide_ref[HEAD:, :]], axis=0)


def middle_kernel(me_ref, table_ref, pair_ref, states_ref, patch_ref, delta_ref,
                  near_ref, halves_ref, lag_ref):
    long_ref, gated_ref, small_ref = near_parts(near_ref)
    gi_ref, gl_ref = pair_ref.at[0], pair_ref.at[1]
    rates = table_ref[0]
    row = mode_row(rates)
    column = mode_column(row)
    lag = iota((CHANNELS, CHUNK), 1)
    back_lag = lax.rem(CHUNK - lag, CHUNK)
    ascending = jnp.exp(-column * lag.astype(F32))
    descending = jnp.exp(-column * (CHUNK - 1 - lag).astype(F32))
    turned = jnp.exp(-column * back_lag.astype(F32))
    residue_row = mode_row(table_ref[1]) * lane_group(GROUPS)
    filters = lax.dot_general(residue_row, ascending, MM, precision=EXACT, preferred_element_type=F32)
    turned_filters = lax.dot_general(residue_row, turned, MM, precision=EXACT, preferred_element_type=F32)
    gi = split(spliced(gi_ref, patch_ref[2]))
    gl = split(spliced(gl_ref, patch_ref[3]))
    down = iota((CHUNK, CHUNK), 0)
    across = iota((CHUNK, CHUNK), 1)
    mirror = (down + across == CHUNK - 1).astype(F32).astype(BF16)
    mirrored = [
        lax.dot_general(mirror, part, MM, preferred_element_type=F32).astype(BF16) for part in gl
    ]
    wide_group = (iota((1, ROWS), 1) % CHANNELS) // WIDTH
    lane_of = iota((CHUNK, CHANNELS), 1) // WIDTH
    for g in range(GROUPS):
        straight = jnp.broadcast_to(turned_filters[g : g + 1, :], (CHUNK, CHUNK))
        straight = pltpu.roll(straight, 0, 1, stride=1, stride_axis=0)
        straight = split(jnp.where(across <= down, straight, 0.0))
        flipped = jnp.broadcast_to(filters[g : g + 1, :], (CHUNK, CHUNK))
        flipped = pltpu.roll(flipped, 0, 1, stride=1, stride_axis=0)
        flipped = split(jnp.where(across >= down, flipped, 0.0))
        forward = dot3(straight, gi)
        backward = dot3(flipped, gl)
        for q in range(CHUNKS):
            rows = pl.ds(q * CHUNK, CHUNK)
            if g == 0:
                long_ref[rows, :] = chunk_lanes(forward, q)
                gated_ref[rows, :] = chunk_lanes(backward, q)
            else:
                long_ref[rows, :] = jnp.where(lane_of == g, chunk_lanes(forward, q), long_ref[rows, :])
                gated_ref[rows, :] = jnp.where(lane_of == g, chunk_lanes(backward, q), gated_ref[rows, :])
        own = (wide_group == g).astype(F32).astype(BF16)
        products = dot3((mirrored[0] * own, mirrored[1] * own), gi, NT)
        products = jnp.where(across + down <= CHUNK - 1, products, 0.0)
        sheared = pltpu.roll(products, 1, 1, stride=1, stride_axis=0)
        lag_ref[g : g + 1, :] = jnp.sum(sheared, axis=0, keepdims=True)
    lag_grad = lag_ref[...]
    down_lag = lax.rem(CHUNK - down, CHUNK).astype(F32)
    powers = jnp.exp(-row * down_lag)
    residue_sums = lax.dot_general(lag_grad, powers, MM, precision=EXACT, preferred_element_type=F32)
    moment_sums = lax.dot_general(lag_grad, powers * down_lag, MM, precision=EXACT, preferred_element_type=F32)
    own_group = lane_group(GROUPS)
    small_ref[LOCAL + 2 : LOCAL + 3, :] = -row * mode_row(table_ref[1])
    small_ref[LOCAL : LOCAL + 1, :] = jnp.sum(residue_sums * own_group, axis=0, keepdims=True)
    small_ref[LOCAL + 1 : LOCAL + 2, :] = jnp.sum(moment_sums * own_group, axis=0, keepdims=True)
    small_rates = mode_compact(rates)
    small_residues = mode_compact(table_ref[1])
    chunk_decay = jnp.exp(-small_rates * CHUNK)
    lag_value = lag.astype(F32)
    end_moments = compact(dot3(split(descending * (CHUNK - 1 - lag_value)), gi))
    lead_moments = compact(dot3(split(ascending * (jnp.exp(-column) * (lag_value + 1.0))), gl))
    zero = jnp.zeros((MODES, CHANNELS), F32)
    leads = []
    state, moment = zero, zero
    residue_part, moment_part, lead_moment = zero, zero, zero
    offset_decay = jnp.ones((MODES, CHANNELS), F32)
    for q in range(CHUNKS):
        lead = chunk_lanes(states_ref[1], q)
        end = chunk_lanes(states_ref[0], q)
        if q == 0:
            end, lead = end + delta_ref[0], lead + delta_ref[1]
        leads.append(lead)
        lead_here = chunk_lanes(lead_moments, q)
        small_ref[piece(q), :] = small_residues * state
        residue_part = residue_part + lead * state
        moment_part = moment_part + lead_here * state + lead * moment
        lead_moment = lead_moment + offset_decay * (lead_here + float(q * CHUNK) * lead)
        offset_decay = offset_decay * chunk_decay
        moment = chunk_decay * (moment + float(CHUNK) * state) + chunk_lanes(end_moments, q)
        state = chunk_decay * state + end
    back = zero
    for q in reversed(range(CHUNKS)):
        small_ref[piece(CHUNKS + q), :] = small_residues * back
        back = chunk_decay * back + leads[q]
    for at, value in enumerate((residue_part, moment_part, lead_moment, moment, back)):
        small_ref[piece(2 * CHUNKS + at), :] = value
    factor = small_residues
    for q in range(CHUNKS):
        small_ref[piece(FACTOR + q), :] = factor
        factor = factor * chunk_decay
    count = small_ref.shape[0] // MODES - POWER
    for at in range(count):
        away = jnp.maximum(jnp.abs(me_ref[0] - member(at, count)) - 1, 0).astype(F32) * float(ROWS)
        small_ref[piece(POWER + at), :] = jnp.exp(-small_rates * away)
    steps = down.astype(F32)
    halves_ref[0], halves_ref[1] = split(jnp.exp(-row * (steps + 1.0)))
    halves_ref[2], halves_ref[3] = split(jnp.exp(-row * (CHUNK - 1 - steps)))


def finish_kernel(me_ref, arrived_ref, near_ref, halves_ref,
                  kv_ref, patch_ref, out_grad_ref, proj_ref, before_ref, feature_ref, stats_ref, ext_ref):
    for i in range(3):
        ext_ref[i, 0:LEAD, :] = before_ref[i].astype(F32)
        ext_ref[i, LEAD:, :] = proj_ref[i].astype(F32)
    long_ref, gated_ref, small_ref = near_parts(near_ref)
    me = me_ref[0]
    zero = jnp.zeros((MODES, CHANNELS), F32)
    state_in, late_in, back_in = zero, zero, zero
    for at in range(arrived_ref.shape[0]):
        d = member(at, arrived_ref.shape[0])
        away = (jnp.abs(me - d) - 1).astype(F32) * float(ROWS)
        scale = jnp.exp2(arrived_ref[at, MODES : MODES + 1, :])
        term = small_ref[piece(POWER + at), :] * (arrived_ref[at, 0:MODES, :] * scale)
        state_in = state_in + jnp.where(d < me, term, 0.0)
        late_in = late_in + jnp.where(d < me, term * away, 0.0)
        back_in = back_in + jnp.where(d > me, term, 0.0)
    states, backs = [], []
    for q in range(CHUNKS):
        states.append(small_ref[piece(q), :] + small_ref[piece(FACTOR + q), :] * state_in)
        backs.append(small_ref[piece(CHUNKS + q), :] + small_ref[piece(FACTOR + CHUNKS - 1 - q), :] * back_in)
    long_far = dot3((halves_ref[0], halves_ref[1]), expand(jnp.concatenate(states, axis=1)))
    gated_far = dot3((halves_ref[2], halves_ref[3]), expand(jnp.concatenate(backs, axis=1)))
    sums = [jnp.zeros((8, CHANNELS), F32) for _ in range(3 * KW)]
    for q in range(CHUNKS):
        rows = pl.ds(q * CHUNK, CHUNK)
        signal = out_grad_ref[rows, :].astype(F32)
        grad_gated = gated_ref[rows, :] + chunk_lanes(gated_far, q)
        keyed, valued = kv_ref[0, rows, :], kv_ref[1, rows, :]
        if q == 0:
            keyed = jnp.concatenate([patch_ref[0], keyed[HEAD:, :]], axis=0)
            valued = jnp.concatenate([patch_ref[1], valued[HEAD:, :]], axis=0)
        parts = (
            signal * (long_ref[rows, :] + chunk_lanes(long_far, q)),
            grad_gated * valued,
            grad_gated * keyed,
        )
        for i in range(3):
            feature_ref[i, rows, :] = parts[i]
            for j in range(KW):
                product = parts[i] * ext_ref[i, pl.ds(LEAD - j + q * CHUNK, CHUNK), :]
                sums[i * KW + j] = sums[i * KW + j] + jnp.sum(
                    product.reshape(CHUNK // 8, 8, CHANNELS), axis=0
                )
    residue_part, moment_part, lead_moment, end_moment, lead = (
        small_ref[piece(2 * CHUNKS + at), :] for at in range(5)
    )
    residue_part = residue_part + lead * state_in
    moment_part = moment_part + lead_moment * state_in + lead * late_in + end_moment * back_in
    same = (iota((CHANNELS, CHANNELS), 0) // WIDTH == iota((CHANNELS, CHANNELS), 1) // MODES).astype(F32)
    pick = (iota((MODES, CHANNELS), 1) % MODES == iota((MODES, CHANNELS), 0)).astype(F32)

    def by_mode(part):
        spread = lax.dot_general(part, same, MM, precision=EXACT, preferred_element_type=F32)
        return jnp.sum(spread * pick, axis=0, keepdims=True)

    residue_row = small_ref[LOCAL : LOCAL + 1, :] + by_mode(residue_part)
    moment_row = small_ref[LOCAL + 1 : LOCAL + 2, :] + by_mode(moment_part)
    rate_row = small_ref[LOCAL + 2 : LOCAL + 3, :] * moment_row
    lines = [jnp.sum(part, axis=0, keepdims=True) for part in sums]
    stats = jnp.concatenate(lines + [residue_row, rate_row, jnp.zeros((1, CHANNELS), F32)], axis=0)
    scaled, exponent = scaled_columns(stats)
    last = iota((STATS, CHANNELS), 0) == STATS - 1
    stats_ref[...] = jnp.where(last, exponent, scaled)


def inputs_kernel(feature_ref, after_ref, weight_ref, total_ref, out_ref, table_ref, ext_ref):
    pick = (iota((MODES, CHANNELS), 1) % MODES == iota((MODES, CHANNELS), 0)).astype(F32)
    for at in range(2):
        line = total_ref[3 * KW + at : 3 * KW + at + 1, :] * lane_group(GROUPS)
        table_ref[at] = lax.dot_general(line, pick, NT, precision=EXACT, preferred_element_type=F32)
    for i in range(3):
        ext_ref[0:ROWS, :] = feature_ref[i]
        ext_ref[ROWS:, :] = after_ref[i]
        for q in range(CHUNKS):
            total = None
            for j in range(KW):
                term = weight_ref[i, j : j + 1, :] * ext_ref[pl.ds(j + q * CHUNK, CHUNK), :]
                total = term if total is None else total + term
            out_ref[i, pl.ds(q * CHUNK, CHUNK), :] = total.astype(BF16)


def total_kernel(stats_ref, total_ref, square_ref):
    total = jnp.zeros((STATS, CHANNELS), F32)
    for d in range(stats_ref.shape[0]):
        total = total + stats_ref[d] * jnp.exp2(stats_ref[d, STATS - 1 :, :])
    total = jnp.where(iota((STATS, CHANNELS), 0) == STATS - 1, 0.0, total)
    total_ref[...] = total
    square = jnp.sum(total * total, axis=0, keepdims=True)
    for d in range(square_ref.shape[0]):
        square_ref[d] = jnp.broadcast_to(square, square_ref.shape[1:])


def scale_kernel(square_ref, total_ref, table_ref, conv_ref, residue_ref, rate_ref):
    squares = jnp.sum(jnp.sum(square_ref[:, 0, :], axis=0, keepdims=True), axis=1, keepdims=True)
    factor = jnp.minimum(1.0, lax.rsqrt(squares / (3 * KW * D + 2 * G * MODES) + 1e-6))
    for i in range(3):
        conv_ref[i] = total_ref[i * KW : (i + 1) * KW, :] * factor
    residue_ref[...] = table_ref[0] * factor
    rate_ref[...] = table_ref[1] * factor


def shape(*dims, dtype=F32):
    return jax.ShapeDtypeStruct(dims, dtype)


VMEM = pl.BlockSpec(memory_space=pltpu.VMEM)
SMEM = pl.BlockSpec(memory_space=pltpu.SMEM)


HBM = pl.BlockSpec(memory_space=pltpu.HBM)


def call(kernel, name, out_shape, specs, cost_us, scratch=()):
    return pl.pallas_call(
        kernel,
        out_shape=out_shape,
        in_specs=specs,
        out_specs=jax.tree.map(lambda _: VMEM, out_shape),
        scratch_shapes=list(scratch),
        compiler_params=pltpu.CompilerParams(vmem_limit_bytes=12 * 2**20),
        cost_estimate=pl.CostEstimate(
            flops=int(cost_us * 1e9), bytes_accessed=int(cost_us * 3e6), transcendentals=0
        ),
        name=name,
    )


def exchange(blocks, axis, first):
    count = blocks.shape[0]
    return lax.all_to_all(blocks, axis, 0, 0, axis_index_groups=[[(first + p) % count for p in range(count)]])


def shards(projected, conv_weight, residues, decay_rates, grad_out):
    ctx = lax.axis_size("ctx")
    planes = lax.axis_size("ch")
    me = lax.axis_index("ctx").astype(jnp.int32).reshape(1)
    before = lax.ppermute(
        projected[:, ROWS - LEAD :, :], "ctx", [(source, source + 1) for source in range(ctx - 1)]
    )
    kv, pair, states, ends, head, powers, table = call(
        prepare_kernel, "prepare",
        (shape(2, ROWS, CHANNELS), shape(2, CHUNK, CHUNKS * CHANNELS), shape(2, MODES, CHUNKS * CHANNELS),
         shape(2, MODES, CHANNELS), shape(4, HEAD, CHANNELS), shape(3, HEAD, MODES, CHANNELS),
         shape(2, GROUPS, MODES)),
        [VMEM] * 3 + [HBM] * 2, 3,
        scratch=[pltpu.VMEM((3, ROWS, CHANNELS), BF16), pltpu.VMEM((ROWS, CHANNELS), BF16),
                 pltpu.VMEM((3, LEAD + ROWS, CHANNELS), F32), pltpu.SemaphoreType.DMA((2,))],
    )(conv_weight, decay_rates, residues,
      *(pltpu.with_memory_space_constraint(part, pltpu.HBM) for part in (projected, grad_out)))
    patch, delta, send = call(
        patch_kernel, "patch",
        (shape(4, HEAD, CHANNELS), shape(2, MODES, CHANNELS), shape(2, MODES + 8, CHANNELS)),
        [VMEM] * 5, 1,
        scratch=[pltpu.VMEM((LEAD + HEAD, CHANNELS), F32)],
    )(before, conv_weight, head, powers, ends)
    later = member(lax.broadcasted_iota(jnp.int32, (ctx, 1, 1), 0), ctx) > me.reshape(1, 1, 1)
    send = jnp.where(later, send[1], send[0]).astype(F16)
    arrived = exchange(send, "ctx", ctx // 2 + 1).astype(F32)
    near, halves = call(
        middle_kernel, "within",
        (shape(2 * ROWS + (POWER + ctx) * MODES, CHANNELS), shape(4, CHUNK, CHANNELS, dtype=BF16)),
        [SMEM] + [VMEM] * 5, 8,
        scratch=[pltpu.VMEM((GROUPS, CHANNELS), F32)],
    )(me, table, pair, states, patch, delta)
    grad_feature, stats = call(
        finish_kernel, "across",
        (shape(3, ROWS, CHANNELS), shape(STATS, CHANNELS)),
        [SMEM] + [VMEM] * 8, 4,
        scratch=[pltpu.VMEM((3, LEAD + ROWS, CHANNELS), F32)],
    )(me, arrived, near, halves, kv, patch, grad_out, projected, before)
    after = lax.ppermute(
        grad_feature[:, :8, :], "ctx", [(source + 1, source) for source in range(ctx - 1)]
    )
    stats = jnp.broadcast_to(stats.astype(F16), (ctx, STATS, CHANNELS))
    gathered = exchange(stats, "ctx", ctx // 2).astype(F32)
    total, square = call(
        total_kernel, "total", (shape(STATS, CHANNELS), shape(planes, 1, CHANNELS)), [VMEM], 1,
    )(gathered)
    squares = exchange(square, "ch", planes // 2 + planes // 8)
    grad_projected, table = call(
        inputs_kernel, "inputs",
        (shape(3, ROWS, CHANNELS, dtype=BF16), shape(2, GROUPS, MODES)), [VMEM] * 4, 2,
        scratch=[pltpu.VMEM((ROWS + 8, CHANNELS), F32)],
    )(grad_feature, after, conv_weight, total)
    grad_conv, grad_residues, grad_log_rates = call(
        scale_kernel, "scale",
        (shape(3, KW, CHANNELS), shape(GROUPS, MODES), shape(GROUPS, MODES)), [VMEM] * 3, 1,
    )(squares, total, table)
    return grad_projected, grad_conv, grad_residues, grad_log_rates


def solution(mesh):
    in_specs = (
        P(None, "ctx", "ch"),
        P(None, None, "ch"),
        P("ch", None),
        P("ch", None),
        P("ctx", "ch"),
    )
    out_specs = (P(None, "ctx", "ch"), P(None, None, "ch"), P("ch", None), P("ch", None))
    return jax.shard_map(shards, mesh=mesh, in_specs=in_specs, out_specs=out_specs, check_vma=False)
```
